32 devices in a mesh: dp: 8 (over z, x), tensor: 4 (over y, core).
Axes of the slice: x: 2, y: 2, z: 4, core: 2. Of those that a mesh axis runs over, the one named last changes fastest.
Arguments:
- inputs: bfloat16 [24, 1024, 512], P('dp', 'tensor'), may hold values from -6 to 6
- cotangent: bfloat16 [24, 1024, 512], P('dp', 'tensor'), may hold values from -6 to 6
- mix_weight: bfloat16 [512, 1536], P(('dp', 'tensor')), may hold values from -0.25 to 0.25
- gate_weight: bfloat16 [512, 8], P(('dp', 'tensor')), may hold values from -0.25 to 0.25
- gate_bias: float32 [8], replicated, may hold values from 2.5 to 8
- out_weight: bfloat16 [512, 512], P(('dp', 'tensor')), may hold values from -1 to 1
- gain_first: bfloat16 [512], P(('dp', 'tensor')), may hold values from 0.5 to 1.5
- shift_first: bfloat16 [512], P(('dp', 'tensor')), may hold values from -2.5 to 2.5
- gain_second: bfloat16 [512], P(('dp', 'tensor')), may hold values from 0.5 to 1.5
- shift_second: bfloat16 [512], P(('dp', 'tensor')), may hold values from -2.5 to 2.5
- up_weight: bfloat16 [512, 2048], P('dp', 'tensor'), may hold values from -0.25 to 0.25
- down_weight: bfloat16 [2048, 512], P('tensor', 'dp'), may hold values from -0.125 to 0.125
- random_maps: bfloat16 [8, 64, 64], replicated, may hold values from -0.75 to 0.75
Outputs:
- output: bfloat16 [24, 1024, 512], P('dp', 'tensor')
- input_grad: float32 [24, 1024, 512], P('dp', 'tensor')
- mix_grad: float32 [512, 1536], P(('dp', 'tensor'))
- gate_grad: float32 [512, 8], P(('dp', 'tensor'))
- bias_grad: float32 [8], replicated
- out_grad: float32 [512, 512], P(('dp', 'tensor'))
- first_gain_grad: float32 [512], P(('dp', 'tensor'))
- first_shift_grad: float32 [512], P(('dp', 'tensor'))
- second_gain_grad: float32 [512], P(('dp', 'tensor'))
- second_shift_grad: float32 [512], P(('dp', 'tensor'))
- up_grad: float32 [512, 2048], P('dp', 'tensor')
- down_grad: float32 [2048, 512], P('tensor', 'dp')
The draws below stay inside these ranges and needn't reach their ends.
All inputs are finite; a program needn't handle non-finite values.
Results may differ from the reference program's by a relative error of at most 0.012.
Values may be sent and summed in bfloat16 or wider, within the bound.
No kernel may reach another device: no remote copies, remote signals or barrier semaphores. Data moves between devices by JAX's collectives and lax.ppermute only.
A program may use at most 192 MiB of HBM per device.

```python
import math
import jax
import jax.numpy as jnp
from jax import lax

D = 512
H = 8
HEAD = 64
FEAT = 64
FF = 2048
BLOCK = 128
LEN = 1024
SEQS = 24


def shard_levels(own_key, dims, cuts, least, largest):
    factor_of = 1.0
    for position, parts in cuts:
        steps = jax.random.uniform(jax.random.fold_in(jax.random.fold_in(own_key, 6), position), (parts,), jnp.float32, least / len(cuts), largest / len(cuts))
        factor_of = factor_of * jnp.repeat(jnp.exp(steps), dims[position] // parts).reshape((-1,) + (1,) * (len(dims) - 1 - position))
    return factor_of


def gaussian(rng, extent, deviation, bound, cuts=(), kind=jnp.bfloat16):
    values = deviation * jax.random.normal(rng, extent, jnp.float32)
    if cuts:
        values = values * shard_levels(rng, extent, cuts, -0.22, 0.18)
    return jnp.clip(values, -bound, bound).astype(kind)


def setup_inputs(seed: int = 0) -> dict:
    streams_of = jax.random.split(jax.random.key(seed), 14)
    return {
        "inputs": gaussian(streams_of[0], (SEQS, LEN, D), 1.0, 6.0, ((0, 8), (1, 4))),
        "cotangent": gaussian(streams_of[1], (SEQS, LEN, D), 1.0, 6.0, ((0, 8), (1, 4))),
        "mix_weight": gaussian(streams_of[2], (D, 3 * D), D ** -0.5, 0.25, ((0, 32),)),
        "gate_weight": gaussian(streams_of[3], (D, H), D ** -0.5, 0.25, ((0, 32),)),
        "gate_bias": jnp.clip(jax.random.uniform(streams_of[4], (H,), jnp.float32, 2.5, 8.0), 2.5, 8.0),
        "out_weight": gaussian(streams_of[5], (D, D), (D // 16) ** -0.5, 1.0, ((0, 32),)),
        "gain_first": jnp.clip(1.0 + 0.1 * jax.random.normal(streams_of[6], (D,), jnp.float32), 0.5, 1.5).astype(jnp.bfloat16),
        "shift_first": gaussian(streams_of[7], (D,), 0.3, 2.5, ((0, 32),)),
        "gain_second": jnp.clip(1.0 + 0.1 * jax.random.normal(streams_of[8], (D,), jnp.float32), 0.5, 1.5).astype(jnp.bfloat16),
        "shift_second": gaussian(streams_of[9], (D,), 0.3, 2.5, ((0, 32),)),
        "up_weight": gaussian(streams_of[10], (D, FF), D ** -0.5, 0.25, ((0, 8), (1, 4))),
        "down_weight": gaussian(streams_of[11], (FF, D), FF ** -0.5, 0.125, ((0, 4), (1, 8))),
        "random_maps": gaussian(streams_of[12], (H, HEAD, FEAT), HEAD ** -0.5, 0.75),
    }


@jax.custom_vjp
def low(v):
    return lax.optimization_barrier(v.astype(jnp.bfloat16)).astype(jnp.float32)

@jax.custom_vjp
def low_back(v):
    return v

def low_keep(v):
    return (low(v), None)

def low_pass(kept, grad):
    return (grad,)

def back_keep(v):
    return (v, None)

def back_low(kept, grad):
    return (low(grad),)
low.defvjp(low_keep, low_pass)
low_back.defvjp(back_keep, back_low)
HIGHEST = lax.Precision.HIGHEST

def product(pattern, *operands):
    return jnp.einsum(pattern, *operands, precision=HIGHEST)

def norm_rows(values, gain_vec, shift_vec):
    row_mean = lax.optimization_barrier(jnp.mean(values, axis=-1, keepdims=True))
    centered = values - row_mean
    variance = lax.optimization_barrier(jnp.mean(centered * centered, axis=-1, keepdims=True))
    return centered * lax.rsqrt(variance + 1e-05) * gain_vec + shift_vec

def features(rows, random_maps):
    angles = product('blhd,hdf->bhlf', rows, random_maps)
    return jnp.concatenate([jnp.sin(angles), jnp.cos(angles)], axis=-1)

def block_step(carried, pieces):
    state_mat, state_sum, offset = carried
    query_feats, key_feats, values, log_gate, fresh_share = pieces
    cum_log = jnp.cumsum(log_gate, axis=-1)
    positions = jnp.arange(cum_log.shape[-1])
    causal = positions[:, None] >= positions[None, :]
    log_gap = jnp.minimum(cum_log[..., :, None] - cum_log[..., None, :], 0.0)
    weights = jnp.where(causal, jnp.exp(log_gap), 0.0) * fresh_share[..., None, :]
    kernel = product('bhtf,bhsf->bhts', query_feats, key_feats) * weights
    decay_in = jnp.exp(cum_log)
    numerator = product('bhts,bhsd->bhtd', kernel, values) + decay_in[..., None] * product('bhtf,bhfd->bhtd', query_feats, state_mat)
    denominator = lax.optimization_barrier(jnp.sum(kernel, axis=-1)) + decay_in * product('bhtf,bhf->bht', query_feats, state_sum)
    decay_out = jnp.exp(cum_log[..., -1:] - cum_log) * fresh_share
    decay_all = decay_in[..., -1]
    state_mat = decay_all[..., None, None] * state_mat + product('bhs,bhsf,bhsd->bhfd', decay_out, key_feats, values)
    state_sum = decay_all[..., None] * state_sum + product('bhs,bhsf->bhf', decay_out, key_feats)
    return ((state_mat, state_sum, offset + cum_log[..., -1]), (numerator, denominator, offset[..., None] + cum_log))

def run_blocks(query_feats, key_feats, values, log_gate, fresh_share, block_size):
    seq_count, head_count, length = log_gate.shape
    block_count = length // block_size

    def to_blocks(array):
        shaped = array.reshape((seq_count, head_count, block_count, block_size) + array.shape[3:])
        return jnp.moveaxis(shaped, 2, 0)

    def join_back(array):
        moved = jnp.moveaxis(array, 0, 2)
        return moved.reshape((seq_count, head_count, length) + moved.shape[4:])
    feat_width = query_feats.shape[-1]
    head_size = values.shape[-1]
    start = (jnp.zeros((seq_count, head_count, feat_width, head_size), query_feats.dtype), jnp.zeros((seq_count, head_count, feat_width), query_feats.dtype), jnp.zeros((seq_count, head_count), query_feats.dtype))
    pieces = (to_blocks(query_feats), to_blocks(key_feats), to_blocks(values), to_blocks(log_gate), to_blocks(fresh_share))
    final, outputs = lax.scan(jax.checkpoint(block_step), start, pieces)
    return (join_back(outputs[0]), join_back(outputs[1]), join_back(outputs[2]), final)

def mixer_base(query_rows, key_rows, value_rows, gate_logits, random_maps, block_size):
    query_feats = features(query_rows, random_maps)
    key_feats = features(key_rows, random_maps)
    values = jnp.transpose(value_rows, (0, 2, 1, 3))
    log_gate = jnp.transpose(jax.nn.log_sigmoid(gate_logits), (0, 2, 1))
    fresh_share = jnp.transpose(jax.nn.sigmoid(-gate_logits), (0, 2, 1))
    numerator, denominator, cumulative, final = run_blocks(query_feats, key_feats, values, log_gate, fresh_share, block_size)
    return (numerator, denominator, cumulative, query_feats, jnp.exp(final[2]), final[0], final[1])

def block_forward(inputs, mix_weight, gate_weight, gate_bias, out_weight, gain_first, shift_first, gain_second, shift_second, up_weight, down_weight, random_maps):
    seq_count, length, model_width = inputs.shape
    head_count = gate_bias.shape[0]
    head_size = model_width // head_count
    normed = low(norm_rows(inputs, gain_first, shift_first))
    mixed_rows = low(low_back(product('bld,de->ble', normed, mix_weight)))
    gate_logits = low_back(product('bld,dh->blh', normed, gate_weight)) + gate_bias
    split_rows = mixed_rows.reshape(seq_count, length, 3, head_count, head_size)
    based = mixer_base(split_rows[:, :, 0], split_rows[:, :, 1], split_rows[:, :, 2], gate_logits, random_maps, BLOCK)
    numerator, denominator = (based[0], based[1])
    attended = numerator / jnp.sqrt(denominator * denominator + 1.0)[..., None]
    attended = low(jnp.transpose(attended, (0, 2, 1, 3)).reshape(seq_count, length, model_width))
    branch = low_back(product('bld,de->ble', attended, out_weight))
    middle = inputs + branch
    normed_two = low(norm_rows(middle, gain_second, shift_second))
    pre_act = low_back(product('bld,df->blf', normed_two, up_weight))
    hidden = low(jax.nn.gelu(pre_act, approximate=False))
    return middle + low_back(product('blf,fd->bld', hidden, down_weight))

def reference(inputs, cotangent, mix_weight, gate_weight, gate_bias, out_weight, gain_first, shift_first, gain_second, shift_second, up_weight, down_weight, random_maps):
    params = tuple((tensor_arg.astype(jnp.float32) for tensor_arg in (mix_weight, gate_weight, gate_bias, out_weight, gain_first, shift_first, gain_second, shift_second, up_weight, down_weight)))
    maps_wide = random_maps.astype(jnp.float32)
    group_size = math.gcd(SEQS, max(1, 4096 // LEN))
    shaped_in = inputs.astype(jnp.float32).reshape(SEQS // group_size, group_size, LEN, D)
    shaped_ct = cotangent.astype(jnp.float32).reshape(SEQS // group_size, group_size, LEN, D)

    def forward_rows(rows, *weights):
        return block_forward(rows, *weights, maps_wide)

    def one_group(totals, group_pair):
        block_in, block_ct = group_pair
        result, pullback = jax.vjp(forward_rows, block_in, *params)
        pulled = pullback(block_ct)
        totals = tuple((running + adding for running, adding in zip(totals, pulled[1:])))
        return (totals, (result.astype(jnp.bfloat16), pulled[0]))
    zero_grads = tuple((jnp.zeros_like(param_arr) for param_arr in params))
    totals, stacked = lax.scan(one_group, zero_grads, (shaped_in, shaped_ct))
    output = stacked[0].reshape(SEQS, LEN, D)
    input_grad = stacked[1].reshape(SEQS, LEN, D)
    return (output, input_grad, totals[0], totals[1], totals[2], totals[3], totals[4], totals[5], totals[6], totals[7], totals[8], totals[9])
```

```python
import functools

import jax
import jax.numpy as jnp
from jax import lax
from jax.experimental import pallas as pl
from jax.experimental.pallas import tpu as pltpu
from jax.sharding import PartitionSpec as P

BOTH = ("dp", "tensor")
F32 = jnp.float32
BF16 = jnp.bfloat16
EPSILON = 1e-05
ROOT_HALF = 0.7071067811865476
DENSITY = 0.3989422804014327
SIN = (9.9999999998e-01, -1.6666666617e-01, 8.3333309689e-03, -1.9840860382e-04, 2.7525224003e-06, -2.3888330913e-08)
COS = (9.9999999978e-01, -4.9999999354e-01, 4.1666636104e-02, -1.3888359409e-03, 2.4760057595e-05, -2.6049626765e-07)

NN = (((1,), (0,)), ((), ()))
NT = (((1,), (1,)), ((), ()))
TN = (((0,), (0,)), ((), ()))


def mm(a, b, dims=NN):
    return lax.dot_general(a, b, dims, preferred_element_type=F32)


def low(a):
    return a.astype(BF16)


def lanes_of(shape):
    return lax.broadcasted_iota(jnp.int32, shape, len(shape) - 1)


def swap_halves(a):
    return pltpu.roll(a, 64, 1)


def sincos(a):
    turns = jnp.floor(a * 0.3183098861837907 + 0.5)
    r = (a - turns * 3.140625) - turns * 9.676535897932e-4
    half = turns * 0.5
    sign = 1.0 - 4.0 * (half - jnp.floor(half))
    r2 = r * r
    s = r * (SIN[0] + r2 * (SIN[1] + r2 * (SIN[2] + r2 * (SIN[3] + r2 * (SIN[4] + r2 * SIN[5])))))
    c = COS[0] + r2 * (COS[1] + r2 * (COS[2] + r2 * (COS[3] + r2 * (COS[4] + r2 * COS[5]))))
    return sign * s, sign * c


def normal_parts(v):
    x = jnp.abs(v) * ROOT_HALF
    base = 1.0 + 0.3275911 * x
    t = pl.reciprocal(base, approx=True)
    t = t * (2.0 - base * t)
    bell = jnp.exp(-0.5 * v * v)
    poly = t * (0.254829592 + t * (-0.284496736 + t * (1.421413741 + t * (-1.453152027 + t * 1.061405429))))
    tail = 0.5 * poly * bell
    return jnp.where(v >= 0.0, 1.0 - tail, tail), DENSITY * bell


def three_parts(a):
    high = a.astype(BF16)
    rest = a - high.astype(F32)
    mid = rest.astype(BF16)
    return high, mid, (rest - mid.astype(F32)).astype(BF16)


def tri_sum(tri, a):
    high, mid, rest = three_parts(a)
    return mm(tri, high) + (mm(tri, mid) + mm(tri, rest))


def norm_of(x):
    mean = jnp.mean(x, axis=-1, keepdims=True)
    centered = x - mean
    inv = lax.rsqrt(jnp.mean(centered * centered, axis=-1, keepdims=True) + EPSILON)
    return centered * inv, inv


def norm_back(s, unit, inv):
    return inv * (
        s
        - jnp.mean(s, axis=-1, keepdims=True)
        - unit * jnp.mean(s * unit, axis=-1, keepdims=True)
    )


def chip_row(pos, mz, mx, my):
    return (((pos[0] ^ mz) * 2 + (pos[1] ^ mx)) * 2 + (pos[2] ^ my)) * 32


def lower_tri(n):
    row = lax.broadcasted_iota(jnp.int32, (n, n), 0)
    col = lax.broadcasted_iota(jnp.int32, (n, n), 1)
    return row, col


def unpack_states(pack, b, zcols, last=65):
    lane = lanes_of((128, 128))
    out = []
    for p in range(2):
        both = pack[2 * b + p].astype(F32)
        for h, mat in ((2 * p, both), (2 * p + 1, swap_halves(both))):
            z = jnp.sum(jnp.where(lane == 4 * b + h, zcols, 0.0), axis=1, keepdims=True)
            out.append(jnp.where(lane < 64, mat, jnp.where(lane <= last, z, 0.0)))
    return out


def pack_states(states, pack_o, b, last, split=False):
    lane = lanes_of((128, 128))
    zcols = jnp.where(b == 0, 0.0, pack_o[last].astype(F32))

    def sum_of(s):
        return s[:, 64:65] + s[:, 65:66] if split else s[:, 64:65]

    for p in range(2):
        s0, s1 = states[2 * p], states[2 * p + 1]
        pack_o[2 * b + p] = jnp.where(lane < 64, s0, swap_halves(s1)).astype(BF16)
        zcols = jnp.where(lane == 4 * b + 2 * p, sum_of(s0), zcols)
        zcols = jnp.where(lane == 4 * b + 2 * p + 1, sum_of(s1), zcols)
    pack_o[last] = zcols.astype(BF16)


def project_kernel(
    b, pos, own, oth, w0, w1, w2, w3, bias, maps,
    a_o, fq_o, fk_o, fql_o, fkl_o, va_o, ccol_o, ucol_o, crow_o, urow_o, smid_o, pack_o, wmix_o, vec_o, vbar_o,
):
    chunk = own.shape[1]
    nz = w0.shape[0]

    @pl.when(b == 0)
    def _():
        for piece, (my, mx) in ((w0, (0, 0)), (w1, (0, 1)), (w2, (1, 0)), (w3, (1, 1))):
            for mz in range(nz):
                base = chip_row(pos, mz, mx, my)
                for mc in range(2):
                    row = pl.multiple_of(base + (pos[3] ^ mc) * 16, 16)
                    wmix_o[pl.ds(row, 16), :] = piece[mz, mc]
        vec_o[...] = wmix_o[:, 768:896].astype(F32).T[0:8]
        vbar_o[...] = mm(jnp.broadcast_to(vec_o[5:6], vec_o.shape).astype(BF16), wmix_o[:, 512:768])

    gain, shift = vec_o[4:5], vec_o[5:6]
    first = pos[3] == 0
    row, col = lower_tri(chunk)
    tri = jnp.where(row >= col, 1.0, 0.0).astype(BF16)
    lane = lanes_of((chunk, 128))
    states = [None] * 4
    for j in range(2):
        rows = slice(j * chunk, (j + 1) * chunk)
        mine, theirs = own[0], oth[0]
        x = jnp.where(first == (j == 0), mine, theirs).astype(F32)
        unit, _ = norm_of(x)
        a = (unit * gain + shift).astype(BF16)
        a_o[0, rows] = a
        mixed = mm(a, wmix_o[:, 0:768]).astype(BF16)
        logits = jnp.where(lane < 4, mm(a, wmix_o[:, 768:896]) + bias[...], 0.0)
        e = jnp.exp(-jnp.abs(logits))
        w = 1.0 + e
        log1 = jnp.where(w == 1.0, e, jnp.log(w) * (e / jnp.where(w == 1.0, 1.0, w - 1.0)))
        log_gate = jnp.minimum(logits, 0.0) - log1
        fresh = jnp.where(logits >= 0.0, e, 1.0) / w
        cum = tri_sum(tri, log_gate)
        ccol_o[0, rows] = cum
        ucol_o[0, rows] = fresh
        crow_o[0, j] = cum.T[0:8]
        urow_o[0, j] = fresh.T[0:8]
        dout = jnp.exp(cum[chunk - 1 : chunk] - cum) * fresh
        for p in range(2):
            for base, target, rest in ((0, fq_o, fql_o), (256, fk_o, fkl_o)):
                angles = mm(mixed[:, base + 128 * p : base + 128 * p + 128], maps[p])
                s, c = sincos(angles)
                for h, f in (
                    (2 * p, jnp.where(lane < 64, s, swap_halves(c))),
                    (2 * p + 1, jnp.where(lane < 64, swap_halves(s), c)),
                ):
                    high = low(f)
                    target[0, h, rows] = high
                    rest[0, h, rows] = low(f - high.astype(F32))
            v = mixed[:, 512 + 128 * p : 640 + 128 * p].astype(F32) - vbar_o[0:1, 128 * p : 128 * p + 128]
            one = jnp.where((lane == 64) | (lane == 65), 1.0, 0.0)
            for h, vh in ((2 * p, v), (2 * p + 1, swap_halves(v))):
                aug = jnp.where(lane < 64, vh, one)
                va_o[0, h, rows] = aug.astype(BF16)
                local = mm(fk_o[0, h, rows], low(aug * dout[:, h : h + 1]), TN)
                if j == 0:
                    states[h] = local
                    smid_o[0, h] = local
                else:
                    states[h] = states[h] * jnp.exp(cum[chunk - 1 : chunk, h : h + 1]) + local
    pack_states(states, pack_o, b, pack_o.shape[0] - 1)


def weights_of(ccol, ucol_row, crow, row, col):
    gap = jnp.minimum(ccol - crow, 0.0)
    return jnp.where(row >= col, jnp.exp(gap), 0.0) * ucol_row


def scores(fq, fk, fql, fkl, h, rows):
    q, k = fq[0, h, rows], fk[0, h, rows]
    return mm(
        jnp.concatenate([q, fql[0, h, rows], q], axis=1), jnp.concatenate([k, k, fkl[0, h, rows]], axis=1), NT
    )


def local_kernel(b, fq, fk, fql, fkl, va, ccol, crow, urow, o_o):
    chunk = crow.shape[3]
    row, col = lower_tri(chunk)
    for j in range(2):
        rows = slice(j * chunk, (j + 1) * chunk)
        for h in range(4):
            w = weights_of(ccol[0, rows, h : h + 1], urow[0, j, h : h + 1], crow[0, j, h : h + 1], row, col)
            qk = scores(fq, fk, fql, fkl, h, rows)
            o_o[0, h, rows] = mm(low(qk * w), va[0, h, rows])


def mean_of(vbar, h):
    pair = vbar[:, 128 * (h // 2) : 128 * (h // 2) + 128]
    return (pair if h % 2 == 0 else swap_halves(pair))[0:1]


def finish_kernel(b, pos, o_loc, fq, ccol, pack, smid, vbar, o_o, st_o, keep_o, send_o):
    chunk = ccol.shape[1] // 2
    zcols = pack[pack.shape[0] - 1].astype(F32)
    states = unpack_states(pack, b, zcols)
    lane = lanes_of((chunk, 128))
    cend = ccol[0, chunk - 1 : chunk]
    att = [[None] * 4, [None] * 4]
    for h in range(4):
        s0 = states[h]
        s1 = jnp.exp(cend[:, h : h + 1]) * s0 + smid[0, h]
        for j, s in ((0, s0), (1, s1)):
            rows = slice(j * chunk, (j + 1) * chunk)
            near = low(s)
            st_o[0, h, j] = near
            o = o_loc[0, h, rows] + jnp.exp(ccol[0, rows, h : h + 1]) * mm(fq[0, h, rows], near)
            o_o[0, h, rows] = o
            den = o[:, 64:65]
            att[j][h] = (o + den * mean_of(vbar, h)) * lax.rsqrt(den * den + 1.0)
    first = pos[3] == 0
    for p in range(2):
        both = [
            jnp.where(lane < 64, att[j][2 * p], swap_halves(att[j][2 * p + 1])) for j in range(2)
        ]
        keep_o[0, :, 128 * p : 128 * p + 128] = jnp.where(first, both[0], both[1]).astype(BF16)
        send_o[0, :, 128 * p : 128 * p + 128] = jnp.where(first, both[1], both[0]).astype(BF16)


def feed_kernel(
    pos, akeep, arecv, x, cot, vec, q0, q1, q2, q3, q4, q5, q6, q7,
    out_o, gm_o, gak_o, gas_o, gsend_o, gkeep_o, gv_o,
    up_s, dn_s, ow_s, feed_s, feedt_s, cott_s, att_s, hid_s, gp_s, gb_s, mid_s, unit_s, acc_s, gf_s, big_s,
):
    seqs, chunk, width = x.shape
    nz = q0.shape[0]
    pieces = (q0, q1, q2, q3, q4, q5, q6, q7)
    z, xbit, y, c = pos[0], pos[1], pos[2], pos[3]
    rows_up = up_s.shape[1] // (2 * nz)

    def dp_of(mz, mx):
        return (z ^ mz) * 2 + (xbit ^ mx)

    for mc in range(2):
        for my in range(2):
            t = (y ^ my) * 2 + (c ^ mc)
            for mx in range(2):
                piece = pieces[(mc * 2 + my) * 2 + mx]
                for mz in range(nz):
                    d = dp_of(mz, mx)
                    at = pl.multiple_of(d * rows_up, rows_up)
                    up_s[mc * 2 + my, pl.ds(at, rows_up), :] = piece[mz, 0:rows_up]
                    dn_s[mc * 2 + my, pl.ds(at, rows_up), :] = piece[mz, rows_up : 2 * rows_up]
                    ow_s[pl.ds(pl.multiple_of((d * 4 + t) * 16, 16), 16), :] = piece[mz, 2 * rows_up :]
    first = c == 0
    gain, shift = vec[6:7], vec[7:8]
    for r in range(seqs):
        rows = slice(r * chunk, (r + 1) * chunk)
        mine, theirs = akeep[r], arecv[r]
        att = jnp.concatenate(
            [jnp.where(first, mine, theirs), jnp.where(first, theirs, mine)], axis=1
        )
        att_s[rows] = att
        mid = x[r].astype(F32) + mm(att, ow_s[...])
        mid_s[rows] = mid
        unit, inv = norm_of(mid)
        unit_s[rows] = unit
        feed_s[rows] = (unit * gain + shift).astype(BF16)
        cott_s[:, rows] = cot[r].astype(F32).T.astype(BF16)
        feedt_s[:, rows] = (unit * gain + shift).T.astype(BF16)
    acc_s[...] = jnp.zeros_like(acc_s)
    gf_s[...] = jnp.zeros_like(gf_s)

    def scatter(source, target, my, offset, nrows):
        for mx in range(2):
            for mz in range(nz):
                at = pl.multiple_of(dp_of(mz, mx) * nrows, nrows)
                target[my, mx, mz, offset : offset + nrows, :] = source[pl.ds(at, nrows), :]

    for mc, target in ((1, gsend_o), (0, gkeep_o)):

        def one(my, carry, mc=mc, target=target):
            k = mc * 2 + my
            up, dn = up_s[k], dn_s[k]
            for r in range(seqs):
                rows = slice(r * chunk, (r + 1) * chunk)
                pre = mm(feed_s[rows], up)
                cdf, pdf = normal_parts(pre)
                hid = (pre * cdf).astype(BF16)
                gp = (mm(cot[r], dn) * (cdf + pre * pdf)).astype(BF16)
                hid_s[rows] = hid
                gp_s[rows] = gp
                acc_s[rows] += mm(hid, dn, NT)
                gf_s[rows] += mm(gp, up, NT)
            big_s[...] = mm(feedt_s[...], gp_s[...]).astype(BF16)
            scatter(big_s, target, my, 0, rows_up)
            big_s[...] = mm(cott_s[...], hid_s[...]).astype(BF16)
            scatter(big_s, target, my, rows_up, rows_up)
            return carry

        lax.fori_loop(0, 2, one, 0)

    gain_sum = jnp.zeros((1, width), F32)
    shift_sum = jnp.zeros((1, width), F32)
    for r in range(seqs):
        rows = slice(r * chunk, (r + 1) * chunk)
        mid = mid_s[rows]
        out_o[r] = (mid + acc_s[rows]).astype(BF16)
        unit = unit_s[rows]
        _, inv = norm_of(mid)
        gf = gf_s[rows]
        gain_sum += jnp.sum(gf * unit, axis=0, keepdims=True)
        shift_sum += jnp.sum(gf, axis=0, keepdims=True)
        gm = cot[r].astype(F32) + norm_back(gf * gain, unit, inv)
        gm_o[r] = gm
        gb = gm.astype(BF16)
        gb_s[rows] = gb
        ga = mm(gb, ow_s[...], NT).astype(BF16)
        half = width // 2
        gak_o[r] = jnp.where(first, ga[:, :half], ga[:, half:])
        gas_o[r] = jnp.where(first, ga[:, half:], ga[:, :half])
    gv_o[...] = jnp.concatenate([gain_sum, shift_sum, jnp.zeros((6, width), F32)], axis=0)
    big_s[...] = mm(att_s[...], gb_s[...], TN).astype(BF16)
    for mc, target in ((0, gkeep_o), (1, gsend_o)):
        for my in range(2):
            t = (y ^ my) * 2 + (c ^ mc)
            for mx in range(2):
                for mz in range(nz):
                    at = pl.multiple_of((dp_of(mz, mx) * 4 + t) * 16, 16)
                    target[my, mx, mz, 2 * rows_up :, :] = big_s[pl.ds(at, 16), :]


def adjoint_kernel(b, pos, gak, gar, o_all, fq, ccol, vbar, g_o, l1_o, pack_o):
    chunk = ccol.shape[1] // 2
    lane = lanes_of((chunk, 128))
    first = pos[3] == 0
    states = [None] * 4
    for j in range(2):
        rows = slice(j * chunk, (j + 1) * chunk)
        for p in range(2):
            cols = slice(128 * p, 128 * p + 128)
            pair = jnp.where(first == (j == 0), gak[0, :, cols], gar[0, :, cols]).astype(F32)
            for h, ga in ((2 * p, pair), (2 * p + 1, swap_halves(pair))):
                o = o_all[0, h, rows]
                den = o[:, 64:65]
                inv = lax.rsqrt(den * den + 1.0)
                gn = jnp.where(lane < 64, ga * inv, 0.0).astype(BF16).astype(F32)
                mean = mean_of(vbar, h)
                share = den * inv * inv
                gd = jnp.sum(gn * (mean - share * (o + den * mean)), axis=1, keepdims=True)
                high = gd.astype(BF16).astype(F32)
                g = jnp.where(lane == 64, high, jnp.where(lane == 65, gd - high, gn))
                g_o[0, h, rows] = low(g)
                decay = jnp.exp(ccol[0, rows, h : h + 1])
                local = mm(fq[0, h, rows], low(g * decay), TN)
                if j == 0:
                    states[h] = local
                else:
                    l1_o[0, h] = local
                    states[h] = states[h] + jnp.exp(ccol[0, chunk - 1 : chunk, h : h + 1]) * local
    pack_states(states, pack_o, b, pack_o.shape[0] - 1, split=True)


def local_back_kernel(b, fq, fk, fql, fkl, va, g, st, ccol, crow, urow, dfq_o, dfk_o, dva_o):
    chunk = crow.shape[3]
    row, col = lower_tri(chunk)
    for j in range(2):
        rows = slice(j * chunk, (j + 1) * chunk)
        for h in range(4):
            w = weights_of(ccol[0, rows, h : h + 1], urow[0, j, h : h + 1], crow[0, j, h : h + 1], row, col)
            q, k, v, gh = fq[0, h, rows], fk[0, h, rows], va[0, h, rows], g[0, h, rows]
            attn = low(scores(fq, fk, fql, fkl, h, rows) * w)
            dp = low(mm(gh, v, NT) * w)
            decay = jnp.exp(ccol[0, rows, h : h + 1])
            dfq_o[0, h, rows] = mm(dp, k) + decay * mm(gh, st[0, h, j], NT)
            dfk_o[0, h, rows] = mm(dp, q, TN)
            dva_o[0, h, rows] = mm(attn, gh, TN)


def close_kernel(
    b, pos, own, oth, a, fq, fk, va, dfq, dfk, dva, ccol, ucol, pack, l1, st, wmix, vec, gv, back,
    m00_o, m01_o, m10_o, m11_o, gnk_o, gns_o,
    acc_s, gate_s, vsum_s, big_s,
    *, seqs_total,
):
    seqs = seqs_total
    chunk = own.shape[1]
    nz = m00_o.shape[0]
    lane = lanes_of((chunk, 128))
    row, col = lower_tri(chunk)
    upper = jnp.where(row <= col, 1.0, 0.0).astype(BF16)
    zcols = pack[pack.shape[0] - 1].astype(F32)
    arrived = unpack_states(pack, b, zcols, last=64)
    wide = lanes_of((128, 128))
    first = pos[3] == 0

    @pl.when(b == 0)
    def _():
        acc_s[...] = jnp.zeros_like(acc_s)
        gate_s[...] = jnp.zeros_like(gate_s)
        vsum_s[...] = jnp.zeros_like(vsum_s)

    gain_sum = jnp.zeros((1, own.shape[2]), F32)
    shift_sum = jnp.zeros((1, own.shape[2]), F32)
    bias_sum = jnp.zeros((1, 128), F32)
    normed = [None, None]
    for j in range(2):
        rows = slice(j * chunk, (j + 1) * chunk)
        cum, fresh = ccol[0, rows], ucol[0, rows]
        dout = jnp.exp(cum[chunk - 1 : chunk] - cum) * fresh
        kd = jnp.zeros((chunk, 128), F32)
        qd = jnp.zeros((chunk, 128), F32)
        level = jnp.zeros((1, 128), F32)
        grads = [None] * 6
        for p in range(2):
            dvs, pq, pk = [None, None], [None, None], [None, None]
            for i in range(2):
                h = 2 * p + i
                adj = arrived[h]
                if j == 0:
                    adj = l1[0, h] + jnp.exp(ccol[0, 2 * chunk - 1 : 2 * chunk, h : h + 1]) * adj
                zs = adj[:, 64:65] + adj[:, 65:66]
                high = zs.astype(BF16).astype(F32)
                near = low(jnp.where(wide == 64, high, jnp.where(wide == 65, zs - high, adj)))
                d = dout[:, h : h + 1]
                keys = fk[0, h, rows]
                keys32 = keys.astype(F32)
                dk_far = d * mm(va[0, h, rows], near, NT)
                dk_near = dfk[0, h, rows]
                dvs[i] = dva[0, h, rows] + d * mm(keys, near)
                kd_far = jnp.sum(keys32 * dk_far, axis=1, keepdims=True)
                kd_near = jnp.sum(keys32 * dk_near, axis=1, keepdims=True)
                kd = jnp.where(lane == h, kd_far + kd_near, kd)
                passed = st[0, h, j].astype(F32) * near.astype(F32)
                passed = jnp.sum(jnp.sum(passed, axis=1, keepdims=True), axis=0, keepdims=True)
                total = jnp.sum(kd_far, axis=0, keepdims=True) + jnp.exp(cum[chunk - 1 : chunk, h : h + 1]) * passed
                level = jnp.where(lanes_of((1, 128)) == h, total, level)
                dk = dk_far + dk_near
                pk[i] = low(dk * swap_halves(keys32))
                dq, queries32 = dfq[0, h, rows], fq[0, h, rows].astype(F32)
                qd = jnp.where(lane == h, jnp.sum(queries32 * dq, axis=1, keepdims=True), qd)
                pq[i] = low(dq * swap_halves(queries32))
            grads[p] = mm(jnp.concatenate(pq, axis=1), back[p])
            grads[2 + p] = mm(jnp.concatenate(pk, axis=1), back[p])
            grads[4 + p] = jnp.where(lane < 64, dvs[0], swap_halves(dvs[1]))
        flow = qd - kd
        dlog = tri_sum(upper, flow) + level
        dlogit = jnp.where(lane < 4, fresh * dlog - (1.0 - fresh) * kd, 0.0)
        bias_sum += jnp.sum(dlogit, axis=0, keepdims=True)
        gm = jnp.concatenate([g.astype(BF16) for g in grads] + [dlogit.astype(BF16)], axis=1)
        acc_s[...] += mm(a[0, rows], gm, TN)
        back_in = mm(gm, wmix[...], NT)
        x = jnp.where(first == (j == 0), own[0], oth[0]).astype(F32)
        unit, _ = norm_of(x)
        gain_sum += jnp.sum(back_in * unit, axis=0, keepdims=True)
        shift_sum += jnp.sum(back_in, axis=0, keepdims=True)
        normed[j] = back_in
    gnk_o[0] = jnp.where(first, normed[0], normed[1])
    gns_o[0] = jnp.where(first, normed[1], normed[0]).astype(BF16)
    vsum_s[0:1] += gain_sum
    vsum_s[1:2] += shift_sum
    gate_s[0:1] += bias_sum

    @pl.when(b == seqs - 1)
    def _():
        width = vsum_s.shape[1]
        table = jnp.concatenate(
            [jnp.zeros((4, width), F32), vsum_s[0:2], gv[0:2], jnp.zeros((120, width), F32)], axis=0
        ).T
        total = gate_s[0:1]
        high = low(total).astype(F32)
        rest = jnp.broadcast_to(total - high, (8, 128))
        both = pltpu.roll(jnp.broadcast_to(high, (8, 128)), 8, 1) + pltpu.roll(rest, 12, 1)
        biases = jnp.broadcast_to(both[0:1], (width, 128))
        side = jnp.where(lanes_of((width, 128)) < 4, acc_s[:, 768:896], table) + biases
        big_s[:, 0:768] = acc_s[:, 0:768].astype(BF16)
        big_s[:, 768:896] = side.astype(BF16)
        for my in range(2):
            for mx in range(2):
                for mz in range(nz):
                    at = pl.multiple_of(chip_row(pos, mz, mx, my), 32)
                    (m00_o, m01_o, m10_o, m11_o)[2 * my + mx][mz] = big_s[pl.ds(at, 32), :]


def input_kernel(b, x, gm, keep, recv, vec, o):
    unit, inv = norm_of(x[0].astype(F32))
    grad = keep[0] + recv[0].astype(F32)
    o[0] = gm[0] + norm_back(grad * vec[4:5], unit, inv)


def join_kernel(*refs):
    for i, ref in enumerate(refs[:-1]):
        refs[-1][i] = ref[...]


def pair_sum_kernel(keep, recv, *outs):
    for i, out in enumerate(outs):
        out[...] = (keep[i // 2, i % 2].astype(F32) + recv[i // 2, i % 2].astype(F32)).astype(out.dtype)


def four_sum_kernel(a, b, c, d, out, *, carry):
    total = (a[...].astype(F32) + b[...].astype(F32)) + (c[...].astype(F32) + d[...].astype(F32))
    if carry:
        side = total[..., 768:896]
        rest = side - low(side).astype(F32)
        lane = lanes_of(side.shape)
        moved = jnp.where((lane >= 12) & (lane < 16), side + pltpu.roll(rest, 4, side.ndim - 1), side)
        out[..., 0:768] = low(total[..., 0:768])
        out[..., 768:896] = low(moved)
    else:
        out[...] = total.astype(out.dtype)


def call(kernel, steps, ins, outs, scratch=(), flops=0, name=None, limit=14):
    def spec(kind):
        if kind == "d":
            return pl.BlockSpec(memory_space=pl.ANY)
        return pl.BlockSpec(memory_space=pltpu.SMEM if kind == "m" else pltpu.VMEM)

    kinds = [kind for kind, _ in ins]
    out_kinds = [kind for kind, _, _ in outs]
    all_kinds = kinds + out_kinds + ["w"] * len(scratch)

    def run(*refs):
        used = [(kind, ref) for kind, ref in zip(all_kinds, refs) if kind != "d"]
        if not steps:
            kernel(*[ref for _, ref in used])
            return

        def one(b, carry):
            kernel(b, *[ref.at[pl.ds(b, 1)] if kind == "s" else ref for kind, ref in used])
            return carry

        lax.fori_loop(0, steps, one, 0)

    return pl.pallas_call(
        run,
        in_specs=[spec(kind) for kind in kinds],
        out_specs=[spec(kind) for kind in out_kinds],
        out_shape=[jax.ShapeDtypeStruct(shape, dtype) for _, shape, dtype in outs],
        scratch_shapes=list(scratch),
        compiler_params=pltpu.CompilerParams(vmem_limit_bytes=limit * 1024 * 1024),
        cost_estimate=pl.CostEstimate(flops=flops, bytes_accessed=1000000, transcendentals=0),
        name=name,
    )(*[a for _, a in ins])


def xor_with(a, mask, count):
    return lax.ppermute(a, BOTH, [(i, i ^ mask) for i in range(count)])


def body(
    inputs, cotangent, mix_weight, gate_weight, gate_bias, out_weight, gain_first, shift_first, gain_second,
    shift_second, up_weight, down_weight, random_maps,
):
    dp, tensor = lax.axis_size("dp"), lax.axis_size("tensor")
    count = dp * tensor
    place_dp, place_t = lax.axis_index("dp"), lax.axis_index("tensor")
    seqs, chunk, width = inputs.shape
    heads, head = random_maps.shape[0], random_maps.shape[1]
    hidden = up_weight.shape[1]
    core = place_t % 2
    first = core == 0
    direct = dp == 8
    nz = 4
    if direct:
        pos = jnp.stack([place_dp // 2, place_dp % 2, place_t // 2, core]).astype(jnp.int32)
    else:
        pos = jnp.stack([jnp.zeros_like(core)] * 3 + [core]).astype(jnp.int32)
    swap_core = functools.partial(xor_with, mask=1, count=count)

    def mix_pack(mix_w, gate_w, vecs):
        rows = mix_w.shape[0]
        split = mix_w.reshape(rows, 3, 2, width // 2)
        sides = [v[:, None] for v in vecs]
        pad = jnp.zeros((rows, 120), BF16)
        return [
            jnp.concatenate(
                [split[:, 0, s], split[:, 1, s], split[:, 2, s], gate_w[:, 4 * s : 4 * s + 4]] + sides + [pad], axis=1
            )
            for s in range(2)
        ]

    def join(parts, after=()):
        (out,) = call(
            join_kernel, 0, [("w", a) for a in parts] + [("d", a) for a in after],
            [("w", (len(parts), *parts[0].shape), parts[0].dtype)], name="join",
        )
        return out

    def sum_four(parts, dtype, after=(), carry=False):
        shape = parts[0].shape
        (out,) = call(
            functools.partial(four_sum_kernel, carry=carry), 0,
            [("w", a) for a in parts] + [("d", a) for a in after], [("w", shape, dtype)], name="sum_four",
        )
        return out

    other_in = swap_core(inputs)
    vectors = (gain_first, shift_first, gain_second, shift_second)
    if direct:
        rows = mix_weight.shape[0]

        def half(which):
            def placed(a, at):
                return lax.pad(a, jnp.zeros((), BF16), [(0, 0, 0), (at, 896 - at - a.shape[1], 0)])

            parts = [
                placed(lax.dynamic_slice(mix_weight, (0, width * i + (width // 2) * which), (rows, width // 2)), 256 * i)
                for i in range(3)
            ]
            parts.append(placed(lax.dynamic_slice(gate_weight, (0, 4 * which), (rows, 4)), 768))
            parts += [placed(v[:, None], 772 + i) for i, v in enumerate(vectors)]
            return functools.reduce(jnp.add, parts)

        keep, send = half(core), half(1 - core)
        pair = join([keep, swap_core(send)])
        line = join([pair] + [xor_with(pair, 8 * m, count) for m in range(1, nz)])
        w_pieces = [line] + [xor_with(line, m, count) for m in (4, 2, 6)]
        block = jnp.concatenate([up_weight, down_weight.T, out_weight], axis=0)
        (block,) = call(
            lambda a, out: out.__setitem__(..., a[...]), 0, [("w", block), ("d", line)],
            [("w", block.shape, BF16)], name="hold",
        )
        ff_line = join([block] + [xor_with(block, 8 * m, count) for m in range(1, nz)], after=w_pieces)
        ff_pieces = [ff_line] + [xor_with(ff_line, m, count) for m in (4, 2, 6)]
        ff_pieces = ff_pieces + [swap_core(piece) for piece in ff_pieces]
    else:
        whole = [
            lax.all_gather(a, BOTH, axis=0, tiled=True) for a in (mix_weight, gate_weight, out_weight) + vectors
        ]
        p0, p1 = mix_pack(whole[0], whole[1], whole[3:])
        blocks = jnp.where(first, p0, p1).reshape(nz, 2, 2, 2, 16, 896)
        blocks = jnp.where(first, blocks, blocks[:, :, :, ::-1])
        w_pieces = [blocks[:, mx, my] for my, mx in ((0, 0), (0, 1), (1, 0), (1, 1))]
        up_all = lax.all_gather(up_weight, BOTH, axis=0, tiled=False).reshape(dp, tensor, -1, hidden)
        dn_all = lax.all_gather(down_weight.T, BOTH, axis=0, tiled=False).reshape(dp, tensor, -1, hidden)
        up_all = jnp.moveaxis(up_all, 1, 0).reshape(2, 2, nz, 2, -1, hidden)
        dn_all = jnp.moveaxis(dn_all, 1, 0).reshape(2, 2, nz, 2, -1, hidden)
        out_all = whole[2].reshape(nz, 2, 2, 2, 16, width).transpose(2, 3, 0, 1, 4, 5)
        ff_all = jnp.concatenate([up_all, dn_all, out_all], axis=4)
        ff_all = jnp.where(first, ff_all, ff_all[:, ::-1])
        ff_pieces = [ff_all[my, mc, :, mx] for mc in range(2) for my in range(2) for mx in range(2)]

    maps = lax.dynamic_slice_in_dim(random_maps, core * 4, 4, 0)
    zero = jnp.zeros((head, head), BF16)
    maps_pair = jnp.stack(
        [
            jnp.concatenate(
                [jnp.concatenate([maps[2 * p], zero], 1), jnp.concatenate([zero, maps[2 * p + 1]], 1)], 0
            )
            for p in range(2)
        ]
    )
    flip = jnp.swapaxes(maps, 1, 2)
    maps_back = jnp.stack(
        [
            jnp.concatenate(
                [
                    jnp.concatenate([flip[2 * p], zero], 1),
                    jnp.concatenate([-flip[2 * p], zero], 1),
                    jnp.concatenate([zero, flip[2 * p + 1]], 1),
                    jnp.concatenate([zero, -flip[2 * p + 1]], 1),
                ],
                0,
            )
            for p in range(2)
        ]
    )
    bias = jnp.pad(lax.dynamic_slice_in_dim(gate_bias, core * 4, 4, 0), (0, 124))[None]

    long = 2 * chunk
    tokens = seqs * long
    feats = (seqs, 4, long, 128)
    npack = 2 * seqs + 1
    attend, fq, fk, fql, fkl, va, ccol, ucol, crow, urow, smid, pack, wmix, vec, vbar = call(
        project_kernel, seqs,
        [("m", pos), ("s", inputs), ("s", other_in)] + [("w", w) for w in w_pieces] + [("w", bias), ("w", maps_pair)],
        [
            ("s", (seqs, long, width), BF16), ("s", feats, BF16), ("s", feats, BF16), ("s", feats, BF16), ("s", feats, BF16), ("s", feats, BF16),
            ("s", (seqs, long, 128), F32), ("s", (seqs, long, 128), F32),
            ("s", (seqs, 2, 8, chunk), F32), ("s", (seqs, 2, 8, chunk), F32),
            ("s", (seqs, 4, 128, 128), F32),
            ("w", (npack, 128, 128), BF16), ("w", (width, 896), BF16), ("w", (8, width), F32),
            ("w", (8, width // 2), F32),
        ],
        flops=2 * tokens * width * 896, name="project",
    )
    ahead = [(i, i + 2) for i in range(count) if (i % tensor) < 2]
    arrived = lax.ppermute(pack, BOTH, ahead)
    (o_loc,) = call(
        local_kernel, seqs,
        [("s", fq), ("s", fk), ("s", fql), ("s", fkl), ("s", va), ("s", ccol), ("s", crow), ("s", urow)],
        [("s", feats, F32)], flops=2 * 2 * 24 * chunk * chunk * 128, name="local",
    )
    o_all, st, att_keep, att_send = call(
        finish_kernel, seqs,
        [("m", pos), ("s", o_loc), ("s", fq), ("s", ccol), ("w", arrived), ("s", smid), ("w", vbar)],
        [
            ("s", feats, F32), ("s", (seqs, 4, 2, 128, 128), BF16),
            ("s", (seqs, chunk, width // 2), BF16), ("s", (seqs, chunk, width // 2), BF16),
        ],
        flops=2 * 24 * chunk * 128 * 128, name="finish",
    )
    att_recv = swap_core(att_send)

    own = seqs * chunk
    nrows = ff_pieces[0].shape[1]
    payload = (2, 2, nz, nrows, hidden)
    output, grad_middle, ga_keep, ga_send, g_send, g_keep, grad_vec = call(
        feed_kernel, 0,
        [("m", pos)] + [("w", a) for a in (att_keep, att_recv, inputs, cotangent, vec, *ff_pieces)],
        [
            ("w", (seqs, chunk, width), BF16), ("w", (seqs, chunk, width), F32),
            ("w", (seqs, chunk, width // 2), BF16), ("w", (seqs, chunk, width // 2), BF16),
            ("w", payload, BF16), ("w", payload, BF16), ("w", (8, width), F32),
        ],
        scratch=[
            pltpu.VMEM((4, width, hidden), BF16), pltpu.VMEM((4, width, hidden), BF16),
            pltpu.VMEM((width, width), BF16),
            pltpu.VMEM((own, width), BF16), pltpu.VMEM((width, own), BF16), pltpu.VMEM((width, own), BF16),
            pltpu.VMEM((own, width), BF16), pltpu.VMEM((own, hidden), BF16), pltpu.VMEM((own, hidden), BF16),
            pltpu.VMEM((own, width), BF16), pltpu.VMEM((own, width), F32), pltpu.VMEM((own, width), F32),
            pltpu.VMEM((own, width), F32), pltpu.VMEM((own, width), F32), pltpu.VMEM((width, hidden), BF16),
        ],
        flops=12 * own * width * 4 * hidden, name="feed", limit=30,
    )
    ga_recv = swap_core(ga_send)

    if direct:
        g_recv = swap_core(g_send)
        s00, s01, s10, s11 = call(
            pair_sum_kernel, 0, [("w", g_keep), ("w", g_recv)], [("w", (nz, nrows, hidden), BF16)] * 4, name="pair_sum",
        )
        g_plane = [s00, xor_with(s01, 4, count), xor_with(s10, 2, count), xor_with(s11, 6, count)]
        before_adjoint = [s00]
    else:
        before_adjoint = []
        by_core = jnp.where(first, jnp.stack([g_keep, g_send]), jnp.stack([g_send, g_keep]))
        ordered = by_core.transpose(3, 2, 1, 0, 4, 5)
        rows_up = (nrows - 16) // 2
        ups = ordered[..., :rows_up, :].reshape(nz * 2, 4, rows_up, hidden).transpose(1, 0, 2, 3)
        dns = ordered[..., rows_up : 2 * rows_up, :].reshape(nz * 2, 4, rows_up, hidden).transpose(1, 0, 2, 3)
        ups = ups.reshape(4, dp, -1, hidden).transpose(1, 0, 2, 3)
        dns = dns.reshape(4, dp, -1, hidden).transpose(1, 0, 2, 3)
        outs = ordered[..., 2 * rows_up :, :].reshape(width, width)

        def reduced(a):
            return lax.psum_scatter(a.astype(F32).reshape(count, -1, a.shape[-1]), BOTH, scatter_dimension=0)

        up_grad, down_grad, out_grad = reduced(ups), reduced(dns).T, reduced(outs)

    g, l1, pack_b = call(
        adjoint_kernel, seqs,
        [("m", pos), ("s", ga_keep), ("s", ga_recv), ("s", o_all), ("s", fq), ("s", ccol), ("w", vbar)]
        + [("d", a) for a in before_adjoint],
        [
            ("s", feats, BF16), ("s", (seqs, 4, 128, 128), F32), ("w", (npack, 128, 128), BF16),
        ],
        flops=2 * 24 * chunk * 128 * 128, name="adjoint",
    )
    behind = [(i, i - 2) for i in range(count) if (i % tensor) >= 2]
    arrived_b = lax.ppermute(pack_b, BOTH, behind)
    dfq, dfk, dva = call(
        local_back_kernel, seqs,
        [("s", fq), ("s", fk), ("s", fql), ("s", fkl), ("s", va), ("s", g), ("s", st), ("s", ccol), ("s", crow), ("s", urow)],
        [("s", feats, F32), ("s", feats, F32), ("s", feats, F32)],
        flops=2 * 6 * 24 * chunk * chunk * 128, name="local_back",
    )
    before_close = []
    if direct:
        g_line = sum_four(g_plane, BF16, after=[dfq])
        before_close = [g_line]
    m00, m01, m10, m11, gn_keep, gn_send = call(
        functools.partial(close_kernel, seqs_total=seqs), seqs,
        [("m", pos), ("s", inputs), ("s", other_in), ("s", attend), ("s", fq), ("s", fk), ("s", va), ("s", dfq),
         ("s", dfk), ("s", dva), ("s", ccol), ("s", ucol), ("w", arrived_b), ("s", l1), ("s", st),
         ("w", wmix), ("w", vec), ("w", grad_vec), ("w", maps_back)]
        + [("d", a) for a in before_close],
        [
            *[("w", (nz, 32, 896), BF16)] * 4, ("s", (seqs, chunk, width), F32), ("s", (seqs, chunk, width), BF16),
        ],
        scratch=[
            pltpu.VMEM((width, 896), F32), pltpu.VMEM((8, 128), F32), pltpu.VMEM((8, width), F32),
            pltpu.VMEM((width, 896), BF16),
        ],
        flops=4 * tokens * width * 896, name="close",
    )
    gn_recv = swap_core(gn_send)
    (input_grad,) = call(
        input_kernel, seqs,
        [("s", inputs), ("s", grad_middle), ("s", gn_keep), ("s", gn_recv), ("w", vec)],
        [("s", (seqs, chunk, width), F32)], name="input_grad",
    )
    if direct:
        m_plane = sum_four(
            [m00, xor_with(m01, 4, count), xor_with(m10, 2, count), xor_with(m11, 6, count)], BF16, carry=True,
            after=[input_grad],
        )
        g_fin = sum_four([g_line[0]] + [xor_with(g_line[m], 8 * m, count) for m in range(1, nz)], F32)
        up_rows = up_weight.shape[0]
        up_grad, down_grad, out_grad = g_fin[:up_rows], g_fin[up_rows : 2 * up_rows].T, g_fin[2 * up_rows :]
        m_mine = sum_four(
            [m_plane[0]] + [xor_with(m_plane[m], 8 * m, count) for m in range(1, nz)], F32, after=[g_fin]
        )
        m_mine = m_mine.reshape(2, 16, 896)
        m_keep = jnp.where(first, m_mine[0], m_mine[1])
        m_recv = swap_core(jnp.where(first, m_mine[1], m_mine[0]))
    else:
        m_all = jnp.stack([jnp.stack([m00, m01]), jnp.stack([m10, m11])])
        mine_rows = m_all.transpose(2, 1, 0, 3, 4).reshape(count, -1, 896).astype(F32)
        keep_part = lax.psum_scatter(mine_rows * jnp.where(first, 1.0, 0.0), BOTH, scatter_dimension=0)
        far_part = lax.psum_scatter(mine_rows * jnp.where(first, 0.0, 1.0), BOTH, scatter_dimension=0)
        m_keep = jnp.where(first, keep_part, far_part)
        m_recv = jnp.where(first, far_part, keep_part)
    m_low = jnp.where(first, m_keep, m_recv)
    m_high = jnp.where(first, m_recv, m_keep)
    mix_grad = jnp.concatenate(
        [part[:, 256 * i : 256 * i + 256] for i in range(3) for part in (m_low, m_high)], axis=1
    )
    gate_grad = jnp.concatenate([m_low[:, 768:772], m_high[:, 768:772]], axis=1)
    bias_grad = jnp.concatenate([m[0, 776:780] + m[0, 780:784] for m in (m_low, m_high)])
    sides = m_keep[:, 772:776] + m_recv[:, 772:776]

    return (
        output, input_grad, mix_grad, gate_grad, bias_grad, out_grad,
        sides[:, 0], sides[:, 1], sides[:, 2], sides[:, 3], up_grad, down_grad,
    )


def solution(mesh):
    rows, spread = P(("dp", "tensor"), None), P(("dp", "tensor"))
    tokens = P("dp", "tensor", None)
    in_specs = (
        tokens, tokens, rows, rows, P(), rows, spread, spread, spread, spread, P("dp", "tensor"), P("tensor", "dp"), P(),
    )
    out_specs = (
        tokens, tokens, rows, rows, P(), rows, spread, spread, spread, spread, P("dp", "tensor"), P("tensor", "dp"),
    )
    return jax.shard_map(body, mesh=mesh, in_specs=in_specs, out_specs=out_specs, check_vma=False)
```

```python
import functools

import jax
import jax.numpy as jnp
from jax import lax
from jax.experimental import pallas as pl
from jax.experimental.pallas import tpu as pltpu
from jax.sharding import PartitionSpec as P

BOTH = ("dp", "tensor")
F32 = jnp.float32
BF16 = jnp.bfloat16
EPSILON = 1e-05
DENSITY = 0.3989422804014327
SIN = (9.9999999998e-01, -1.6666666617e-01, 8.3333309689e-03, -1.9840860382e-04, 2.7525224003e-06, -2.3888330913e-08)
COS = (9.9999999978e-01, -4.9999999354e-01, 4.1666636104e-02, -1.3888359409e-03, 2.4760057595e-05, -2.6049626765e-07)

NN = (((1,), (0,)), ((), ()))
NT = (((1,), (1,)), ((), ()))
TN = (((0,), (0,)), ((), ()))


def mm(a, b, dims=NN):
    return lax.dot_general(a, b, dims, preferred_element_type=F32)


def low(a):
    return a.astype(BF16)


def lanes_of(shape):
    return lax.broadcasted_iota(jnp.int32, shape, len(shape) - 1)


def swap_halves(a):
    return pltpu.roll(a, 64, 1)


def sincos(a):
    turns = jnp.floor(a * 0.3183098861837907 + 0.5)
    r = (a - turns * 3.140625) - turns * 9.676535897932e-4
    half = turns * 0.5
    sign = 1.0 - 4.0 * (half - jnp.floor(half))
    r2 = r * r
    s = r * (SIN[0] + r2 * (SIN[1] + r2 * (SIN[2] + r2 * (SIN[3] + r2 * (SIN[4] + r2 * SIN[5])))))
    c = COS[0] + r2 * (COS[1] + r2 * (COS[2] + r2 * (COS[3] + r2 * (COS[4] + r2 * COS[5]))))
    return sign * s, sign * c


def normal_parts(v):
    t = pl.reciprocal(1.0 + 0.23164189 * jnp.abs(v), approx=True)
    bell = jnp.exp(-0.5 * (v * v))
    poly = t * (0.127414796 + t * (-0.142248368 + t * (0.7107068705 + t * (-0.7265760135 + t * 0.5307027145))))
    tail = poly * bell
    return jnp.where(v >= 0.0, 1.0 - tail, tail), DENSITY * bell


def three_parts(a):
    high = a.astype(BF16)
    rest = a - high.astype(F32)
    mid = rest.astype(BF16)
    return high, mid, (rest - mid.astype(F32)).astype(BF16)


def tri_sum(tri, a):
    high, mid, rest = (part.astype(F32) for part in three_parts(a))
    packed = mm(tri, low(high + pltpu.roll(mid, 4, 1) + pltpu.roll(rest, 8, 1)))
    return packed + pltpu.roll(packed, 124, 1) + pltpu.roll(packed, 120, 1)


def norm_of(x):
    mean = jnp.mean(x, axis=-1, keepdims=True)
    centered = x - mean
    inv = lax.rsqrt(jnp.mean(centered * centered, axis=-1, keepdims=True) + EPSILON)
    return centered * inv, inv


def norm_back(s, unit, inv):
    return inv * (
        s
        - jnp.mean(s, axis=-1, keepdims=True)
        - unit * jnp.mean(s * unit, axis=-1, keepdims=True)
    )


def chip_row(pos, mz, mx, my):
    return (((pos[0] ^ mz) * 2 + (pos[1] ^ mx)) * 2 + (pos[2] ^ my)) * 32


def lower_tri(n):
    row = lax.broadcasted_iota(jnp.int32, (n, n), 0)
    col = lax.broadcasted_iota(jnp.int32, (n, n), 1)
    return row, col


def unpack_states(pack, b, zcols, last=65):
    lane = lanes_of((128, 128))
    out = []
    for p in range(2):
        both = pack[2 * b + p].astype(F32)
        for h, mat in ((2 * p, both), (2 * p + 1, swap_halves(both))):
            z = jnp.sum(jnp.where(lane == 4 * b + h, zcols, 0.0), axis=1, keepdims=True)
            out.append(jnp.where(lane < 64, mat, jnp.where(lane <= last, z, 0.0)))
    return out


def pack_states(states, pack_o, b, last, split=False):
    lane = lanes_of((128, 128))
    zcols = jnp.where(b == 0, 0.0, pack_o[last].astype(F32))

    def sum_of(s):
        return s[:, 64:65] + s[:, 65:66] if split else s[:, 64:65]

    for p in range(2):
        s0, s1 = states[2 * p], states[2 * p + 1]
        pack_o[2 * b + p] = jnp.where(lane < 64, s0, swap_halves(s1)).astype(BF16)
        zcols = jnp.where(lane == 4 * b + 2 * p, sum_of(s0), zcols)
        zcols = jnp.where(lane == 4 * b + 2 * p + 1, sum_of(s1), zcols)
    pack_o[last] = zcols.astype(BF16)


def pack_kernel(pos, mix, side, keep_o, send_o):
    width = mix.shape[1] // 6
    lane = lanes_of(side.shape)
    sides = side[...].astype(F32)
    moved = pltpu.roll(sides, 124, 1)
    halves = []
    for s, block in ((0, jnp.where(lane < 4, sides, moved)), (1, moved)):
        parts = [mix[:, (2 * i + s) * width : (2 * i + s + 1) * width] for i in range(3)]
        halves.append(jnp.concatenate(parts + [low(jnp.where(lane < 8, block, 0.0))], axis=1))
    first = pos[3] == 0
    keep_o[...] = jnp.where(first, halves[0], halves[1])
    send_o[...] = jnp.where(first, halves[1], halves[0])


def prepare_kernel(b, pos, own, oth, cot, unit_o, cott_o):
    chunk = own.shape[1]
    first = pos[3] == 0
    mine, theirs = own[0], oth[0]
    for j in range(2):
        unit, _ = norm_of(jnp.where(first == (j == 0), mine, theirs).astype(F32))
        unit_o[0, j * chunk : (j + 1) * chunk] = unit
    cott_o[0] = low(cot[0].astype(F32).T)


def project_kernel(
    b, pos, units, w0, w1, w2, w3, bias, maps,
    a_o, fq_o, fk_o, fql_o, fkl_o, va_o, ccol_o, ucol_o, crow_o, smid_o, pack_o, wmix_o, vec_o, vbar_o,
    w_s, sems,
):
    chunk = units.shape[1] // 2

    @pl.when(b == 0)
    def _():
        copies = [
            pltpu.make_async_copy(piece, w_s.at[:, pos[1] ^ mx, pos[2] ^ my], sems.at[2 * my + mx])
            for piece, (my, mx) in ((w0, (0, 0)), (w1, (0, 1)), (w2, (1, 0)), (w3, (1, 1)))
        ]
        for copy in copies:
            copy.start()
        for copy in copies:
            copy.wait()
        wmix_o[...] = w_s[...].reshape(wmix_o.shape)
        vec_o[...] = wmix_o[:, 768:896].astype(F32).T[0:8]
        vbar_o[...] = mm(jnp.broadcast_to(vec_o[5:6], vec_o.shape).astype(BF16), wmix_o[:, 512:768])

    gain, shift = vec_o[4:5], vec_o[5:6]
    row, col = lower_tri(chunk)
    tri = jnp.where(row >= col, 1.0, 0.0).astype(BF16)
    lane = lanes_of((chunk, 128))
    spans = [slice(j * chunk, (j + 1) * chunk) for j in range(2)]
    attends = [low(units[0, rows] * gain + shift) for rows in spans]
    for a, rows in zip(attends, spans):
        a_o[0, rows] = a
    wide = [mm(a, wmix_o[...]) for a in attends]
    mixed = [low(m[:, 0:768]) for m in wide]
    angles = [
        [mm(m[:, base : base + 128], maps[p]) for base, p in ((0, 0), (128, 1), (256, 0), (384, 1))] for m in mixed
    ]
    douts, ends = [], []
    for j, rows in enumerate(spans):
        logits = wide[j][:, 768:896] + bias[...]
        e = jnp.exp(-jnp.abs(logits))
        w = 1.0 + e
        log1 = jnp.where(w == 1.0, e, jnp.log(w) * (e / jnp.where(w == 1.0, 1.0, w - 1.0)))
        log_gate = jnp.where(lane < 4, jnp.minimum(logits, 0.0) - log1, 0.0)
        fresh = jnp.where(lane < 4, jnp.where(logits >= 0.0, e, 1.0) / w, 0.0)
        cum = jnp.where(lane < 4, tri_sum(tri, log_gate), 0.0)
        ccol_o[0, rows] = cum
        ucol_o[0, rows] = fresh
        crow_o[0, j] = (cum + pltpu.roll(fresh, 4, 1)).T[0:8]
        ends.append(cum[chunk - 1 : chunk])
        douts.append(jnp.exp(ends[j] - cum) * fresh)
    one = jnp.where((lane == 64) | (lane == 65), 1.0, 0.0)
    shares = [[None] * 4, [None] * 4]
    for j, rows in enumerate(spans):
        for p in range(2):
            v = mixed[j][:, 512 + 128 * p : 640 + 128 * p].astype(F32) - vbar_o[0:1, 128 * p : 128 * p + 128]
            for h, vh in ((2 * p, v), (2 * p + 1, swap_halves(v))):
                aug = jnp.where(lane < 64, vh, one)
                va_o[0, h, rows] = low(aug)
                shares[j][h] = low(aug * douts[j][:, h : h + 1])
    locals_ = [[None] * 4, [None] * 4]
    for base, target, rest in ((2, fk_o, fkl_o), (0, fq_o, fql_o)):
        for j, rows in enumerate(spans):
            for p in range(2):
                s, c = sincos(angles[j][base + p])
                for h, f in (
                    (2 * p, jnp.where(lane < 64, s, swap_halves(c))),
                    (2 * p + 1, jnp.where(lane < 64, swap_halves(s), c)),
                ):
                    high = low(f)
                    target[0, h, rows] = high
                    rest[0, h, rows] = low(f - high.astype(F32))
                    if base == 2:
                        locals_[j][h] = mm(high, shares[j][h], TN)
    states = []
    for h in range(4):
        smid_o[0, h] = locals_[0][h]
        states.append(locals_[0][h] * jnp.exp(ends[1][:, h : h + 1]) + locals_[1][h])
    pack_states(states, pack_o, b, pack_o.shape[0] - 1)


def weights_of(ccol, ucol_row, crow, row, col):
    gap = jnp.minimum(ccol - crow, 0.0)
    return jnp.where(row >= col, jnp.exp(gap), 0.0) * ucol_row


def pairs_of(chunk):
    return [(j, h, slice(j * chunk, (j + 1) * chunk)) for j in range(2) for h in range(4)]


def scores(fq, fk, fql, fkl, h, rows):
    q, k = fq[0, h, rows], fk[0, h, rows]
    return mm(
        jnp.concatenate([q, fql[0, h, rows], q], axis=1), jnp.concatenate([k, k, fkl[0, h, rows]], axis=1), NT
    )


def local_kernel(b, fq, fk, fql, fkl, va, ccol, crow, o_o):
    chunk = crow.shape[3]
    row, col = lower_tri(chunk)
    pairs = pairs_of(chunk)
    qk = [scores(fq, fk, fql, fkl, h, rows) for j, h, rows in pairs]
    attn = [
        low(q * weights_of(ccol[0, rows, h : h + 1], crow[0, j, 4 + h : 5 + h], crow[0, j, h : h + 1], row, col))
        for q, (j, h, rows) in zip(qk, pairs)
    ]
    outs = [mm(a, va[0, h, rows]) for a, (j, h, rows) in zip(attn, pairs)]
    for out, (j, h, rows) in zip(outs, pairs):
        o_o[0, h, rows] = out


def mean_of(vbar, h):
    pair = vbar[:, 128 * (h // 2) : 128 * (h // 2) + 128]
    return (pair if h % 2 == 0 else swap_halves(pair))[0:1]


def finish_kernel(b, pos, o_loc, fq, ccol, pack, smid, vbar, inv_o, turn_o, st_o, keep_o, send_o):
    chunk = ccol.shape[1] // 2
    zcols = pack[pack.shape[0] - 1].astype(F32)
    states = unpack_states(pack, b, zcols)
    lane = lanes_of((chunk, 128))
    cend = ccol[0, chunk - 1 : chunk]
    pairs = pairs_of(chunk)
    near = []
    for h in range(4):
        near.append(low(states[h]))
        near.append(low(jnp.exp(cend[:, h : h + 1]) * states[h] + smid[0, h]))
        for j in range(2):
            st_o[0, h, j] = near[2 * h + j]
    inter = [mm(fq[0, h, rows], near[2 * h + j]) for j, h, rows in pairs]
    outs = [
        o_loc[0, h, rows] + jnp.exp(ccol[0, rows, h : h + 1]) * part for part, (j, h, rows) in zip(inter, pairs)
    ]
    dens = [jnp.broadcast_to(o[:, 64:65], o.shape) for o in outs]
    invs = [lax.rsqrt(den * den + 1.0) for den in dens]
    att = [[None] * 4, [None] * 4]
    for o, den, inv, (j, h, rows) in zip(outs, dens, invs, pairs):
        mean = mean_of(vbar, h)
        att[j][h] = (o + den * mean) * inv
        inv_o[0, h, rows] = jnp.where(lane < 64, inv, 0.0)
        turn_o[0, h, rows] = mean - den * inv * att[j][h]
    first = pos[3] == 0
    for p in range(2):
        both = [
            jnp.where(lane < 64, att[j][2 * p], swap_halves(att[j][2 * p + 1])) for j in range(2)
        ]
        keep_o[0, :, 128 * p : 128 * p + 128] = jnp.where(first, both[0], both[1]).astype(BF16)
        send_o[0, :, 128 * p : 128 * p + 128] = jnp.where(first, both[1], both[0]).astype(BF16)


def dp_of(pos, mz, mx):
    return (pos[0] ^ mz) * 2 + (pos[1] ^ mx)


def feed_chunks(pos, near, far, cot, cott, feed, feedt, target, up_s, dn_s, hid_s, gp_s, big_s):
    seqs, chunk, _ = cot.shape
    nz = far.shape[0]
    width, both = up_s.shape
    hidden = both // 2
    rows_up = width // (2 * nz)
    for my in range(2):
        cols = slice(my * hidden, (my + 1) * hidden)
        for mx in range(2):
            k = 2 * my + mx
            piece = far if k == 3 else near.at[pl.ds(k * nz, nz)]
            for z in range(nz):
                at = pl.multiple_of((2 * z + (pos[1] ^ mx)) * rows_up, rows_up)
                up_s[pl.ds(at, rows_up), cols] = piece[z, 0:rows_up]
                dn_s[pl.ds(at, rows_up), cols] = piece[z, rows_up : 2 * rows_up]

    def scatter(offset):
        for my in range(2):
            cols = slice(my * hidden, (my + 1) * hidden)
            for mx in range(2):
                for mz in range(nz):
                    at = pl.multiple_of(dp_of(pos, mz, mx) * rows_up, rows_up)
                    target[my, mx, mz, offset : offset + rows_up, :] = big_s[pl.ds(at, rows_up), cols]

    spans = [slice(r * chunk, (r + 1) * chunk) for r in range(seqs)]
    outs, grads = [], []
    for r, rows in enumerate(spans):
        pre = mm(feed[rows], up_s[...])
        gh = mm(cot[r], dn_s[...])
        cdf, pdf = normal_parts(pre)
        hid_s[rows] = low(pre * cdf)
        gp_s[rows] = low(gh * (cdf + pre * pdf))
    for rows in spans:
        outs.append(mm(hid_s[rows], dn_s[...], NT))
        grads.append(mm(gp_s[rows], up_s[...], NT))
    big_s[...] = low(mm(feedt[...], gp_s[...]))
    scatter(0)
    big_s[...] = low(mm(jnp.concatenate([cott[r] for r in range(seqs)], axis=1), hid_s[...]))
    scatter(rows_up)
    return outs, grads


def feed_first_kernel(
    pos, akeep, arecv, x, cot, cott, vec, near_own, far_own, near, far,
    gsend_o, acc_o, gf_o, mid_o, feed_o, feedt_o, att_o, ow_o,
    up_s, dn_s, hid_s, gp_s, big_s,
):
    seqs, chunk, _ = x.shape
    nz = far.shape[0]
    rows_up = up_s.shape[0] // (2 * nz)
    first = pos[3] == 0
    for mc, (some, rest) in enumerate(((near_own, far_own), (near, far))):
        for my in range(2):
            t = (pos[2] ^ my) * 2 + (pos[3] ^ mc)
            for mx in range(2):
                k = 2 * my + mx
                for z in range(nz):
                    at = pl.multiple_of(((2 * z + (pos[1] ^ mx)) * 4 + t) * 16, 16)
                    source = rest if k == 3 else some.at[pl.ds(k * nz, nz)]
                    ow_o[pl.ds(at, 16), :] = source[z, 2 * rows_up :]
    gain, shift = vec[6:7], vec[7:8]
    for r in range(seqs):
        rows = slice(r * chunk, (r + 1) * chunk)
        mine, theirs = akeep[r], arecv[r]
        att = jnp.concatenate([jnp.where(first, mine, theirs), jnp.where(first, theirs, mine)], axis=1)
        att_o[rows] = att
        mid = x[r].astype(F32) + mm(att, ow_o[...])
        mid_o[rows] = mid
        unit, _ = norm_of(mid)
        feed = unit * gain + shift
        feed_o[rows] = low(feed)
        feedt_o[:, rows] = low(feed.T)
    outs, grads = feed_chunks(pos, near, far, cot, cott, feed_o, feedt_o, gsend_o, up_s, dn_s, hid_s, gp_s, big_s)
    for r, (out, grad) in enumerate(zip(outs, grads)):
        acc_o[r * chunk : (r + 1) * chunk] = out
        gf_o[r * chunk : (r + 1) * chunk] = grad


def feed_second_kernel(
    pos, cot, cott, vec, near, far, acc, gf_in, mid_in, feed, feedt, att, ow,
    out_o, gm_o, gak_o, gas_o, gkeep_o, okeep_o, osend_o, gv_o,
    up_s, dn_s, hid_s, gp_s, gb_s, big_s,
):
    seqs, chunk, width = cot.shape
    nz = far.shape[0]
    first = pos[3] == 0
    outs, grads = feed_chunks(pos, near, far, cot, cott, feed, feedt, gkeep_o, up_s, dn_s, hid_s, gp_s, big_s)
    gain = vec[6:7]
    gain_sum = jnp.zeros((1, width), F32)
    shift_sum = jnp.zeros((1, width), F32)
    for r in range(seqs):
        rows = slice(r * chunk, (r + 1) * chunk)
        mid = mid_in[rows]
        out_o[r] = low(mid + (acc[rows] + outs[r]))
        unit, inv = norm_of(mid)
        gf = gf_in[rows] + grads[r]
        gain_sum += jnp.sum(gf * unit, axis=0, keepdims=True)
        shift_sum += jnp.sum(gf, axis=0, keepdims=True)
        gm = cot[r].astype(F32) + norm_back(gf * gain, unit, inv)
        gm_o[r] = gm
        gb = low(gm)
        gb_s[rows] = gb
        ga = low(mm(gb, ow[...], NT))
        half = width // 2
        gak_o[r] = jnp.where(first, ga[:, :half], ga[:, half:])
        gas_o[r] = jnp.where(first, ga[:, half:], ga[:, :half])
    gv_o[...] = jnp.concatenate([gain_sum, shift_sum, jnp.zeros((6, width), F32)], axis=0)
    big_s[:, 0:width] = low(mm(att[...], gb_s[...], TN))
    for mc, target in ((0, okeep_o), (1, osend_o)):
        for my in range(2):
            t = (pos[2] ^ my) * 2 + (pos[3] ^ mc)
            for mx in range(2):
                for mz in range(nz):
                    at = pl.multiple_of((dp_of(pos, mz, mx) * 4 + t) * 16, 16)
                    target[my, mx, mz] = big_s[pl.ds(at, 16), 0:width]


def adjoint_kernel(b, pos, gak, gar, inv_root, turn, fq, ccol, g_o, scaled_o, l1_o, pack_o):
    chunk = ccol.shape[1] // 2
    lane = lanes_of((chunk, 128))
    first = pos[3] == 0
    pairs = pairs_of(chunk)
    gas = []
    for j in range(2):
        for p in range(2):
            cols = slice(128 * p, 128 * p + 128)
            pair = jnp.where(first == (j == 0), gak[0, :, cols], gar[0, :, cols]).astype(F32)
            gas += [pair, swap_halves(pair)]
    gns = [low(ga * inv_root[0, h, rows]).astype(F32) for ga, (j, h, rows) in zip(gas, pairs)]
    gds = [
        jnp.sum(gn * turn[0, h, rows], axis=1, keepdims=True) for gn, (j, h, rows) in zip(gns, pairs)
    ]
    scaled = []
    for gn, gd, (j, h, rows) in zip(gns, gds, pairs):
        gd = jnp.broadcast_to(gd, gn.shape)
        high = low(gd).astype(F32)
        g = jnp.where(lane == 64, high, jnp.where(lane == 65, gd - high, gn))
        g_o[0, h, rows] = low(g)
        scaled.append(low(g * jnp.exp(ccol[0, rows, h : h + 1])))
        scaled_o[0, h, rows] = scaled[-1]
    parts = [mm(fq[0, h, rows], g, TN) for g, (j, h, rows) in zip(scaled, pairs)]
    states = []
    for h in range(4):
        l1_o[0, h] = parts[4 + h]
        states.append(parts[h] + jnp.exp(ccol[0, chunk - 1 : chunk, h : h + 1]) * parts[4 + h])
    pack_states(states, pack_o, b, pack_o.shape[0] - 1, split=True)


def local_back_kernel(b, fq, fk, va, g, scaled, st, ccol, crow, dfq_o, dfk_o, dva_o):
    chunk = crow.shape[3]
    row, col = lower_tri(chunk)
    pairs = pairs_of(chunk)
    for half in (pairs[:4], pairs[4:]):
        qk = [mm(fq[0, h, rows], fk[0, h, rows], NT) for j, h, rows in half]
        da = [mm(g[0, h, rows], va[0, h, rows], NT) for j, h, rows in half]
        inter = [mm(scaled[0, h, rows], st[0, h, j], NT) for j, h, rows in half]
        attn, dp = [], []
        for q, d, (j, h, rows) in zip(qk, da, half):
            w = weights_of(ccol[0, rows, h : h + 1], crow[0, j, 4 + h : 5 + h], crow[0, j, h : h + 1], row, col)
            attn.append(low(q * w))
            dp.append(low(d * w))
        dva = [mm(a, g[0, h, rows], TN) for a, (j, h, rows) in zip(attn, half)]
        dfk = [mm(d, fq[0, h, rows], TN) for d, (j, h, rows) in zip(dp, half)]
        dfq = [mm(d, fk[0, h, rows]) for d, (j, h, rows) in zip(dp, half)]
        for i, (j, h, rows) in enumerate(half):
            dfq_o[0, h, rows] = dfq[i] + inter[i]
            dfk_o[0, h, rows] = dfk[i]
            dva_o[0, h, rows] = dva[i]


def close_kernel(
    b, pos, units, attend, fq, fk, va, dfq, dfk, dva, ccol, ucol, pack, l1, st, wmix, gv, back,
    m00_o, m01_o, m10_o, m11_o, gnk_o, gns_o,
    acc_s, gm_s, gate_s, vsum_s, big_s,
    *, seqs_total,
):
    seqs = seqs_total
    chunk = units.shape[1] // 2
    nz = m00_o.shape[0]
    lane = lanes_of((chunk, 128))
    row, col = lower_tri(chunk)
    upper = jnp.where(row <= col, 1.0, 0.0).astype(BF16)
    zcols = pack[pack.shape[0] - 1].astype(F32)
    arrived = unpack_states(pack, b, zcols, last=64)
    wide = lanes_of((128, 128))

    @pl.when(b == 0)
    def _():
        gate_s[...] = jnp.zeros_like(gate_s)
        vsum_s[...] = jnp.zeros_like(vsum_s)

    pairs = pairs_of(chunk)
    spans = [slice(j * chunk, (j + 1) * chunk) for j in range(2)]
    cums = [ccol[0, rows] for rows in spans]
    freshs = [ucol[0, rows] for rows in spans]
    douts = [jnp.exp(cum[chunk - 1 : chunk] - cum) * fresh for cum, fresh in zip(cums, freshs)]
    nears = []
    for j, h, rows in pairs:
        adj = arrived[h]
        if j == 0:
            adj = l1[0, h] + jnp.exp(ccol[0, 2 * chunk - 1 : 2 * chunk, h : h + 1]) * adj
        zs = adj[:, 64:65] + adj[:, 65:66]
        high = low(zs).astype(F32)
        nears.append(low(jnp.where(wide == 64, high, jnp.where(wide == 65, zs - high, adj))))
    dk_fars = [mm(va[0, h, rows], near, NT) for near, (j, h, rows) in zip(nears, pairs)]
    dv_fars = [mm(fk[0, h, rows], near) for near, (j, h, rows) in zip(nears, pairs)]
    kds, qds, levels = [], [], []
    pqs, pks, dvs = [], [], []
    for i, (j, h, rows) in enumerate(pairs):
        d = douts[j][:, h : h + 1]
        keys, queries = fk[0, h, rows].astype(F32), fq[0, h, rows].astype(F32)
        dk_far = d * dk_fars[i]
        kd_far = jnp.sum(keys * dk_far, axis=1, keepdims=True)
        dk = dk_far + dfk[0, h, rows]
        dq = dfq[0, h, rows]
        kds.append(jnp.sum(keys * dk, axis=1, keepdims=True))
        qds.append(jnp.sum(queries * dq, axis=1, keepdims=True))
        passed = st[0, h, j].astype(F32) * nears[i].astype(F32)
        passed = jnp.sum(jnp.sum(passed, axis=0, keepdims=True), axis=1, keepdims=True)
        total = jnp.sum(kd_far, axis=0, keepdims=True)
        levels.append(total + jnp.exp(cums[j][chunk - 1 : chunk, h : h + 1]) * passed)
        dvs.append(dva[0, h, rows] + d * dv_fars[i])
        pks.append(low(dk * swap_halves(keys)))
        pqs.append(low(dq * swap_halves(queries)))
    grads = [
        [mm(jnp.concatenate(ps[4 * j + 2 * p : 4 * j + 2 * p + 2], axis=1), back[p]) for ps in (pqs, pks) for p in range(2)]
        for j in range(2)
    ]
    bias_sum = jnp.zeros((1, 128), F32)
    gms = []
    for j in range(2):
        kd = qd = jnp.zeros((chunk, 128), F32)
        level = jnp.zeros((1, 128), F32)
        for h in range(4):
            kd = jnp.where(lane == h, kds[4 * j + h], kd)
            qd = jnp.where(lane == h, qds[4 * j + h], qd)
            level = jnp.where(lanes_of((1, 128)) == h, levels[4 * j + h], level)
        dlog = tri_sum(upper, qd - kd) + level
        dlogit = jnp.where(lane < 4, freshs[j] * dlog - (1.0 - freshs[j]) * kd, 0.0)
        bias_sum += jnp.sum(dlogit, axis=0, keepdims=True)
        values = [jnp.where(lane < 64, dvs[4 * j + 2 * p], swap_halves(dvs[4 * j + 2 * p + 1])) for p in range(2)]
        gm = jnp.concatenate([low(x) for x in (*grads[j], *values, dlogit)], axis=1)
        gm_s[pl.ds(pl.multiple_of((2 * b + j) * chunk, chunk), chunk), :] = gm
        gms.append(gm)
    normed = [mm(gm, wmix[...], NT) for gm in gms]
    vsum_s[0:1] += sum(jnp.sum(n * units[0, rows], axis=0, keepdims=True) for n, rows in zip(normed, spans))
    vsum_s[1:2] += sum(jnp.sum(n, axis=0, keepdims=True) for n in normed)
    first = pos[3] == 0
    gnk_o[0] = jnp.where(first, normed[0], normed[1])
    gns_o[0] = low(jnp.where(first, normed[1], normed[0]))
    gate_s[0:1] += bias_sum

    @pl.when(b == seqs - 1)
    def _():
        width = acc_s.shape[0]
        acc_s[...] = mm(attend[...].reshape(gm_s.shape[0], width), gm_s[...], TN)
        table = jnp.concatenate(
            [jnp.zeros((4, width), F32), vsum_s[0:2], gv[0:2], jnp.zeros((120, width), F32)], axis=0
        ).T
        total = gate_s[0:1]
        high = low(total).astype(F32)
        rest = jnp.broadcast_to(total - high, (8, 128))
        both = pltpu.roll(jnp.broadcast_to(high, (8, 128)), 8, 1) + pltpu.roll(rest, 12, 1)
        biases = jnp.broadcast_to(both[0:1], (width, 128))
        side = jnp.where(lanes_of((width, 128)) < 4, acc_s[:, 768:896], table) + biases
        big_s[:, 0:768] = acc_s[:, 0:768].astype(BF16)
        big_s[:, 768:896] = side.astype(BF16)
        for my in range(2):
            for mx in range(2):
                for mz in range(nz):
                    at = pl.multiple_of(chip_row(pos, mz, mx, my), 32)
                    (m00_o, m01_o, m10_o, m11_o)[2 * my + mx][mz] = big_s[pl.ds(at, 32), :]


def final_kernel(pos, keep, recv, mix_o, gate_o, bias_o, *vec_o):
    first = pos[3] == 0
    mine, theirs = keep[...], recv[...]
    halves = (jnp.where(first, mine, theirs), jnp.where(first, theirs, mine))
    width = mix_o.shape[1] // 6
    for i in range(3):
        for s in range(2):
            mix_o[:, (2 * i + s) * width : (2 * i + s + 1) * width] = halves[s][:, i * width : (i + 1) * width]
    sides = [half[:, 3 * width :] for half in halves]
    lane = lanes_of(sides[0].shape)
    gate_o[...] = jnp.where(lane < 4, sides[0], pltpu.roll(sides[1], 4, 1))[:, 0 : gate_o.shape[1]]
    both = jnp.concatenate([sides[0] + sides[1], jnp.zeros((112, 128), F32)], axis=0).T
    for i, out in enumerate(vec_o):
        out[...] = both[4 + i, 0:16]
    sums = [side[0:8] + pltpu.roll(side[0:8], 124, 1) for side in sides]
    row = jnp.where(lane[0:8] < 4, pltpu.roll(sums[0], 120, 1), pltpu.roll(sums[1], 124, 1))
    bias_o[...] = row[0, 0:8]


def input_kernel(b, x, gm, keep, recv, vec, o):
    unit, inv = norm_of(x[0].astype(F32))
    grad = keep[0] + recv[0].astype(F32)
    o[0] = gm[0] + norm_back(grad * vec[4:5], unit, inv)


def hold_kernel(*refs):
    sems = refs[-1]
    count = (len(refs) - 1) // 2
    copies = [
        pltpu.make_async_copy(refs[i], refs[count + i], sems.at[i]) for i in range(count)
    ]
    for copy in copies:
        copy.start()
    for copy in copies:
        copy.wait()


def near_kernel(line, by_x, by_y, near, x_half, y_half, sems):
    nz = line.shape[0]
    half = nz // 2
    copies = [
        pltpu.make_async_copy(source, target, sems.at[i])
        for i, (source, target) in enumerate(
            (
                (line, near.at[pl.ds(0, nz)]),
                (by_x, near.at[pl.ds(nz, nz)]),
                (by_y, near.at[pl.ds(2 * nz, nz)]),
                (by_x.at[pl.ds(0, half)], x_half),
                (by_y.at[pl.ds(half, half)], y_half),
            )
        )
    ]
    for copy in copies:
        copy.start()
    for copy in copies:
        copy.wait()


def gather_kernel(*refs):
    parts, out, sems = refs[:-2], refs[-2], refs[-1]
    copies, at = [], 0
    for i, part in enumerate(parts):
        copies.append(pltpu.make_async_copy(part, out.at[pl.ds(at, part.shape[0])], sems.at[i]))
        at += part.shape[0]
    for copy in copies:
        copy.start()
    for copy in copies:
        copy.wait()


def pause_kernel(out):
    out[...] = jnp.zeros_like(out)


def join_kernel(pos, *refs, axis):
    parts, out, sems = refs[:-2], refs[-2], refs[-1]
    copies = [
        pltpu.make_async_copy(part, out.at[pos[axis] ^ i], sems.at[i]) for i, part in enumerate(parts)
    ]
    for copy in copies:
        copy.start()
    for copy in copies:
        copy.wait()


def pair_sum_kernel(keep, recv, okeep, orecv, x_keep, x_send, y_keep, y_send):
    half = x_keep.shape[1]
    rows = keep.shape[3]
    first, second = slice(0, half), slice(half, 2 * half)
    for i in range(2):
        for my, mx, zs, out in ((i, 0, first, x_keep), (i, 1, first, x_send), (0, i, second, y_keep), (1, i, second, y_send)):
            out[i, :, 0:rows] = low(keep[my, mx, zs].astype(F32) + recv[my, mx, zs].astype(F32))
            out[i, :, rows:] = low(okeep[my, mx, zs].astype(F32) + orecv[my, mx, zs].astype(F32))


def half_sum_kernel(x_keep, x_recv, y_keep, y_recv, x_own, x_far, y_own, y_far):
    for keep, recv, own, far in ((x_keep, x_recv, x_own, x_far), (y_keep, y_recv, y_own, y_far)):
        for i, out in ((0, own), (1, far)):
            out[...] = low(keep[i].astype(F32) + recv[i].astype(F32))


def line_sum_kernel(x_own, x_recv, y_own, y_recv, *outs):
    half = x_own.shape[0]
    for i in range(half):
        outs[i][...] = low(x_own[i].astype(F32) + x_recv[i].astype(F32))
        outs[half + i][...] = low(y_own[i].astype(F32) + y_recv[i].astype(F32))


def sum_of_four(refs):
    a, b, c, d = (ref[...].astype(F32) for ref in refs)
    return (a + b) + (c + d)


def mix_sum_kernel(m0, m1, m2, m3, *outs):
    total = sum_of_four((m0, m1, m2, m3))
    side = total[..., 768:896]
    rest = side - low(side).astype(F32)
    lane = lanes_of(side.shape)
    moved = jnp.where((lane >= 12) & (lane < 16), side + pltpu.roll(rest, 4, side.ndim - 1), side)
    for i, out in enumerate(outs):
        out[:, 0:768] = low(total[i, :, 0:768])
        out[:, 768:896] = low(moved[i])


def feed_last_kernel(a, b, c, d, up_o, down_o, out_o):
    total = sum_of_four((a, b, c, d))
    rows = up_o.shape[0]
    up_o[...] = total[0:rows]
    down_o[...] = total[rows : 2 * rows].T
    out_o[...] = total[2 * rows :]


def mix_last_kernel(pos, a, b, c, d, keep_o, send_o):
    total = sum_of_four((a, b, c, d))
    rows = keep_o.shape[0]
    first = pos[3] == 0
    keep_o[...] = jnp.where(first, total[:rows], total[rows:])
    send_o[...] = jnp.where(first, total[rows:], total[:rows])


def call(kernel, steps, ins, outs, scratch=(), us=1.0, name=None, limit=14):
    def spec(kind):
        if kind in "da":
            return pl.BlockSpec(memory_space=pl.ANY)
        return pl.BlockSpec(memory_space=pltpu.SMEM if kind == "m" else pltpu.VMEM)

    kinds = [kind for kind, _ in ins]
    out_kinds = [kind for kind, _, _ in outs]
    all_kinds = kinds + out_kinds + ["w"] * len(scratch)

    def run(*refs):
        used = [(kind, ref) for kind, ref in zip(all_kinds, refs) if kind != "d"]
        if not steps:
            kernel(*[ref for _, ref in used])
            return

        def one(b, carry):
            kernel(b, *[ref.at[pl.ds(b, 1)] if kind == "s" else ref for kind, ref in used])
            return carry

        lax.fori_loop(0, steps, one, 0)

    return pl.pallas_call(
        run,
        in_specs=[spec(kind) for kind in kinds],
        out_specs=[spec(kind) for kind in out_kinds],
        out_shape=[jax.ShapeDtypeStruct(shape, dtype) for _, shape, dtype in outs],
        scratch_shapes=list(scratch),
        compiler_params=pltpu.CompilerParams(vmem_limit_bytes=limit * 1024 * 1024),
        cost_estimate=pl.CostEstimate(flops=int(us * 1.15e9), bytes_accessed=0, transcendentals=0),
        name=name,
    )(*[a for _, a in ins])


def xor_with(a, mask, count):
    return lax.ppermute(a, BOTH, [(i, i ^ mask) for i in range(count)])


def body(
    inputs, cotangent, mix_weight, gate_weight, gate_bias, out_weight, gain_first, shift_first, gain_second,
    shift_second, up_weight, down_weight, random_maps,
):
    dp, tensor = lax.axis_size("dp"), lax.axis_size("tensor")
    count = dp * tensor
    place_dp, place_t = lax.axis_index("dp"), lax.axis_index("tensor")
    seqs, chunk, width = inputs.shape
    heads, head = random_maps.shape[0], random_maps.shape[1]
    hidden = up_weight.shape[1]
    core = place_t % 2
    first = core == 0
    direct = dp == 8
    nz = 4
    if direct:
        pos = jnp.stack([place_dp // 2, place_dp % 2, place_t // 2, core]).astype(jnp.int32)
    else:
        pos = jnp.stack([jnp.zeros_like(core)] * 3 + [core]).astype(jnp.int32)
    swap_core = functools.partial(xor_with, mask=1, count=count)

    def mix_pack(mix_w, gate_w, vecs):
        rows = mix_w.shape[0]
        split = mix_w.reshape(rows, 3, 2, width // 2)
        sides = [v[:, None] for v in vecs]
        pad = jnp.zeros((rows, 120), BF16)
        return [
            jnp.concatenate(
                [split[:, 0, s], split[:, 1, s], split[:, 2, s], gate_w[:, 4 * s : 4 * s + 4]] + sides + [pad], axis=1
            )
            for s in range(2)
        ]

    def join(parts, axis, after=()):
        (out,) = call(
            functools.partial(join_kernel, axis=axis), 0, [("m", pos)] + [("a", a) for a in parts] + [("d", a) for a in after],
            [("w", (len(parts), *parts[0].shape), parts[0].dtype)],
            scratch=[pltpu.SemaphoreType.DMA((len(parts),))], name="join",
        )
        return out

    def pause(after, us):
        (out,) = call(
            pause_kernel, 0, [("d", a) for a in after], [("w", (8, 128), F32)], us=us, name="pause",
        )
        return out

    def from_plane(pieces):
        return [pieces[0], xor_with(pieces[1], 4, count), xor_with(pieces[2], 2, count), xor_with(pieces[3], 6, count)]

    other_in = swap_core(inputs)
    vectors = (gain_first, shift_first, gain_second, shift_second)
    long = 2 * chunk
    unit, cot_t = call(
        prepare_kernel, seqs, [("m", pos), ("s", inputs), ("s", other_in), ("s", cotangent)],
        [("s", (seqs, long, width), F32), ("s", (seqs, width, chunk), BF16)], us=2.5, name="prepare",
    )
    if direct:
        side_lane = lanes_of((mix_weight.shape[0], 128))
        side = jnp.pad(gate_weight, ((0, 0), (0, 128 - heads)))
        for i, v in enumerate(vectors):
            side = jnp.where(side_lane == heads + i, lax.broadcast_in_dim(v, side_lane.shape, (0,)), side)
        rows = mix_weight.shape[0]
        keep, send = call(
            pack_kernel, 0, [("m", pos), ("w", mix_weight), ("w", side)], [("w", (rows, 896), BF16)] * 2, name="pack",
        )
        pair = join([keep, swap_core(send)], 3)
        line = join([pair] + [xor_with(pair, 8 * m, count) for m in range(1, nz)], 0, after=[unit])
        w_pieces = [line] + [xor_with(line, m, count) for m in (4, 2, 6)]
        block = jnp.concatenate([up_weight, down_weight.T, out_weight], axis=0)
        (block,) = call(
            hold_kernel, 0, [("a", block), ("d", line)],
            [("w", block.shape, BF16)], scratch=[pltpu.SemaphoreType.DMA((1,))], name="hold",
        )
        ff_line = join([block] + [xor_with(block, 8 * m, count) for m in range(1, nz)], 0, after=w_pieces)
        by_x, by_y = xor_with(ff_line, 4, count), xor_with(ff_line, 2, count)
    else:
        whole = [
            lax.all_gather(a, BOTH, axis=0, tiled=True) for a in (mix_weight, gate_weight, out_weight) + vectors
        ]
        p0, p1 = mix_pack(whole[0], whole[1], whole[3:])
        blocks = jnp.where(first, p0, p1).reshape(nz, 2, 2, 2, 16, 896)
        w_pieces = [blocks[:, mx, my] for my, mx in ((0, 0), (0, 1), (1, 0), (1, 1))]
        up_all = lax.all_gather(up_weight, BOTH, axis=0, tiled=False).reshape(dp, tensor, -1, hidden)
        dn_all = lax.all_gather(down_weight.T, BOTH, axis=0, tiled=False).reshape(dp, tensor, -1, hidden)
        up_all = jnp.moveaxis(up_all, 1, 0).reshape(2, 2, nz, 2, -1, hidden)
        dn_all = jnp.moveaxis(dn_all, 1, 0).reshape(2, 2, nz, 2, -1, hidden)
        out_all = whole[2].reshape(nz, 2, 2, 2, 16, width).transpose(2, 3, 0, 1, 4, 5)
        ff_all = jnp.concatenate([up_all, dn_all, out_all], axis=4)
        ff_all = jnp.where(first, ff_all, ff_all[:, ::-1])
        ff_own, ff_other = (
            jnp.concatenate([ff_all[my, mc, :, mx] for my in range(2) for mx in range(2)]) for mc in range(2)
        )

    maps = lax.dynamic_slice_in_dim(random_maps, core * 4, 4, 0)
    zero = jnp.zeros((head, head), BF16)
    maps_pair = jnp.stack(
        [
            jnp.concatenate(
                [jnp.concatenate([maps[2 * p], zero], 1), jnp.concatenate([zero, maps[2 * p + 1]], 1)], 0
            )
            for p in range(2)
        ]
    )
    flip = jnp.swapaxes(maps, 1, 2)
    maps_back = jnp.stack(
        [
            jnp.concatenate(
                [
                    jnp.concatenate([flip[2 * p], zero], 1),
                    jnp.concatenate([-flip[2 * p], zero], 1),
                    jnp.concatenate([zero, flip[2 * p + 1]], 1),
                    jnp.concatenate([zero, -flip[2 * p + 1]], 1),
                ],
                0,
            )
            for p in range(2)
        ]
    )
    bias = jnp.pad(lax.dynamic_slice_in_dim(gate_bias, core * 4, 4, 0), (0, 124))[None]

    tokens = seqs * long
    feats = (seqs, 4, long, 128)
    npack = 2 * seqs + 1
    attend, fq, fk, fql, fkl, va, ccol, ucol, crow, smid, pack, wmix, vec, vbar = call(
        project_kernel, seqs,
        [("m", pos), ("s", unit)] + [("a", w) for w in w_pieces] + [("w", bias), ("w", maps_pair)],
        [
            ("s", (seqs, long, width), BF16), ("s", feats, BF16), ("s", feats, BF16), ("s", feats, BF16), ("s", feats, BF16), ("s", feats, BF16),
            ("s", (seqs, long, 128), F32), ("s", (seqs, long, 128), F32),
            ("s", (seqs, 2, 8, chunk), F32),
            ("s", (seqs, 4, 128, 128), F32),
            ("w", (npack, 128, 128), BF16), ("w", (width, 896), BF16), ("w", (8, width), F32),
            ("w", (8, width // 2), F32),
        ],
        scratch=[pltpu.VMEM((nz, 2, 2, 2, 16, 896), BF16), pltpu.SemaphoreType.DMA((4,))], us=12, name="project",
    )
    if direct:
        half_z = nz // 2
        near_shape, far_shape = (3 * nz, *ff_line.shape[1:]), (half_z, *ff_line.shape[1:])
        ff_near, x_half, y_half = call(
            near_kernel, 0, [("a", ff_line), ("a", by_x), ("a", by_y), ("d", pack)],
            [("w", near_shape, BF16), ("w", far_shape, BF16), ("w", far_shape, BF16)],
            scratch=[pltpu.SemaphoreType.DMA((5,))], name="near",
        )
    ahead = [(i, i + 2) for i in range(count) if (i % tensor) < 2]
    arrived = lax.ppermute(pack, BOTH, ahead)
    (o_loc,) = call(
        local_kernel, seqs,
        [("s", fq), ("s", fk), ("s", fql), ("s", fkl), ("s", va), ("s", ccol), ("s", crow)],
        [("s", feats, F32)], us=0.3, name="local",
    )
    (inv_root, turn, st, att_keep, att_send) = call(
        finish_kernel, seqs,
        [("m", pos), ("s", o_loc), ("s", fq), ("s", ccol), ("w", arrived), ("s", smid), ("w", vbar)],
        [
            ("s", feats, F32), ("s", feats, F32), ("s", (seqs, 4, 2, 128, 128), BF16),
            ("s", (seqs, chunk, width // 2), BF16), ("s", (seqs, chunk, width // 2), BF16),
        ],
        us=0.3, name="finish",
    )
    att_recv = swap_core(att_send)
    if direct:
        near_other = swap_core(ff_near)
        far_parts = [xor_with(x_half, 2, count), xor_with(y_half, 4, count)]
        (ff_far,) = call(
            gather_kernel, 0, [("a", a) for a in far_parts] + [("d", att_keep)],
            [("w", ff_line.shape, BF16)], scratch=[pltpu.SemaphoreType.DMA((2,))], name="gather",
        )
        far_other = swap_core(ff_far)
    else:
        ff_near, ff_far, near_other, far_other = ff_own[: 3 * nz], ff_own[3 * nz :], ff_other[: 3 * nz], ff_other[3 * nz :]

    own = seqs * chunk
    nrows = ff_near.shape[1]
    payload, out_payload = (2, 2, nz, nrows - 16, hidden), (2, 2, nz, 16, hidden)
    rows_low, rows_full = ("w", (own, width), BF16), ("w", (own, width), F32)
    work = [
        pltpu.VMEM((width, 2 * hidden), BF16), pltpu.VMEM((width, 2 * hidden), BF16),
        pltpu.VMEM((own, 2 * hidden), BF16), pltpu.VMEM((own, 2 * hidden), BF16),
    ]
    big = pltpu.VMEM((width, 2 * hidden), BF16)
    g_send, *fed = call(
        feed_first_kernel, 0,
        [("m", pos)] + [
            ("w", a) for a in (
                att_keep, att_recv, inputs, cotangent, cot_t, vec, ff_near, ff_far, near_other, far_other
            )
        ],
        [
            ("w", payload, BF16), rows_full, rows_full, rows_full, rows_low, ("w", (width, own), BF16), rows_low,
            ("w", (width, width), BF16),
        ],
        scratch=[*work, big], us=10, name="feed_first", limit=24,
    )
    g_recv = swap_core(g_send)
    output, grad_middle, ga_keep, ga_send, g_keep, o_keep, o_send, grad_vec = call(
        feed_second_kernel, 0,
        [("m", pos)] + [("w", a) for a in (cotangent, cot_t, vec, ff_near, ff_far, *fed)],
        [
            ("w", (seqs, chunk, width), BF16), ("w", (seqs, chunk, width), F32),
            ("w", (seqs, chunk, width // 2), BF16), ("w", (seqs, chunk, width // 2), BF16),
            ("w", payload, BF16), ("w", out_payload, BF16), ("w", out_payload, BF16), ("w", (8, width), F32),
        ],
        scratch=[
            *work, pltpu.VMEM((own, width), BF16), big,
        ],
        us=10, name="feed_second", limit=24,
    )
    ga_recv = swap_core(ga_send)

    if direct:
        o_recv = swap_core(o_send)
        half_z = nz // 2
        two, one = (2, half_z, nrows, hidden), (half_z, nrows, hidden)
        x_keep, x_send, y_keep, y_send = call(
            pair_sum_kernel, 0, [("w", g_keep), ("w", g_recv), ("w", o_keep), ("w", o_recv)], [("w", two, BF16)] * 4,
            us=0.6, name="pair_sum",
        )
        x_recv, y_recv = xor_with(x_send, 4, count), xor_with(y_send, 2, count)
        before_adjoint = [x_keep]
    else:
        before_adjoint = []
        g_keep, g_send = (jnp.concatenate(parts, axis=3) for parts in ((g_keep, o_keep), (g_send, o_send)))
        by_core = jnp.where(first, jnp.stack([g_keep, g_send]), jnp.stack([g_send, g_keep]))
        by_rows = by_core.transpose(3, 2, 1, 0, 4, 5)
        rows_up = (nrows - 16) // 2
        ups = by_rows[..., :rows_up, :].reshape(nz * 2, 4, rows_up, hidden).transpose(1, 0, 2, 3)
        dns = by_rows[..., rows_up : 2 * rows_up, :].reshape(nz * 2, 4, rows_up, hidden).transpose(1, 0, 2, 3)
        ups = ups.reshape(4, dp, -1, hidden).transpose(1, 0, 2, 3)
        dns = dns.reshape(4, dp, -1, hidden).transpose(1, 0, 2, 3)
        outs = by_rows[..., 2 * rows_up :, :].reshape(width, width)

        def reduced(a):
            return lax.psum_scatter(a.astype(F32).reshape(count, -1, a.shape[-1]), BOTH, scatter_dimension=0)

        up_grad, down_grad, out_grad = reduced(ups), reduced(dns).T, reduced(outs)

    g, scaled, l1, pack_b = call(
        adjoint_kernel, seqs,
        [("m", pos), ("s", ga_keep), ("s", ga_recv), ("s", inv_root), ("s", turn), ("s", fq), ("s", ccol)]
        + [("d", a) for a in before_adjoint],
        [
            ("s", feats, BF16), ("s", feats, BF16), ("s", (seqs, 4, 128, 128), F32), ("w", (npack, 128, 128), BF16),
        ],
        us=0.3, name="adjoint",
    )
    behind = [(i, i - 2) for i in range(count) if (i % tensor) >= 2]
    arrived_b = lax.ppermute(pack_b, BOTH, behind)
    dfq, dfk, dva = call(
        local_back_kernel, seqs,
        [("s", fq), ("s", fk), ("s", va), ("s", g), ("s", scaled), ("s", st), ("s", ccol), ("s", crow)],
        [("s", feats, F32), ("s", feats, F32), ("s", feats, F32)],
        us=0.3, name="local_back",
    )
    before_close = []
    if direct:
        x_own, x_far, y_own, y_far = call(
            half_sum_kernel, 0, [("w", a) for a in (x_keep, x_recv, y_keep, y_recv)] + [("d", dfq)],
            [("w", one, BF16)] * 4, us=0.4, name="half_sum",
        )
        x_recv, y_recv = xor_with(x_far, 2, count), xor_with(y_far, 4, count)
        before_close = [x_own]
    *m_pieces, gn_keep, gn_send = call(
        functools.partial(close_kernel, seqs_total=seqs), seqs,
        [("m", pos), ("s", unit), ("w", attend), ("s", fq), ("s", fk), ("s", va), ("s", dfq),
         ("s", dfk), ("s", dva), ("s", ccol), ("s", ucol), ("w", arrived_b), ("s", l1), ("s", st),
         ("w", wmix), ("w", grad_vec), ("w", maps_back)] + [("d", a) for a in before_close],
        [*[("w", (nz, 32, 896), BF16)] * 4, ("s", (seqs, chunk, width), F32), ("s", (seqs, chunk, width), BF16)],
        scratch=[
            pltpu.VMEM((width, 896), F32), pltpu.VMEM((tokens, 896), BF16), pltpu.VMEM((8, 128), F32),
            pltpu.VMEM((8, width), F32), pltpu.VMEM((width, 896), BF16),
        ],
        us=14.7, name="close",
    )
    if direct:
        g_line = call(
            line_sum_kernel, 0, [("w", a) for a in (x_own, x_recv, y_own, y_recv)] + [("d", gn_keep)],
            [("w", (nrows, hidden), BF16)] * nz, us=0.4, name="line_sum",
        )
        m_parts = from_plane(m_pieces)
    gn_recv = swap_core(gn_send)
    def finish_input(after):
        return call(
            input_kernel, seqs,
            [("s", inputs), ("s", grad_middle), ("s", gn_keep), ("s", gn_recv), ("w", vec)] + [("d", a) for a in after],
            [("s", (seqs, chunk, width), F32)], us=0.3, name="input_grad",
        )

    if direct:
        m_plane = call(
            mix_sum_kernel, 0, [("w", a) for a in m_parts] + [("d", pause([g_line[0]], 40))],
            [("w", (32, 896), BF16)] * nz, us=0.4, name="mix_sum",
        )
        (input_grad,) = finish_input([m_plane[0]])
        g_parts = [g_line[0]] + [xor_with(g_line[m], 8 * m, count) for m in range(1, nz)]
        up_grad, down_grad, out_grad = call(
            feed_last_kernel, 0, [("w", a) for a in g_parts],
            [("w", a.shape, F32) for a in (up_weight, down_weight, out_weight)], us=0.3, name="feed_last",
        )
        mix_parts = [m_plane[0]] + [xor_with(m_plane[m], 8 * m, count) for m in range(1, nz)]
        m_keep, m_send = call(
            mix_last_kernel, 0, [("m", pos)] + [("w", a) for a in mix_parts] + [("d", out_grad), ("d", input_grad)],
            [("w", (mix_weight.shape[0], 896), F32)] * 2, name="mix_last",
        )
        m_recv = swap_core(m_send)
    else:
        (input_grad,) = finish_input([])
        m_all = jnp.stack(m_pieces).astype(F32).reshape(2, 2, nz, 32, 896)
        mine_rows = m_all.transpose(2, 1, 0, 3, 4).reshape(count, -1, 896)
        keep_part = lax.psum_scatter(mine_rows * jnp.where(first, 1.0, 0.0), BOTH, scatter_dimension=0)
        far_part = lax.psum_scatter(mine_rows * jnp.where(first, 0.0, 1.0), BOTH, scatter_dimension=0)
        m_keep = jnp.where(first, keep_part, far_part)
        m_recv = jnp.where(first, far_part, keep_part)
    if direct:
        mix_grad, gate_grad, bias_grad, *per_row = call(
            final_kernel, 0, [("m", pos), ("w", m_keep), ("w", m_recv)],
            [("w", mix_weight.shape, F32), ("w", gate_weight.shape, F32), ("w", (heads,), F32)]
            + [("w", gain_first.shape, F32)] * 4,
            us=1.2, name="final",
        )
    else:
        m_low = jnp.where(first, m_keep, m_recv)
        m_high = jnp.where(first, m_recv, m_keep)
        mix_grad = jnp.concatenate(
            [part[:, 256 * i : 256 * i + 256] for i in range(3) for part in (m_low, m_high)], axis=1
        )
        gate_grad = jnp.concatenate([m_low[:, 768:772], m_high[:, 768:772]], axis=1)
        bias_grad = jnp.concatenate([m[0, 776:780] + m[0, 780:784] for m in (m_low, m_high)])
        per_row = [m_keep[:, 772 + i] + m_recv[:, 772 + i] for i in range(4)]
    return (
        output, input_grad, mix_grad, gate_grad, bias_grad, out_grad,
        *per_row, up_grad, down_grad,
    )


def solution(mesh):
    rows, spread = P(("dp", "tensor"), None), P(("dp", "tensor"))
    tokens = P("dp", "tensor", None)
    in_specs = (
        tokens, tokens, rows, rows, P(), rows, spread, spread, spread, spread, P("dp", "tensor"), P("tensor", "dp"), P(),
    )
    out_specs = (
        tokens, tokens, rows, rows, P(), rows, spread, spread, spread, spread, P("dp", "tensor"), P("tensor", "dp"),
    )
    return jax.shard_map(body, mesh=mesh, in_specs=in_specs, out_specs=out_specs, check_vma=False)
```

```python
import functools

import jax
import jax.numpy as jnp
from jax import lax
from jax.experimental import pallas as pl
from jax.experimental.pallas import tpu as pltpu
from jax.sharding import PartitionSpec as P

BOTH = ("dp", "tensor")
F32 = jnp.float32
BF16 = jnp.bfloat16
EPSILON = 1e-05
DENSITY = 0.3989422804014327
SIN = (9.9999999998e-01, -1.6666666617e-01, 8.3333309689e-03, -1.9840860382e-04, 2.7525224003e-06, -2.3888330913e-08)
COS = (9.9999999978e-01, -4.9999999354e-01, 4.1666636104e-02, -1.3888359409e-03, 2.4760057595e-05, -2.6049626765e-07)

NN = (((1,), (0,)), ((), ()))
NT = (((1,), (1,)), ((), ()))
TN = (((0,), (0,)), ((), ()))


def mm(a, b, dims=NN):
    return lax.dot_general(a, b, dims, preferred_element_type=F32)


def low(a):
    return a.astype(BF16)


def lanes_of(shape):
    return lax.broadcasted_iota(jnp.int32, shape, len(shape) - 1)


def swap_halves(a):
    return pltpu.roll(a, 64, 1)


def sincos(a):
    turns = jnp.floor(a * 0.3183098861837907 + 0.5)
    r = (a - turns * 3.140625) - turns * 9.676535897932e-4
    half = turns * 0.5
    sign = 1.0 - 4.0 * (half - jnp.floor(half))
    r2 = r * r
    s = r * (SIN[0] + r2 * (SIN[1] + r2 * (SIN[2] + r2 * (SIN[3] + r2 * (SIN[4] + r2 * SIN[5])))))
    c = COS[0] + r2 * (COS[1] + r2 * (COS[2] + r2 * (COS[3] + r2 * (COS[4] + r2 * COS[5]))))
    return sign * s, sign * c


def normal_parts(v):
    t = pl.reciprocal(1.0 + 0.23164189 * jnp.abs(v), approx=True)
    bell = jnp.exp(-0.5 * (v * v))
    poly = t * (0.127414796 + t * (-0.142248368 + t * (0.7107068705 + t * (-0.7265760135 + t * 0.5307027145))))
    tail = poly * bell
    return jnp.where(v >= 0.0, 1.0 - tail, tail), DENSITY * bell


def three_parts(a):
    high = a.astype(BF16)
    rest = a - high.astype(F32)
    mid = rest.astype(BF16)
    return high, mid, (rest - mid.astype(F32)).astype(BF16)


def tri_sum(tri, a):
    high, mid, rest = (part.astype(F32) for part in three_parts(a))
    packed = mm(tri, low(high + pltpu.roll(mid, 4, 1) + pltpu.roll(rest, 8, 1)))
    return packed + pltpu.roll(packed, 124, 1) + pltpu.roll(packed, 120, 1)


def norm_of(x):
    mean = jnp.mean(x, axis=-1, keepdims=True)
    centered = x - mean
    inv = lax.rsqrt(jnp.mean(centered * centered, axis=-1, keepdims=True) + EPSILON)
    return centered * inv, inv


def norm_back(s, unit, inv):
    return inv * (
        s
        - jnp.mean(s, axis=-1, keepdims=True)
        - unit * jnp.mean(s * unit, axis=-1, keepdims=True)
    )


def chip_row(pos, mz, mx, my):
    return (((pos[0] ^ mz) * 2 + (pos[1] ^ mx)) * 2 + (pos[2] ^ my)) * 32


def lower_tri(n):
    row = lax.broadcasted_iota(jnp.int32, (n, n), 0)
    col = lax.broadcasted_iota(jnp.int32, (n, n), 1)
    return row, col


def unpack_states(pack, b, zcols, last=65):
    lane = lanes_of((128, 128))
    out = []
    for p in range(2):
        both = pack[2 * b + p].astype(F32)
        for h, mat in ((2 * p, both), (2 * p + 1, swap_halves(both))):
            z = jnp.sum(jnp.where(lane == 4 * b + h, zcols, 0.0), axis=1, keepdims=True)
            out.append(jnp.where(lane < 64, mat, jnp.where(lane <= last, z, 0.0)))
    return out


def pack_states(states, pack_o, b, last, split=False):
    lane = lanes_of((128, 128))
    zcols = jnp.where(b == 0, 0.0, pack_o[last].astype(F32))

    def sum_of(s):
        return s[:, 64:65] + s[:, 65:66] if split else s[:, 64:65]

    for p in range(2):
        s0, s1 = states[2 * p], states[2 * p + 1]
        pack_o[2 * b + p] = jnp.where(lane < 64, s0, swap_halves(s1)).astype(BF16)
        zcols = jnp.where(lane == 4 * b + 2 * p, sum_of(s0), zcols)
        zcols = jnp.where(lane == 4 * b + 2 * p + 1, sum_of(s1), zcols)
    pack_o[last] = zcols.astype(BF16)


def pack_kernel(pos, mix, columns, keep_o, send_o):
    width = mix.shape[1] // 6
    rows = mix.shape[0]
    table = jnp.concatenate(
        [columns[...].astype(F32), jnp.zeros((128 - columns.shape[0], rows), F32)], axis=0
    )
    sides = jnp.concatenate([table, jnp.zeros((128, 128 - rows), F32)], axis=1).T[0:rows]
    lane = lanes_of(sides.shape)
    moved = pltpu.roll(sides, 124, 1)
    halves = []
    for s, block in ((0, jnp.where(lane < 4, sides, moved)), (1, moved)):
        parts = [mix[:, (2 * i + s) * width : (2 * i + s + 1) * width] for i in range(3)]
        halves.append(jnp.concatenate(parts + [low(jnp.where(lane < 8, block, 0.0))], axis=1))
    first = pos[3] == 0
    keep_o[...] = jnp.where(first, halves[0], halves[1])
    send_o[...] = jnp.where(first, halves[1], halves[0])


def prepare_kernel(b, pos, own, oth, cot, unit_o, cott_o):
    chunk = own.shape[1]
    first = pos[3] == 0
    mine, theirs = own[0], oth[0]
    for j in range(2):
        unit, _ = norm_of(jnp.where(first == (j == 0), mine, theirs).astype(F32))
        unit_o[0, j * chunk : (j + 1) * chunk] = unit
    cott_o[0] = low(cot[0].astype(F32).T)


def feature_parts(angles, lane):
    s, c = sincos(angles)
    out = []
    for f in (jnp.where(lane < 64, s, swap_halves(c)), jnp.where(lane < 64, swap_halves(s), c)):
        high = low(f)
        out.append((high, low(f - high.astype(F32))))
    return out


def query_kernel(b, a, wmix, maps, fq_o, fql_o):
    chunk = a.shape[1] // 2
    lane = lanes_of((chunk, 128))
    spans = [slice(j * chunk, (j + 1) * chunk) for j in range(2)]
    mixed = [low(mm(a[0, rows], wmix[:, 0:256])) for rows in spans]
    angles = [[mm(m[:, 128 * p : 128 * p + 128], maps[p]) for p in range(2)] for m in mixed]
    for j, rows in enumerate(spans):
        for p in range(2):
            for i, (high, rest) in enumerate(feature_parts(angles[j][p], lane)):
                fq_o[0, 2 * p + i, rows], fql_o[0, 2 * p + i, rows] = high, rest


def project_kernel(
    b, pos, units, w0, w1, w2, w3, bias, maps,
    a_o, fk_o, fkl_o, va_o, ccol_o, ucol_o, crow_o, smid_o, pack_o, wmix_o, vec_o, vbar_o,
    w_s, sems,
):
    chunk = units.shape[1] // 2

    @pl.when(b == 0)
    def _():
        copies = [
            pltpu.make_async_copy(piece, w_s.at[:, pos[1] ^ mx, pos[2] ^ my], sems.at[2 * my + mx])
            for piece, (my, mx) in ((w0, (0, 0)), (w1, (0, 1)), (w2, (1, 0)), (w3, (1, 1)))
        ]
        for copy in copies:
            copy.start()
        for copy in copies:
            copy.wait()
        wmix_o[...] = w_s[...].reshape(wmix_o.shape)
        vec_o[...] = wmix_o[:, 768:896].astype(F32).T[0:8]
        vbar_o[...] = mm(jnp.broadcast_to(vec_o[5:6], vec_o.shape).astype(BF16), wmix_o[:, 512:768])

    gain, shift = vec_o[4:5], vec_o[5:6]
    row, col = lower_tri(chunk)
    tri = jnp.where(row >= col, 1.0, 0.0).astype(BF16)
    lane = lanes_of((chunk, 128))
    spans = [slice(j * chunk, (j + 1) * chunk) for j in range(2)]
    attends = [low(units[0, rows] * gain + shift) for rows in spans]
    for a, rows in zip(attends, spans):
        a_o[0, rows] = a
    wide = [mm(a, wmix_o[:, 256:896]) for a in attends]
    mixed = [low(m[:, 0:512]) for m in wide]
    angles = [[mm(m[:, 128 * p : 128 * p + 128], maps[p]) for p in range(2)] for m in mixed]
    douts, ends = [], []
    for j, rows in enumerate(spans):
        logits = wide[j][:, 512:640] + bias[...]
        e = jnp.exp(-jnp.abs(logits))
        w = 1.0 + e
        log1 = jnp.where(w == 1.0, e, jnp.log(w) * (e / jnp.where(w == 1.0, 1.0, w - 1.0)))
        log_gate = jnp.where(lane < 4, jnp.minimum(logits, 0.0) - log1, 0.0)
        fresh = jnp.where(lane < 4, jnp.where(logits >= 0.0, e, 1.0) / w, 0.0)
        cum = jnp.where(lane < 4, tri_sum(tri, log_gate), 0.0)
        ccol_o[0, rows] = cum
        ucol_o[0, rows] = fresh
        crow_o[0, j] = (cum + pltpu.roll(fresh, 4, 1)).T[0:8]
        ends.append(cum[chunk - 1 : chunk])
        douts.append(jnp.exp(ends[j] - cum) * fresh)
    one = jnp.where((lane == 64) | (lane == 65), 1.0, 0.0)
    shares = [[None] * 4, [None] * 4]
    for j, rows in enumerate(spans):
        for p in range(2):
            v = mixed[j][:, 256 + 128 * p : 384 + 128 * p].astype(F32) - vbar_o[0:1, 128 * p : 128 * p + 128]
            for h, vh in ((2 * p, v), (2 * p + 1, swap_halves(v))):
                aug = jnp.where(lane < 64, vh, one)
                va_o[0, h, rows] = low(aug)
                shares[j][h] = low(aug * douts[j][:, h : h + 1])
    locals_ = [[None] * 4, [None] * 4]
    for j, rows in enumerate(spans):
        for p in range(2):
            parts = feature_parts(angles[j][p], lane)
            for h in (2 * p, 2 * p + 1):
                fk_o[0, h, rows], fkl_o[0, h, rows] = parts[h - 2 * p]
                locals_[j][h] = mm(parts[h - 2 * p][0], shares[j][h], TN)
    states = []
    for h in range(4):
        smid_o[0, h] = locals_[0][h]
        states.append(locals_[0][h] * jnp.exp(ends[1][:, h : h + 1]) + locals_[1][h])
    pack_states(states, pack_o, b, pack_o.shape[0] - 1)


def weights_of(ccol, ucol_row, crow, row, col):
    gap = jnp.minimum(ccol - crow, 0.0)
    return jnp.where(row >= col, jnp.exp(gap), 0.0) * ucol_row


def pairs_of(chunk):
    return [(j, h, slice(j * chunk, (j + 1) * chunk)) for j in range(2) for h in range(4)]


def scores(fq, fk, fql, fkl, h, rows):
    q, k = fq[0, h, rows], fk[0, h, rows]
    return mm(
        jnp.concatenate([q, fql[0, h, rows], q], axis=1), jnp.concatenate([k, k, fkl[0, h, rows]], axis=1), NT
    )


def local_kernel(b, fq, fk, fql, fkl, va, ccol, crow, o_o):
    chunk = crow.shape[3]
    row, col = lower_tri(chunk)
    pairs = pairs_of(chunk)
    qk = [scores(fq, fk, fql, fkl, h, rows) for j, h, rows in pairs]
    attn = [
        low(q * weights_of(ccol[0, rows, h : h + 1], crow[0, j, 4 + h : 5 + h], crow[0, j, h : h + 1], row, col))
        for q, (j, h, rows) in zip(qk, pairs)
    ]
    outs = [mm(a, va[0, h, rows]) for a, (j, h, rows) in zip(attn, pairs)]
    for out, (j, h, rows) in zip(outs, pairs):
        o_o[0, h, rows] = out


def mean_of(vbar, h):
    pair = vbar[:, 128 * (h // 2) : 128 * (h // 2) + 128]
    return (pair if h % 2 == 0 else swap_halves(pair))[0:1]


def finish_kernel(b, pos, o_loc, fq, ccol, pack, smid, vbar, inv_o, turn_o, st_o, keep_o, send_o):
    chunk = ccol.shape[1] // 2
    zcols = pack[pack.shape[0] - 1].astype(F32)
    states = unpack_states(pack, b, zcols)
    lane = lanes_of((chunk, 128))
    cend = ccol[0, chunk - 1 : chunk]
    pairs = pairs_of(chunk)
    near = []
    for h in range(4):
        near.append(low(states[h]))
        near.append(low(jnp.exp(cend[:, h : h + 1]) * states[h] + smid[0, h]))
        for j in range(2):
            st_o[0, h, j] = near[2 * h + j]
    inter = [mm(fq[0, h, rows], near[2 * h + j]) for j, h, rows in pairs]
    outs = [
        o_loc[0, h, rows] + jnp.exp(ccol[0, rows, h : h + 1]) * part for part, (j, h, rows) in zip(inter, pairs)
    ]
    dens = [jnp.broadcast_to(o[:, 64:65], o.shape) for o in outs]
    invs = [lax.rsqrt(den * den + 1.0) for den in dens]
    att = [[None] * 4, [None] * 4]
    for o, den, inv, (j, h, rows) in zip(outs, dens, invs, pairs):
        mean = mean_of(vbar, h)
        att[j][h] = (o + den * mean) * inv
        inv_o[0, h, rows] = jnp.where(lane < 64, inv, 0.0)
        turn_o[0, h, rows] = mean - den * inv * att[j][h]
    first = pos[3] == 0
    for p in range(2):
        both = [
            jnp.where(lane < 64, att[j][2 * p], swap_halves(att[j][2 * p + 1])) for j in range(2)
        ]
        keep_o[0, :, 128 * p : 128 * p + 128] = jnp.where(first, both[0], both[1]).astype(BF16)
        send_o[0, :, 128 * p : 128 * p + 128] = jnp.where(first, both[1], both[0]).astype(BF16)


def dp_of(pos, mz, mx):
    return (pos[0] ^ mz) * 2 + (pos[1] ^ mx)


def feed_chunks(pos, near, far, cot, cott, feed, feedt, target, up_s, dn_s, hid_s, gp_s, big_s):
    seqs, chunk, _ = cot.shape
    nz = far.shape[0]
    width, both = up_s.shape
    hidden = both // 2
    rows_up = width // (2 * nz)
    for my in range(2):
        cols = slice(my * hidden, (my + 1) * hidden)
        for mx in range(2):
            k = 2 * my + mx
            piece = far if k == 3 else near.at[pl.ds(k * nz, nz)]
            for z in range(nz):
                at = pl.multiple_of((2 * z + (pos[1] ^ mx)) * rows_up, rows_up)
                up_s[pl.ds(at, rows_up), cols] = piece[z, 0:rows_up]
                dn_s[pl.ds(at, rows_up), cols] = piece[z, rows_up : 2 * rows_up]

    def scatter(offset):
        for my in range(2):
            cols = slice(my * hidden, (my + 1) * hidden)
            for mx in range(2):
                for mz in range(nz):
                    at = pl.multiple_of(dp_of(pos, mz, mx) * rows_up, rows_up)
                    target[my, mx, mz, offset : offset + rows_up, :] = big_s[pl.ds(at, rows_up), cols]

    spans = [slice(r * chunk, (r + 1) * chunk) for r in range(seqs)]
    outs, grads = [], []
    pres = [mm(feed[rows], up_s[...]) for rows in spans]
    ghs = [mm(cot[r], dn_s[...]) for r in range(seqs)]
    for r, rows in enumerate(spans):
        cdf, pdf = normal_parts(pres[r])
        hid_s[rows] = low(pres[r] * cdf)
        gp_s[rows] = low(ghs[r] * (cdf + pres[r] * pdf))
    for rows in spans:
        outs.append(mm(hid_s[rows], dn_s[...], NT))
        grads.append(mm(gp_s[rows], up_s[...], NT))
    big_s[...] = low(mm(feedt[...], gp_s[...]))
    scatter(0)
    big_s[...] = low(mm(jnp.concatenate([cott[r] for r in range(seqs)], axis=1), hid_s[...]))
    scatter(rows_up)
    return outs, grads


def feed_first_kernel(
    pos, akeep, arecv, x, cot, cott, vec, near_own, far_own, near, far,
    gsend_o, acc_o, gf_o, mid_o, feed_o, feedt_o, att_o, ow_o,
    up_s, dn_s, hid_s, gp_s, big_s,
):
    seqs, chunk, _ = x.shape
    nz = far.shape[0]
    rows_up = up_s.shape[0] // (2 * nz)
    first = pos[3] == 0
    for mc, (some, rest) in enumerate(((near_own, far_own), (near, far))):
        for my in range(2):
            t = (pos[2] ^ my) * 2 + (pos[3] ^ mc)
            for mx in range(2):
                k = 2 * my + mx
                for z in range(nz):
                    at = pl.multiple_of(((2 * z + (pos[1] ^ mx)) * 4 + t) * 16, 16)
                    source = rest if k == 3 else some.at[pl.ds(k * nz, nz)]
                    ow_o[pl.ds(at, 16), :] = source[z, 2 * rows_up :]
    gain, shift = vec[6:7], vec[7:8]
    for r in range(seqs):
        rows = slice(r * chunk, (r + 1) * chunk)
        mine, theirs = akeep[r], arecv[r]
        att = jnp.concatenate([jnp.where(first, mine, theirs), jnp.where(first, theirs, mine)], axis=1)
        att_o[rows] = att
        mid = x[r].astype(F32) + mm(att, ow_o[...])
        mid_o[rows] = mid
        unit, _ = norm_of(mid)
        feed = unit * gain + shift
        feed_o[rows] = low(feed)
        feedt_o[:, rows] = low(feed.T)
    outs, grads = feed_chunks(pos, near, far, cot, cott, feed_o, feedt_o, gsend_o, up_s, dn_s, hid_s, gp_s, big_s)
    for r, (out, grad) in enumerate(zip(outs, grads)):
        acc_o[r * chunk : (r + 1) * chunk] = out
        gf_o[r * chunk : (r + 1) * chunk] = grad


def feed_second_kernel(
    pos, cot, cott, vec, near, far, acc, gf_in, mid_in, feed, feedt, att, ow,
    out_o, gm_o, gak_o, gas_o, gkeep_o, okeep_o, osend_o, gv_o,
    up_s, dn_s, hid_s, gp_s, gb_s, big_s,
):
    seqs, chunk, width = cot.shape
    nz = far.shape[0]
    first = pos[3] == 0
    outs, grads = feed_chunks(pos, near, far, cot, cott, feed, feedt, gkeep_o, up_s, dn_s, hid_s, gp_s, big_s)
    gain = vec[6:7]
    gain_sum = jnp.zeros((1, width), F32)
    shift_sum = jnp.zeros((1, width), F32)
    for r in range(seqs):
        rows = slice(r * chunk, (r + 1) * chunk)
        mid = mid_in[rows]
        out_o[r] = low(mid + (acc[rows] + outs[r]))
        unit, inv = norm_of(mid)
        gf = gf_in[rows] + grads[r]
        gain_sum += jnp.sum(gf * unit, axis=0, keepdims=True)
        shift_sum += jnp.sum(gf, axis=0, keepdims=True)
        gm = cot[r].astype(F32) + norm_back(gf * gain, unit, inv)
        gm_o[r] = gm
        gb = low(gm)
        gb_s[rows] = gb
        ga = low(mm(gb, ow[...], NT))
        half = width // 2
        gak_o[r] = jnp.where(first, ga[:, :half], ga[:, half:])
        gas_o[r] = jnp.where(first, ga[:, half:], ga[:, :half])
    gv_o[...] = jnp.concatenate([gain_sum, shift_sum, jnp.zeros((6, width), F32)], axis=0)
    big_s[:, 0:width] = low(mm(att[...], gb_s[...], TN))
    for mc, target in ((0, okeep_o), (1, osend_o)):
        for my in range(2):
            t = (pos[2] ^ my) * 2 + (pos[3] ^ mc)
            for mx in range(2):
                for mz in range(nz):
                    at = pl.multiple_of((dp_of(pos, mz, mx) * 4 + t) * 16, 16)
                    target[my, mx, mz] = big_s[pl.ds(at, 16), 0:width]


def adjoint_kernel(b, pos, gak, gar, inv_root, turn, fq, ccol, g_o, scaled_o, l1_o, pack_o):
    chunk = ccol.shape[1] // 2
    lane = lanes_of((chunk, 128))
    first = pos[3] == 0
    pairs = pairs_of(chunk)
    gas = []
    for j in range(2):
        for p in range(2):
            cols = slice(128 * p, 128 * p + 128)
            pair = jnp.where(first == (j == 0), gak[0, :, cols], gar[0, :, cols]).astype(F32)
            gas += [pair, swap_halves(pair)]
    gns = [low(ga * inv_root[0, h, rows]).astype(F32) for ga, (j, h, rows) in zip(gas, pairs)]
    gds = [
        jnp.sum(gn * turn[0, h, rows], axis=1, keepdims=True) for gn, (j, h, rows) in zip(gns, pairs)
    ]
    scaled = []
    for gn, gd, (j, h, rows) in zip(gns, gds, pairs):
        gd = jnp.broadcast_to(gd, gn.shape)
        high = low(gd).astype(F32)
        g = jnp.where(lane == 64, high, jnp.where(lane == 65, gd - high, gn))
        g_o[0, h, rows] = low(g)
        scaled.append(low(g * jnp.exp(ccol[0, rows, h : h + 1])))
        scaled_o[0, h, rows] = scaled[-1]
    parts = [mm(fq[0, h, rows], g, TN) for g, (j, h, rows) in zip(scaled, pairs)]
    states = []
    for h in range(4):
        l1_o[0, h] = parts[4 + h]
        states.append(parts[h] + jnp.exp(ccol[0, chunk - 1 : chunk, h : h + 1]) * parts[4 + h])
    pack_states(states, pack_o, b, pack_o.shape[0] - 1, split=True)


def local_back_kernel(b, fq, fk, va, g, scaled, st, ccol, crow, dfq_o, dfk_o, dva_o):
    chunk = crow.shape[3]
    row, col = lower_tri(chunk)
    pairs = pairs_of(chunk)
    for half in (pairs[:4], pairs[4:]):
        qk = [mm(fq[0, h, rows], fk[0, h, rows], NT) for j, h, rows in half]
        da = [mm(g[0, h, rows], va[0, h, rows], NT) for j, h, rows in half]
        inter = [mm(scaled[0, h, rows], st[0, h, j], NT) for j, h, rows in half]
        attn, dp = [], []
        for q, d, (j, h, rows) in zip(qk, da, half):
            w = weights_of(ccol[0, rows, h : h + 1], crow[0, j, 4 + h : 5 + h], crow[0, j, h : h + 1], row, col)
            attn.append(low(q * w))
            dp.append(low(d * w))
        dva = [mm(a, g[0, h, rows], TN) for a, (j, h, rows) in zip(attn, half)]
        dfk = [mm(d, fq[0, h, rows], TN) for d, (j, h, rows) in zip(dp, half)]
        dfq = [mm(d, fk[0, h, rows]) for d, (j, h, rows) in zip(dp, half)]
        for i, (j, h, rows) in enumerate(half):
            dfq_o[0, h, rows] = dfq[i] + inter[i]
            dfk_o[0, h, rows] = dfk[i]
            dva_o[0, h, rows] = dva[i]


def close_kernel(
    b, pos, units, attend, fq, fk, va, dfq, dfk, dva, ccol, ucol, pack, l1, st, wmix, gv, back,
    m00_o, m01_o, m10_o, m11_o, gnk_o, gns_o,
    acc_s, gm_s, gate_s, vsum_s, big_s,
    *, seqs_total,
):
    seqs = seqs_total
    chunk = units.shape[1] // 2
    nz = m00_o.shape[0]
    lane = lanes_of((chunk, 128))
    row, col = lower_tri(chunk)
    upper = jnp.where(row <= col, 1.0, 0.0).astype(BF16)
    zcols = pack[pack.shape[0] - 1].astype(F32)
    arrived = unpack_states(pack, b, zcols, last=64)
    wide = lanes_of((128, 128))

    @pl.when(b == 0)
    def _():
        gate_s[...] = jnp.zeros_like(gate_s)
        vsum_s[...] = jnp.zeros_like(vsum_s)

    pairs = pairs_of(chunk)
    spans = [slice(j * chunk, (j + 1) * chunk) for j in range(2)]
    cums = [ccol[0, rows] for rows in spans]
    freshs = [ucol[0, rows] for rows in spans]
    douts = [jnp.exp(cum[chunk - 1 : chunk] - cum) * fresh for cum, fresh in zip(cums, freshs)]
    nears = []
    for j, h, rows in pairs:
        adj = arrived[h]
        if j == 0:
            adj = l1[0, h] + jnp.exp(ccol[0, 2 * chunk - 1 : 2 * chunk, h : h + 1]) * adj
        zs = adj[:, 64:65] + adj[:, 65:66]
        high = low(zs).astype(F32)
        nears.append(low(jnp.where(wide == 64, high, jnp.where(wide == 65, zs - high, adj))))
    dk_fars = [mm(va[0, h, rows], near, NT) for near, (j, h, rows) in zip(nears, pairs)]
    dv_fars = [mm(fk[0, h, rows], near) for near, (j, h, rows) in zip(nears, pairs)]
    kds, qds, levels = [], [], []
    pqs, pks, dvs = [], [], []
    for i, (j, h, rows) in enumerate(pairs):
        d = douts[j][:, h : h + 1]
        keys, queries = fk[0, h, rows].astype(F32), fq[0, h, rows].astype(F32)
        dk_far = d * dk_fars[i]
        dk = dk_far + dfk[0, h, rows]
        dq = dfq[0, h, rows]
        kds.append(jnp.sum(keys * dk, axis=1, keepdims=True))
        qds.append(jnp.sum(queries * dq, axis=1, keepdims=True))
        passed = st[0, h, j].astype(F32) * nears[i].astype(F32)
        passed = jnp.sum(jnp.sum(passed, axis=0, keepdims=True), axis=1, keepdims=True)
        total = jnp.sum(jnp.sum(keys * dk_far, axis=0, keepdims=True), axis=1, keepdims=True)
        levels.append(total + jnp.exp(cums[j][chunk - 1 : chunk, h : h + 1]) * passed)
        dvs.append(dva[0, h, rows] + d * dv_fars[i])
        pks.append(low(dk * swap_halves(keys)))
        pqs.append(low(dq * swap_halves(queries)))
    grads = [
        [mm(jnp.concatenate(ps[4 * j + 2 * p : 4 * j + 2 * p + 2], axis=1), back[p]) for ps in (pqs, pks) for p in range(2)]
        for j in range(2)
    ]
    bias_sum = jnp.zeros((1, 128), F32)
    gms = []
    for j in range(2):
        kd = qd = jnp.zeros((chunk, 128), F32)
        level = jnp.zeros((1, 128), F32)
        for h in range(4):
            kd = jnp.where(lane == h, kds[4 * j + h], kd)
            qd = jnp.where(lane == h, qds[4 * j + h], qd)
            level = jnp.where(lanes_of((1, 128)) == h, levels[4 * j + h], level)
        dlog = tri_sum(upper, qd - kd) + level
        dlogit = jnp.where(lane < 4, freshs[j] * dlog - (1.0 - freshs[j]) * kd, 0.0)
        bias_sum += jnp.sum(dlogit, axis=0, keepdims=True)
        values = [jnp.where(lane < 64, dvs[4 * j + 2 * p], swap_halves(dvs[4 * j + 2 * p + 1])) for p in range(2)]
        gm = jnp.concatenate([low(x) for x in (*grads[j], *values, dlogit)], axis=1)
        gm_s[pl.ds(pl.multiple_of((2 * b + j) * chunk, chunk), chunk), :] = gm
        gms.append(gm)
    normed = [mm(gm, wmix[...], NT) for gm in gms]
    vsum_s[0:1] += sum(jnp.sum(n * units[0, rows], axis=0, keepdims=True) for n, rows in zip(normed, spans))
    vsum_s[1:2] += sum(jnp.sum(n, axis=0, keepdims=True) for n in normed)
    first = pos[3] == 0
    gnk_o[0] = jnp.where(first, normed[0], normed[1])
    gns_o[0] = low(jnp.where(first, normed[1], normed[0]))
    gate_s[0:1] += bias_sum

    @pl.when(b == seqs - 1)
    def _():
        width = acc_s.shape[0]
        acc_s[...] = mm(attend[...].reshape(gm_s.shape[0], width), gm_s[...], TN)
        table = jnp.concatenate(
            [jnp.zeros((4, width), F32), vsum_s[0:2], gv[0:2], jnp.zeros((120, width), F32)], axis=0
        ).T
        total = gate_s[0:1]
        high = low(total).astype(F32)
        rest = jnp.broadcast_to(total - high, (8, 128))
        both = pltpu.roll(jnp.broadcast_to(high, (8, 128)), 8, 1) + pltpu.roll(rest, 12, 1)
        biases = jnp.broadcast_to(both[0:1], (width, 128))
        side = jnp.where(lanes_of((width, 128)) < 4, acc_s[:, 768:896], table) + biases
        big_s[:, 0:768] = acc_s[:, 0:768].astype(BF16)
        big_s[:, 768:896] = side.astype(BF16)
        for my in range(2):
            for mx in range(2):
                for mz in range(nz):
                    at = pl.multiple_of(chip_row(pos, mz, mx, my), 32)
                    (m00_o, m01_o, m10_o, m11_o)[2 * my + mx][mz] = big_s[pl.ds(at, 32), :]


def final_kernel(pos, keep, recv, mix_o, gate_o, bias_o, *vec_o):
    first = pos[3] == 0
    mine, theirs = keep[...], recv[...]
    halves = (jnp.where(first, mine, theirs), jnp.where(first, theirs, mine))
    width = mix_o.shape[1] // 6
    for i in range(3):
        for s in range(2):
            mix_o[:, (2 * i + s) * width : (2 * i + s + 1) * width] = halves[s][:, i * width : (i + 1) * width]
    sides = [half[:, 3 * width :] for half in halves]
    lane = lanes_of(sides[0].shape)
    both = jnp.concatenate([sides[0] + sides[1], sides[0], sides[1], jnp.zeros((80, 128), F32)], axis=0).T
    gate_o[0:4] = both[0:4, 16:32]
    gate_o[4:8] = both[0:4, 32:48]
    for i, out in enumerate(vec_o):
        out[...] = both[4 + i, 0:16]
    sums = [side[0:8] + pltpu.roll(side[0:8], 124, 1) for side in sides]
    row = jnp.where(lane[0:8] < 4, pltpu.roll(sums[0], 120, 1), pltpu.roll(sums[1], 124, 1))
    bias_o[...] = row[0, 0:8]


def input_kernel(b, x, gm, keep, recv, vec, o, done_o):
    done_o[...] = jnp.zeros_like(done_o)
    unit, inv = norm_of(x[0].astype(F32))
    grad = keep[0] + recv[0].astype(F32)
    o[0] = gm[0] + norm_back(grad * vec[4:5], unit, inv)


def hold_kernel(*refs):
    sems = refs[-1]
    count = (len(refs) - 1) // 2
    copies = [
        pltpu.make_async_copy(refs[i], refs[count + i], sems.at[i]) for i in range(count)
    ]
    for copy in copies:
        copy.start()
    for copy in copies:
        copy.wait()


def halves_kernel(by_x, by_y, x_half, y_half, sems):
    half = x_half.shape[0]
    copies = [
        pltpu.make_async_copy(by_x.at[pl.ds(0, half)], x_half, sems.at[0]),
        pltpu.make_async_copy(by_y.at[pl.ds(half, half)], y_half, sems.at[1]),
    ]
    for copy in copies:
        copy.start()
    for copy in copies:
        copy.wait()


def gather_kernel(*refs):
    parts, out, sems = refs[:-2], refs[-2], refs[-1]
    copies, at = [], 0
    for i, part in enumerate(parts):
        copies.append(pltpu.make_async_copy(part, out.at[pl.ds(at, part.shape[0])], sems.at[i]))
        at += part.shape[0]
    for copy in copies:
        copy.start()
    for copy in copies:
        copy.wait()


def pause_kernel(out):
    out[...] = jnp.zeros_like(out)


def join_kernel(pos, *refs, axis):
    parts, out, sems = refs[:-2], refs[-2], refs[-1]
    copies = [
        pltpu.make_async_copy(part, out.at[pos[axis] ^ i], sems.at[i]) for i, part in enumerate(parts)
    ]
    for copy in copies:
        copy.start()
    for copy in copies:
        copy.wait()


def pair_sum_kernel(keep, recv, okeep, orecv, x_keep, x_send, y_keep, y_send):
    half = x_keep.shape[1]
    rows = keep.shape[3]
    first, second = slice(0, half), slice(half, 2 * half)
    for i in range(2):
        for my, mx, zs, out in ((i, 0, first, x_keep), (i, 1, first, x_send), (0, i, second, y_keep), (1, i, second, y_send)):
            out[i, :, 0:rows] = low(keep[my, mx, zs].astype(F32) + recv[my, mx, zs].astype(F32))
            out[i, :, rows:] = low(okeep[my, mx, zs].astype(F32) + orecv[my, mx, zs].astype(F32))


def half_sum_kernel(x_keep, x_recv, y_keep, y_recv, x_own, x_far, y_own, y_far):
    for keep, recv, own, far in ((x_keep, x_recv, x_own, x_far), (y_keep, y_recv, y_own, y_far)):
        for i, out in ((0, own), (1, far)):
            out[...] = low(keep[i].astype(F32) + recv[i].astype(F32))


def line_sum_kernel(x_own, x_recv, y_own, y_recv, *outs):
    half = x_own.shape[0]
    for i in range(half):
        outs[i][...] = low(x_own[i].astype(F32) + x_recv[i].astype(F32))
        outs[half + i][...] = low(y_own[i].astype(F32) + y_recv[i].astype(F32))


def sum_of_four(refs):
    a, b, c, d = (ref[...].astype(F32) for ref in refs)
    return (a + b) + (c + d)


def mix_sum_kernel(m0, m1, m2, m3, *outs):
    total = sum_of_four((m0, m1, m2, m3))
    side = total[..., 768:896]
    rest = side - low(side).astype(F32)
    lane = lanes_of(side.shape)
    moved = jnp.where((lane >= 12) & (lane < 16), side + pltpu.roll(rest, 4, side.ndim - 1), side)
    for i, out in enumerate(outs):
        out[:, 0:768] = low(total[i, :, 0:768])
        out[:, 768:896] = low(moved[i])


def feed_last_kernel(a, b, c, d, up_o, down_o, out_o, done_o):
    done_o[...] = jnp.zeros_like(done_o)
    total = sum_of_four((a, b, c, d))
    rows = up_o.shape[0]
    up_o[...] = total[0:rows]
    down_o[...] = total[rows : 2 * rows]
    out_o[...] = total[2 * rows :]


def mix_last_kernel(pos, a, b, c, d, keep_o, send_o):
    total = sum_of_four((a, b, c, d))
    rows = keep_o.shape[0]
    first = pos[3] == 0
    keep_o[...] = jnp.where(first, total[:rows], total[rows:])
    send_o[...] = jnp.where(first, total[rows:], total[:rows])


def call(kernel, steps, ins, outs, scratch=(), us=1.0, name=None, limit=12):
    def spec(kind):
        if kind in "da":
            return pl.BlockSpec(memory_space=pl.ANY)
        return pl.BlockSpec(memory_space=pltpu.SMEM if kind == "m" else pltpu.VMEM)

    kinds = [kind for kind, _ in ins]
    out_kinds = [kind for kind, _, _ in outs]
    all_kinds = kinds + out_kinds + ["w"] * len(scratch)

    def run(*refs):
        used = [(kind, ref) for kind, ref in zip(all_kinds, refs) if kind != "d"]
        if not steps:
            kernel(*[ref for _, ref in used])
            return

        def one(b, carry):
            kernel(b, *[ref.at[pl.ds(b, 1)] if kind == "s" else ref for kind, ref in used])
            return carry

        lax.fori_loop(0, steps, one, 0)

    return pl.pallas_call(
        run,
        in_specs=[spec(kind) for kind in kinds],
        out_specs=[spec(kind) for kind in out_kinds],
        out_shape=[jax.ShapeDtypeStruct(shape, dtype) for _, shape, dtype in outs],
        scratch_shapes=list(scratch),
        compiler_params=pltpu.CompilerParams(vmem_limit_bytes=limit * 1024 * 1024),
        cost_estimate=pl.CostEstimate(flops=int(us * 1.15e9), bytes_accessed=0, transcendentals=0),
        name=name,
    )(*[a for _, a in ins])


def xor_with(a, mask, count):
    return lax.ppermute(a, BOTH, [(i, i ^ mask) for i in range(count)])


def body(
    inputs, cotangent, mix_weight, gate_weight, gate_bias, out_weight, gain_first, shift_first, gain_second,
    shift_second, up_weight, down_weight, random_maps,
):
    dp, tensor = lax.axis_size("dp"), lax.axis_size("tensor")
    count = dp * tensor
    place_dp, place_t = lax.axis_index("dp"), lax.axis_index("tensor")
    seqs, chunk, width = inputs.shape
    heads, head = random_maps.shape[0], random_maps.shape[1]
    hidden = up_weight.shape[1]
    core = place_t % 2
    first = core == 0
    direct = dp == 8
    nz = 4
    if direct:
        pos = jnp.stack([place_dp // 2, place_dp % 2, place_t // 2, core]).astype(jnp.int32)
    else:
        pos = jnp.stack([jnp.zeros_like(core)] * 3 + [core]).astype(jnp.int32)
    swap_core = functools.partial(xor_with, mask=1, count=count)

    def mix_pack(mix_w, gate_w, vecs):
        rows = mix_w.shape[0]
        split = mix_w.reshape(rows, 3, 2, width // 2)
        sides = [v[:, None] for v in vecs]
        pad = jnp.zeros((rows, 120), BF16)
        return [
            jnp.concatenate(
                [split[:, 0, s], split[:, 1, s], split[:, 2, s], gate_w[:, 4 * s : 4 * s + 4]] + sides + [pad], axis=1
            )
            for s in range(2)
        ]

    def join(parts, axis, after=()):
        (out,) = call(
            functools.partial(join_kernel, axis=axis), 0, [("m", pos)] + [("a", a) for a in parts] + [("d", a) for a in after],
            [("w", (len(parts), *parts[0].shape), parts[0].dtype)],
            scratch=[pltpu.SemaphoreType.DMA((len(parts),))], name="join",
        )
        return out

    def pause(after, us):
        (out,) = call(
            pause_kernel, 0, [("d", a) for a in after], [("w", (8, 128), F32)], us=us, name="pause",
        )
        return out

    def from_plane(pieces):
        return [pieces[0], xor_with(pieces[1], 4, count), xor_with(pieces[2], 2, count), xor_with(pieces[3], 6, count)]

    other_in = swap_core(inputs)
    vectors = (gain_first, shift_first, gain_second, shift_second)
    long = 2 * chunk
    unit, cot_t = call(
        prepare_kernel, seqs, [("m", pos), ("s", inputs), ("s", other_in), ("s", cotangent)],
        [("s", (seqs, long, width), F32), ("s", (seqs, width, chunk), BF16)], us=2.5, name="prepare",
    )
    if direct:
        rows = mix_weight.shape[0]
        columns = jnp.pad(gate_weight.T, ((0, 16 - heads), (0, 0)))
        place = lax.broadcasted_iota(jnp.int32, columns.shape, 0)
        for i, v in enumerate(vectors):
            columns = jnp.where(place == heads + i, lax.broadcast_in_dim(v, columns.shape, (1,)), columns)
        keep, send = call(
            pack_kernel, 0, [("m", pos), ("w", mix_weight), ("w", columns)], [("w", (rows, 896), BF16)] * 2, name="pack",
        )
        pair = join([keep, swap_core(send)], 3)
        line = join([pair] + [xor_with(pair, 8 * m, count) for m in range(1, nz)], 0, after=[unit])
        w_pieces = [line] + [xor_with(line, m, count) for m in (4, 2, 6)]
        block = jnp.concatenate([up_weight, down_weight.T, out_weight], axis=0)
        (block,) = call(
            hold_kernel, 0, [("a", block), ("d", line)],
            [("w", block.shape, BF16)], scratch=[pltpu.SemaphoreType.DMA((1,))], name="hold",
        )
        ff_line = join([block] + [xor_with(block, 8 * m, count) for m in range(1, nz)], 0, after=w_pieces)
        by_x, by_y = xor_with(ff_line, 4, count), xor_with(ff_line, 2, count)
    else:
        whole = [
            lax.all_gather(a, BOTH, axis=0, tiled=True) for a in (mix_weight, gate_weight, out_weight) + vectors
        ]
        p0, p1 = mix_pack(whole[0], whole[1], whole[3:])
        blocks = jnp.where(first, p0, p1).reshape(nz, 2, 2, 2, 16, 896)
        w_pieces = [blocks[:, mx, my] for my, mx in ((0, 0), (0, 1), (1, 0), (1, 1))]
        up_all = lax.all_gather(up_weight, BOTH, axis=0, tiled=False).reshape(dp, tensor, -1, hidden)
        dn_all = lax.all_gather(down_weight.T, BOTH, axis=0, tiled=False).reshape(dp, tensor, -1, hidden)
        up_all = jnp.moveaxis(up_all, 1, 0).reshape(2, 2, nz, 2, -1, hidden)
        dn_all = jnp.moveaxis(dn_all, 1, 0).reshape(2, 2, nz, 2, -1, hidden)
        out_all = whole[2].reshape(nz, 2, 2, 2, 16, width).transpose(2, 3, 0, 1, 4, 5)
        ff_all = jnp.concatenate([up_all, dn_all, out_all], axis=4)
        ff_all = jnp.where(first, ff_all, ff_all[:, ::-1])
        ff_own, ff_other = (
            jnp.concatenate([ff_all[my, mc, :, mx] for my in range(2) for mx in range(2)]) for mc in range(2)
        )

    maps = lax.dynamic_slice_in_dim(random_maps, core * 4, 4, 0)
    zero = jnp.zeros((head, head), BF16)
    maps_pair = jnp.stack(
        [
            jnp.concatenate(
                [jnp.concatenate([maps[2 * p], zero], 1), jnp.concatenate([zero, maps[2 * p + 1]], 1)], 0
            )
            for p in range(2)
        ]
    )
    flip = jnp.swapaxes(maps, 1, 2)
    maps_back = jnp.stack(
        [
            jnp.concatenate(
                [
                    jnp.concatenate([flip[2 * p], zero], 1),
                    jnp.concatenate([-flip[2 * p], zero], 1),
                    jnp.concatenate([zero, flip[2 * p + 1]], 1),
                    jnp.concatenate([zero, -flip[2 * p + 1]], 1),
                ],
                0,
            )
            for p in range(2)
        ]
    )
    bias = jnp.pad(lax.dynamic_slice_in_dim(gate_bias, core * 4, 4, 0), (0, 124))[None]

    tokens = seqs * long
    feats = (seqs, 4, long, 128)
    npack = 2 * seqs + 1
    attend, fk, fkl, va, ccol, ucol, crow, smid, pack, wmix, vec, vbar = call(
        project_kernel, seqs,
        [("m", pos), ("s", unit)] + [("a", w) for w in w_pieces] + [("w", bias), ("w", maps_pair)],
        [
            ("s", (seqs, long, width), BF16), ("s", feats, BF16), ("s", feats, BF16), ("s", feats, BF16),
            ("s", (seqs, long, 128), F32), ("s", (seqs, long, 128), F32),
            ("s", (seqs, 2, 8, chunk), F32),
            ("s", (seqs, 4, 128, 128), F32),
            ("w", (npack, 128, 128), BF16), ("w", (width, 896), BF16), ("w", (8, width), F32),
            ("w", (8, width // 2), F32),
        ],
        scratch=[pltpu.VMEM((nz, 2, 2, 2, 16, 896), BF16), pltpu.SemaphoreType.DMA((4,))], us=12, name="project",
    )
    ahead = [(i, i + 2) for i in range(count) if (i % tensor) < 2]
    arrived = lax.ppermute(pack, BOTH, ahead)
    fq, fql = call(
        query_kernel, seqs, [("s", attend), ("w", wmix), ("w", maps_pair)], [("s", feats, BF16)] * 2, us=0.3, name="query",
    )
    (o_loc,) = call(
        local_kernel, seqs,
        [("s", fq), ("s", fk), ("s", fql), ("s", fkl), ("s", va), ("s", ccol), ("s", crow)],
        [("s", feats, F32)], us=0.3, name="local",
    )
    if direct:
        half_z = nz // 2
        far_shape = (half_z, *ff_line.shape[1:])
        x_half, y_half = call(
            halves_kernel, 0, [("a", by_x), ("a", by_y), ("d", arrived), ("d", o_loc)], [("w", far_shape, BF16)] * 2,
            scratch=[pltpu.SemaphoreType.DMA((2,))], us=0.3, name="halves",
        )
        near_parts = [ff_line, by_x, by_y]
        (ff_near,) = call(
            gather_kernel, 0, [("a", a) for a in near_parts] + [("d", x_half)],
            [("w", (3 * nz, *ff_line.shape[1:]), BF16)], scratch=[pltpu.SemaphoreType.DMA((3,))], us=0.5, name="near",
        )
        before_finish = [x_half]
    else:
        before_finish = []
    (inv_root, turn, st, att_keep, att_send) = call(
        finish_kernel, seqs,
        [("m", pos), ("s", o_loc), ("s", fq), ("s", ccol), ("w", arrived), ("s", smid), ("w", vbar)]
        + [("d", a) for a in before_finish],
        [
            ("s", feats, F32), ("s", feats, F32), ("s", (seqs, 4, 2, 128, 128), BF16),
            ("s", (seqs, chunk, width // 2), BF16), ("s", (seqs, chunk, width // 2), BF16),
        ],
        us=0.3, name="finish",
    )
    att_recv = swap_core(att_send)
    if direct:
        near_other = swap_core(ff_near)
        far_parts = [xor_with(x_half, 2, count), xor_with(y_half, 4, count)]
        (ff_far,) = call(
            gather_kernel, 0, [("a", a) for a in far_parts] + [("d", att_keep)],
            [("w", ff_line.shape, BF16)], scratch=[pltpu.SemaphoreType.DMA((2,))], name="gather",
        )
        far_other = swap_core(ff_far)
    else:
        ff_near, ff_far, near_other, far_other = ff_own[: 3 * nz], ff_own[3 * nz :], ff_other[: 3 * nz], ff_other[3 * nz :]

    own = seqs * chunk
    nrows = ff_near.shape[1]
    payload, out_payload = (2, 2, nz, nrows - 16, hidden), (2, 2, nz, 16, hidden)
    rows_low, rows_full = ("w", (own, width), BF16), ("w", (own, width), F32)
    work = [
        pltpu.VMEM((width, 2 * hidden), BF16), pltpu.VMEM((width, 2 * hidden), BF16),
        pltpu.VMEM((own, 2 * hidden), BF16), pltpu.VMEM((own, 2 * hidden), BF16),
    ]
    big = pltpu.VMEM((width, 2 * hidden), BF16)
    g_send, *fed = call(
        feed_first_kernel, 0,
        [("m", pos)] + [
            ("w", a) for a in (
                att_keep, att_recv, inputs, cotangent, cot_t, vec, ff_near, ff_far, near_other, far_other
            )
        ],
        [
            ("w", payload, BF16), rows_full, rows_full, rows_full, rows_low, ("w", (width, own), BF16), rows_low,
            ("w", (width, width), BF16),
        ],
        scratch=[*work, big], us=10, name="feed_first", limit=18,
    )
    g_recv = swap_core(g_send)
    output, grad_middle, ga_keep, ga_send, g_keep, o_keep, o_send, grad_vec = call(
        feed_second_kernel, 0,
        [("m", pos)] + [("w", a) for a in (cotangent, cot_t, vec, ff_near, ff_far, *fed)],
        [
            ("w", (seqs, chunk, width), BF16), ("w", (seqs, chunk, width), F32),
            ("w", (seqs, chunk, width // 2), BF16), ("w", (seqs, chunk, width // 2), BF16),
            ("w", payload, BF16), ("w", out_payload, BF16), ("w", out_payload, BF16), ("w", (8, width), F32),
        ],
        scratch=[
            *work, pltpu.VMEM((own, width), BF16), big,
        ],
        us=10, name="feed_second", limit=18,
    )
    ga_recv = swap_core(ga_send)

    if direct:
        o_recv = swap_core(o_send)
        half_z = nz // 2
        two, one = (2, half_z, nrows, hidden), (half_z, nrows, hidden)
        x_keep, x_send, y_keep, y_send = call(
            pair_sum_kernel, 0, [("w", g_keep), ("w", g_recv), ("w", o_keep), ("w", o_recv)], [("w", two, BF16)] * 4,
            us=0.6, name="pair_sum",
        )
        x_recv, y_recv = xor_with(x_send, 4, count), xor_with(y_send, 2, count)
        before_adjoint = [x_keep]
    else:
        before_adjoint = []
        g_keep, g_send = (jnp.concatenate(parts, axis=3) for parts in ((g_keep, o_keep), (g_send, o_send)))
        by_core = jnp.where(first, jnp.stack([g_keep, g_send]), jnp.stack([g_send, g_keep]))
        by_rows = by_core.transpose(3, 2, 1, 0, 4, 5)
        rows_up = (nrows - 16) // 2
        ups = by_rows[..., :rows_up, :].reshape(nz * 2, 4, rows_up, hidden).transpose(1, 0, 2, 3)
        dns = by_rows[..., rows_up : 2 * rows_up, :].reshape(nz * 2, 4, rows_up, hidden).transpose(1, 0, 2, 3)
        ups = ups.reshape(4, dp, -1, hidden).transpose(1, 0, 2, 3)
        dns = dns.reshape(4, dp, -1, hidden).transpose(1, 0, 2, 3)
        outs = by_rows[..., 2 * rows_up :, :].reshape(width, width)

        def reduced(a):
            return lax.psum_scatter(a.astype(F32).reshape(count, -1, a.shape[-1]), BOTH, scatter_dimension=0)

        up_grad, down_grad, out_grad = reduced(ups), reduced(dns).T, reduced(outs)

    g, scaled, l1, pack_b = call(
        adjoint_kernel, seqs,
        [("m", pos), ("s", ga_keep), ("s", ga_recv), ("s", inv_root), ("s", turn), ("s", fq), ("s", ccol)]
        + [("d", a) for a in before_adjoint],
        [
            ("s", feats, BF16), ("s", feats, BF16), ("s", (seqs, 4, 128, 128), F32), ("w", (npack, 128, 128), BF16),
        ],
        us=0.3, name="adjoint",
    )
    behind = [(i, i - 2) for i in range(count) if (i % tensor) >= 2]
    arrived_b = lax.ppermute(pack_b, BOTH, behind)
    dfq, dfk, dva = call(
        local_back_kernel, seqs,
        [("s", fq), ("s", fk), ("s", va), ("s", g), ("s", scaled), ("s", st), ("s", ccol), ("s", crow)],
        [("s", feats, F32), ("s", feats, F32), ("s", feats, F32)],
        us=0.3, name="local_back",
    )
    before_close = []
    if direct:
        x_own, x_far, y_own, y_far = call(
            half_sum_kernel, 0, [("w", a) for a in (x_keep, x_recv, y_keep, y_recv)] + [("d", dfq)],
            [("w", one, BF16)] * 4, us=0.4, name="half_sum",
        )
        x_recv, y_recv = xor_with(x_far, 2, count), xor_with(y_far, 4, count)
        before_close = [x_own]
    *m_pieces, gn_keep, gn_send = call(
        functools.partial(close_kernel, seqs_total=seqs), seqs,
        [("m", pos), ("s", unit), ("w", attend), ("s", fq), ("s", fk), ("s", va), ("s", dfq),
         ("s", dfk), ("s", dva), ("s", ccol), ("s", ucol), ("w", arrived_b), ("s", l1), ("s", st),
         ("w", wmix), ("w", grad_vec), ("w", maps_back)] + [("d", a) for a in before_close],
        [*[("w", (nz, 32, 896), BF16)] * 4, ("s", (seqs, chunk, width), F32), ("s", (seqs, chunk, width), BF16)],
        scratch=[
            pltpu.VMEM((width, 896), F32), pltpu.VMEM((tokens, 896), BF16), pltpu.VMEM((8, 128), F32),
            pltpu.VMEM((8, width), F32), pltpu.VMEM((width, 896), BF16),
        ],
        us=14.7, name="close",
    )
    if direct:
        g_line = call(
            line_sum_kernel, 0, [("w", a) for a in (x_own, x_recv, y_own, y_recv)] + [("d", gn_keep)],
            [("w", (nrows, hidden), BF16)] * nz, us=0.4, name="line_sum",
        )
        m_parts = from_plane(m_pieces)
    gn_recv = swap_core(gn_send)
    def finish_input(after):
        return call(
            input_kernel, seqs,
            [("s", inputs), ("s", grad_middle), ("s", gn_keep), ("s", gn_recv), ("w", vec)] + [("d", a) for a in after],
            [("s", (seqs, chunk, width), F32), ("w", (8, 128), F32)], us=0.3, name="input_grad",
        )

    if direct:
        m_plane = call(
            mix_sum_kernel, 0, [("w", a) for a in m_parts] + [("d", pause([g_line[0]], 40)), ("d", gn_recv)],
            [("w", (32, 896), BF16)] * nz, us=0.4, name="mix_sum",
        )
        input_grad, input_done = finish_input([m_plane[0]])
        g_parts = [g_line[0]] + [xor_with(g_line[m], 8 * m, count) for m in range(1, nz)]
        up_grad, down_back, out_grad, feed_done = call(
            feed_last_kernel, 0, [("w", a) for a in g_parts],
            [("w", shape, F32) for shape in (up_weight.shape, down_weight.shape[::-1], out_weight.shape, (8, 128))],
            us=0.3, name="feed_last",
        )
        down_grad = down_back.T
        mix_parts = [m_plane[0]] + [xor_with(m_plane[m], 8 * m, count) for m in range(1, nz)]
        m_keep, m_send = call(
            mix_last_kernel, 0, [("m", pos)] + [("w", a) for a in mix_parts] + [("d", feed_done), ("d", input_done)],
            [("w", (mix_weight.shape[0], 896), F32)] * 2, name="mix_last",
        )
        m_recv = swap_core(m_send)
    else:
        input_grad, input_done = finish_input([])
        m_all = jnp.stack(m_pieces).astype(F32).reshape(2, 2, nz, 32, 896)
        mine_rows = m_all.transpose(2, 1, 0, 3, 4).reshape(count, -1, 896)
        keep_part = lax.psum_scatter(mine_rows * jnp.where(first, 1.0, 0.0), BOTH, scatter_dimension=0)
        far_part = lax.psum_scatter(mine_rows * jnp.where(first, 0.0, 1.0), BOTH, scatter_dimension=0)
        m_keep = jnp.where(first, keep_part, far_part)
        m_recv = jnp.where(first, far_part, keep_part)
    if direct:
        mix_grad, gate_back, bias_grad, *per_row = call(
            final_kernel, 0, [("m", pos), ("w", m_keep), ("w", m_recv)],
            [("w", mix_weight.shape, F32), ("w", gate_weight.shape[::-1], F32), ("w", (heads,), F32)]
            + [("w", gain_first.shape, F32)] * 4,
            us=1.2, name="final",
        )
        gate_grad = gate_back.T
    else:
        m_low = jnp.where(first, m_keep, m_recv)
        m_high = jnp.where(first, m_recv, m_keep)
        mix_grad = jnp.concatenate(
            [part[:, 256 * i : 256 * i + 256] for i in range(3) for part in (m_low, m_high)], axis=1
        )
        gate_grad = jnp.concatenate([m_low[:, 768:772], m_high[:, 768:772]], axis=1)
        bias_grad = jnp.concatenate([m[0, 776:780] + m[0, 780:784] for m in (m_low, m_high)])
        per_row = [m_keep[:, 772 + i] + m_recv[:, 772 + i] for i in range(4)]
    return (
        output, input_grad, mix_grad, gate_grad, bias_grad, out_grad,
        *per_row, up_grad, down_grad,
    )


def solution(mesh):
    rows, spread = P(("dp", "tensor"), None), P(("dp", "tensor"))
    tokens = P("dp", "tensor", None)
    in_specs = (
        tokens, tokens, rows, rows, P(), rows, spread, spread, spread, spread, P("dp", "tensor"), P("tensor", "dp"), P(),
    )
    out_specs = (
        tokens, tokens, rows, rows, P(), rows, spread, spread, spread, spread, P("dp", "tensor"), P("tensor", "dp"),
    )
    return jax.shard_map(body, mesh=mesh, in_specs=in_specs, out_specs=out_specs, check_vma=False)
```

```python
import functools

import jax
import jax.numpy as jnp
from jax import lax
from jax.experimental import pallas as pl
from jax.experimental.pallas import tpu as pltpu
from jax.sharding import PartitionSpec as P

BOTH = ("dp", "tensor")
F32 = jnp.float32
BF16 = jnp.bfloat16
EPSILON = 1e-05
DENSITY = 0.3989422804014327
SIN = (9.9999999998e-01, -1.6666666617e-01, 8.3333309689e-03, -1.9840860382e-04, 2.7525224003e-06, -2.3888330913e-08)
COS = (9.9999999978e-01, -4.9999999354e-01, 4.1666636104e-02, -1.3888359409e-03, 2.4760057595e-05, -2.6049626765e-07)

NN = (((1,), (0,)), ((), ()))
NT = (((1,), (1,)), ((), ()))
TN = (((0,), (0,)), ((), ()))


def mm(a, b, dims=NN):
    return lax.dot_general(a, b, dims, preferred_element_type=F32)


def low(a):
    return a.astype(BF16)


def lanes_of(shape):
    return lax.broadcasted_iota(jnp.int32, shape, len(shape) - 1)


def swap_halves(a):
    return pltpu.roll(a, 64, 1)


def sincos(a):
    turns = jnp.floor(a * 0.3183098861837907 + 0.5)
    r = (a - turns * 3.140625) - turns * 9.676535897932e-4
    half = turns * 0.5
    sign = 1.0 - 4.0 * (half - jnp.floor(half))
    r2 = r * r
    s = r * (SIN[0] + r2 * (SIN[1] + r2 * (SIN[2] + r2 * (SIN[3] + r2 * (SIN[4] + r2 * SIN[5])))))
    c = COS[0] + r2 * (COS[1] + r2 * (COS[2] + r2 * (COS[3] + r2 * (COS[4] + r2 * COS[5]))))
    return sign * s, sign * c


def normal_parts(v):
    t = pl.reciprocal(1.0 + 0.23164189 * jnp.abs(v), approx=True)
    bell = jnp.exp(-0.5 * (v * v))
    poly = t * (0.127414796 + t * (-0.142248368 + t * (0.7107068705 + t * (-0.7265760135 + t * 0.5307027145))))
    tail = poly * bell
    return jnp.where(v >= 0.0, 1.0 - tail, tail), DENSITY * bell


def three_parts(a):
    high = a.astype(BF16)
    rest = a - high.astype(F32)
    mid = rest.astype(BF16)
    return high, mid, (rest - mid.astype(F32)).astype(BF16)


def tri_sum(tri, a):
    high, mid, rest = (part.astype(F32) for part in three_parts(a))
    packed = mm(tri, low(high + pltpu.roll(mid, 4, 1) + pltpu.roll(rest, 8, 1)))
    return packed + pltpu.roll(packed, 124, 1) + pltpu.roll(packed, 120, 1)


def norm_of(x):
    mean = jnp.mean(x, axis=-1, keepdims=True)
    centered = x - mean
    inv = lax.rsqrt(jnp.mean(centered * centered, axis=-1, keepdims=True) + EPSILON)
    return centered * inv, inv


def norm_back(s, unit, inv):
    return inv * (
        s
        - jnp.mean(s, axis=-1, keepdims=True)
        - unit * jnp.mean(s * unit, axis=-1, keepdims=True)
    )


def chip_row(pos, mz, mx, my):
    return (((pos[0] ^ mz) * 2 + (pos[1] ^ mx)) * 2 + (pos[2] ^ my)) * 32


def lower_tri(n):
    row = lax.broadcasted_iota(jnp.int32, (n, n), 0)
    col = lax.broadcasted_iota(jnp.int32, (n, n), 1)
    return row, col


def unpack_states(pack, b, zcols, last=65):
    lane = lanes_of((128, 128))
    out = []
    for p in range(2):
        both = pack[2 * b + p].astype(F32)
        for h, mat in ((2 * p, both), (2 * p + 1, swap_halves(both))):
            z = jnp.sum(jnp.where(lane == 4 * b + h, zcols, 0.0), axis=1, keepdims=True)
            out.append(jnp.where(lane < 64, mat, jnp.where(lane <= last, z, 0.0)))
    return out


def pack_states(states, pack_o, b, last, split=False):
    lane = lanes_of((128, 128))
    zcols = jnp.where(b == 0, 0.0, pack_o[last].astype(F32))

    def sum_of(s):
        return s[:, 64:65] + s[:, 65:66] if split else s[:, 64:65]

    for p in range(2):
        s0, s1 = states[2 * p], states[2 * p + 1]
        pack_o[2 * b + p] = jnp.where(lane < 64, s0, swap_halves(s1)).astype(BF16)
        zcols = jnp.where(lane == 4 * b + 2 * p, sum_of(s0), zcols)
        zcols = jnp.where(lane == 4 * b + 2 * p + 1, sum_of(s1), zcols)
    pack_o[last] = zcols.astype(BF16)


def pack_kernel(pos, mix, columns, keep_o, send_o):
    width = mix.shape[1] // 6
    rows = mix.shape[0]
    table = jnp.concatenate(
        [columns[...].astype(F32), jnp.zeros((128 - columns.shape[0], rows), F32)], axis=0
    )
    sides = jnp.concatenate([table, jnp.zeros((128, 128 - rows), F32)], axis=1).T[0:rows]
    lane = lanes_of(sides.shape)
    moved = pltpu.roll(sides, 124, 1)
    halves = []
    for s, block in ((0, jnp.where(lane < 4, sides, moved)), (1, moved)):
        parts = [mix[:, (2 * i + s) * width : (2 * i + s + 1) * width] for i in range(3)]
        halves.append(jnp.concatenate(parts + [low(jnp.where(lane < 8, block, 0.0))], axis=1))
    first = pos[3] == 0
    keep_o[...] = jnp.where(first, halves[0], halves[1])
    send_o[...] = jnp.where(first, halves[1], halves[0])


def prepare_kernel(b, pos, own, oth, cot, unit_o, cott_o):
    chunk = own.shape[1]
    first = pos[3] == 0
    mine, theirs = own[0], oth[0]
    for j in range(2):
        unit, _ = norm_of(jnp.where(first == (j == 0), mine, theirs).astype(F32))
        unit_o[0, j * chunk : (j + 1) * chunk] = unit
    cott_o[0] = low(cot[0].astype(F32).T)


def feature_parts(angles, lane):
    s, c = sincos(angles)
    out = []
    turned_s, turned_c = swap_halves(s), swap_halves(c)
    for f, turned in (
        (jnp.where(lane < 64, s, turned_c), jnp.where(lane < 64, c, turned_s)),
        (jnp.where(lane < 64, turned_s, c), jnp.where(lane < 64, turned_c, s)),
    ):
        high = low(f)
        out.append((high, low(f - high.astype(F32)), low(turned)))
    return out


def query_kernel(b, a, wmix, maps, fq_o, fql_o, fqt_o):
    chunk = a.shape[1] // 2
    lane = lanes_of((chunk, 128))
    spans = [slice(j * chunk, (j + 1) * chunk) for j in range(2)]
    mixed = [low(mm(a[0, rows], wmix[:, 0:256])) for rows in spans]
    angles = [[mm(m[:, 128 * p : 128 * p + 128], maps[p]) for p in range(2)] for m in mixed]
    for j, rows in enumerate(spans):
        for p in range(2):
            for i, (high, rest, turned) in enumerate(feature_parts(angles[j][p], lane)):
                fq_o[0, 2 * p + i, rows], fql_o[0, 2 * p + i, rows], fqt_o[0, 2 * p + i, rows] = high, rest, turned


def project_kernel(
    b, pos, units, w0, w1, w2, w3, bias, maps,
    a_o, fk_o, fkl_o, fkt_o, va_o, ccol_o, ucol_o, crow_o, smid_o, pack_o, wmix_o, vec_o, vbar_o,
    w_s, sems,
):
    chunk = units.shape[1] // 2

    @pl.when(b == 0)
    def _():
        copies = [
            pltpu.make_async_copy(piece, w_s.at[:, pos[1] ^ mx, pos[2] ^ my], sems.at[2 * my + mx])
            for piece, (my, mx) in ((w0, (0, 0)), (w1, (0, 1)), (w2, (1, 0)), (w3, (1, 1)))
        ]
        for copy in copies:
            copy.start()
        for copy in copies:
            copy.wait()
        wmix_o[...] = w_s[...].reshape(wmix_o.shape)
        vec_o[...] = wmix_o[:, 768:896].astype(F32).T[0:8]
        vbar_o[...] = mm(jnp.broadcast_to(vec_o[5:6], vec_o.shape).astype(BF16), wmix_o[:, 512:768])

    gain, shift = vec_o[4:5], vec_o[5:6]
    row, col = lower_tri(chunk)
    tri = jnp.where(row >= col, 1.0, 0.0).astype(BF16)
    lane = lanes_of((chunk, 128))
    spans = [slice(j * chunk, (j + 1) * chunk) for j in range(2)]
    attends = [low(units[0, rows] * gain + shift) for rows in spans]
    for a, rows in zip(attends, spans):
        a_o[0, rows] = a
    wide = [mm(a, wmix_o[:, 256:896]) for a in attends]
    mixed = [low(m[:, 0:512]) for m in wide]
    angles = [[mm(m[:, 128 * p : 128 * p + 128], maps[p]) for p in range(2)] for m in mixed]
    douts, ends = [], []
    for j, rows in enumerate(spans):
        logits = wide[j][:, 512:640] + bias[...]
        e = jnp.exp(-jnp.abs(logits))
        w = 1.0 + e
        log1 = jnp.where(w == 1.0, e, jnp.log(w) * (e / jnp.where(w == 1.0, 1.0, w - 1.0)))
        log_gate = jnp.where(lane < 4, jnp.minimum(logits, 0.0) - log1, 0.0)
        fresh = jnp.where(lane < 4, jnp.where(logits >= 0.0, e, 1.0) / w, 0.0)
        cum = jnp.where(lane < 4, tri_sum(tri, log_gate), 0.0)
        ccol_o[0, rows] = cum
        ucol_o[0, rows] = fresh
        crow_o[0, j] = (cum + pltpu.roll(fresh, 4, 1)).T[0:8]
        ends.append(cum[chunk - 1 : chunk])
        douts.append(jnp.exp(ends[j] - cum) * fresh)
    one = jnp.where((lane == 64) | (lane == 65), 1.0, 0.0)
    shares = [[None] * 4, [None] * 4]
    for j, rows in enumerate(spans):
        for p in range(2):
            v = mixed[j][:, 256 + 128 * p : 384 + 128 * p].astype(F32) - vbar_o[0:1, 128 * p : 128 * p + 128]
            for h, vh in ((2 * p, v), (2 * p + 1, swap_halves(v))):
                aug = jnp.where(lane < 64, vh, one)
                va_o[0, h, rows] = low(aug)
                shares[j][h] = low(aug * douts[j][:, h : h + 1])
    locals_ = [[None] * 4, [None] * 4]
    for j, rows in enumerate(spans):
        for p in range(2):
            parts = feature_parts(angles[j][p], lane)
            for h in (2 * p, 2 * p + 1):
                fk_o[0, h, rows], fkl_o[0, h, rows], fkt_o[0, h, rows] = parts[h - 2 * p]
                locals_[j][h] = mm(parts[h - 2 * p][0], shares[j][h], TN)
    states = []
    for h in range(4):
        smid_o[0, h] = locals_[0][h]
        states.append(locals_[0][h] * jnp.exp(ends[1][:, h : h + 1]) + locals_[1][h])
    pack_states(states, pack_o, b, pack_o.shape[0] - 1)


def weights_of(ccol, ucol_row, crow, row, col):
    gap = jnp.minimum(ccol - crow, 0.0)
    return jnp.where(row >= col, jnp.exp(gap), 0.0) * ucol_row


def pairs_of(chunk):
    return [(j, h, slice(j * chunk, (j + 1) * chunk)) for j in range(2) for h in range(4)]


def scores(fq, fk, fql, fkl, h, rows):
    q, k = fq[0, h, rows], fk[0, h, rows]
    return mm(
        jnp.concatenate([q, fql[0, h, rows], q], axis=1), jnp.concatenate([k, k, fkl[0, h, rows]], axis=1), NT
    )


def local_kernel(b, fq, fk, fql, fkl, va, ccol, crow, o_o):
    chunk = crow.shape[3]
    row, col = lower_tri(chunk)
    pairs = pairs_of(chunk)
    qk = [scores(fq, fk, fql, fkl, h, rows) for j, h, rows in pairs]
    attn = [
        low(q * weights_of(ccol[0, rows, h : h + 1], crow[0, j, 4 + h : 5 + h], crow[0, j, h : h + 1], row, col))
        for q, (j, h, rows) in zip(qk, pairs)
    ]
    outs = [mm(a, va[0, h, rows]) for a, (j, h, rows) in zip(attn, pairs)]
    for out, (j, h, rows) in zip(outs, pairs):
        o_o[0, h, rows] = out


def mean_of(vbar, h):
    pair = vbar[:, 128 * (h // 2) : 128 * (h // 2) + 128]
    return (pair if h % 2 == 0 else swap_halves(pair))[0:1]


def finish_kernel(b, pos, o_loc, fq, ccol, pack, smid, vbar, inv_o, turn_o, st_o, keep_o, send_o):
    chunk = ccol.shape[1] // 2
    zcols = pack[pack.shape[0] - 1].astype(F32)
    states = unpack_states(pack, b, zcols)
    lane = lanes_of((chunk, 128))
    cend = ccol[0, chunk - 1 : chunk]
    pairs = pairs_of(chunk)
    near = []
    for h in range(4):
        near.append(low(states[h]))
        near.append(low(jnp.exp(cend[:, h : h + 1]) * states[h] + smid[0, h]))
        for j in range(2):
            st_o[0, h, j] = near[2 * h + j]
    inter = [mm(fq[0, h, rows], near[2 * h + j]) for j, h, rows in pairs]
    outs = [
        o_loc[0, h, rows] + jnp.exp(ccol[0, rows, h : h + 1]) * part for part, (j, h, rows) in zip(inter, pairs)
    ]
    dens = [jnp.broadcast_to(o[:, 64:65], o.shape) for o in outs]
    invs = [lax.rsqrt(den * den + 1.0) for den in dens]
    att = [[None] * 4, [None] * 4]
    for o, den, inv, (j, h, rows) in zip(outs, dens, invs, pairs):
        mean = mean_of(vbar, h)
        att[j][h] = (o + den * mean) * inv
        inv_o[0, h, rows] = jnp.where(lane < 64, inv, 0.0)
        turn_o[0, h, rows] = mean - den * inv * att[j][h]
    first = pos[3] == 0
    for p in range(2):
        both = [
            jnp.where(lane < 64, att[j][2 * p], swap_halves(att[j][2 * p + 1])) for j in range(2)
        ]
        keep_o[0, :, 128 * p : 128 * p + 128] = jnp.where(first, both[0], both[1]).astype(BF16)
        send_o[0, :, 128 * p : 128 * p + 128] = jnp.where(first, both[1], both[0]).astype(BF16)


def dp_of(pos, mz, mx):
    return (pos[0] ^ mz) * 2 + (pos[1] ^ mx)


def feed_chunks(pos, near, far, cot, cott, feed, feedt, target, up_s, dn_s, hid_s, gp_s, big_s):
    seqs, chunk, _ = cot.shape
    nz = far.shape[0]
    width, both = up_s.shape
    hidden = both // 2
    rows_up = width // (2 * nz)
    for my in range(2):
        cols = slice(my * hidden, (my + 1) * hidden)
        for mx in range(2):
            k = 2 * my + mx
            piece = far if k == 3 else near.at[pl.ds(k * nz, nz)]
            for z in range(nz):
                at = pl.multiple_of((2 * z + (pos[1] ^ mx)) * rows_up, rows_up)
                up_s[pl.ds(at, rows_up), cols] = piece[z, 0:rows_up]
                dn_s[pl.ds(at, rows_up), cols] = piece[z, rows_up : 2 * rows_up]

    def scatter(offset):
        for my in range(2):
            cols = slice(my * hidden, (my + 1) * hidden)
            for mx in range(2):
                for mz in range(nz):
                    at = pl.multiple_of(dp_of(pos, mz, mx) * rows_up, rows_up)
                    target[my, mx, mz, offset : offset + rows_up, :] = big_s[pl.ds(at, rows_up), cols]

    spans = [slice(r * chunk, (r + 1) * chunk) for r in range(seqs)]
    outs, grads = [], []
    pres = [mm(feed[rows], up_s[...]) for rows in spans]
    ghs = [mm(cot[r], dn_s[...]) for r in range(seqs)]
    for r, rows in enumerate(spans):
        cdf, pdf = normal_parts(pres[r])
        hid_s[rows] = low(pres[r] * cdf)
        gp_s[rows] = low(ghs[r] * (cdf + pres[r] * pdf))
    for rows in spans:
        outs.append(mm(hid_s[rows], dn_s[...], NT))
        grads.append(mm(gp_s[rows], up_s[...], NT))
    big_s[...] = low(mm(feedt[...], gp_s[...]))
    scatter(0)
    big_s[...] = low(mm(jnp.concatenate([cott[r] for r in range(seqs)], axis=1), hid_s[...]))
    scatter(rows_up)
    return outs, grads


def feed_first_kernel(
    pos, akeep, arecv, x, cot, cott, vec, near_own, far_own, near, far,
    gsend_o, acc_o, gf_o, mid_o, feed_o, feedt_o, att_o, ow_o,
    up_s, dn_s, hid_s, gp_s, big_s,
):
    seqs, chunk, _ = x.shape
    nz = far.shape[0]
    rows_up = up_s.shape[0] // (2 * nz)
    first = pos[3] == 0
    for mc, (some, rest) in enumerate(((near_own, far_own), (near, far))):
        for my in range(2):
            t = (pos[2] ^ my) * 2 + (pos[3] ^ mc)
            for mx in range(2):
                k = 2 * my + mx
                for z in range(nz):
                    at = pl.multiple_of(((2 * z + (pos[1] ^ mx)) * 4 + t) * 16, 16)
                    source = rest if k == 3 else some.at[pl.ds(k * nz, nz)]
                    ow_o[pl.ds(at, 16), :] = source[z, 2 * rows_up :]
    gain, shift = vec[6:7], vec[7:8]
    for r in range(seqs):
        rows = slice(r * chunk, (r + 1) * chunk)
        mine, theirs = akeep[r], arecv[r]
        att = jnp.concatenate([jnp.where(first, mine, theirs), jnp.where(first, theirs, mine)], axis=1)
        att_o[rows] = att
        mid = x[r].astype(F32) + mm(att, ow_o[...])
        mid_o[rows] = mid
        unit, _ = norm_of(mid)
        feed = unit * gain + shift
        feed_o[rows] = low(feed)
        feedt_o[:, rows] = low(feed.T)
    outs, grads = feed_chunks(pos, near, far, cot, cott, feed_o, feedt_o, gsend_o, up_s, dn_s, hid_s, gp_s, big_s)
    for r, (out, grad) in enumerate(zip(outs, grads)):
        acc_o[r * chunk : (r + 1) * chunk] = out
        gf_o[r * chunk : (r + 1) * chunk] = grad


def feed_second_kernel(
    pos, cot, cott, vec, near, far, acc, gf_in, mid_in, feed, feedt, att, ow,
    out_o, gm_o, gak_o, gas_o, gkeep_o, okeep_o, osend_o, gv_o,
    up_s, dn_s, hid_s, gp_s, gb_s, big_s,
):
    seqs, chunk, width = cot.shape
    nz = far.shape[0]
    first = pos[3] == 0
    outs, grads = feed_chunks(pos, near, far, cot, cott, feed, feedt, gkeep_o, up_s, dn_s, hid_s, gp_s, big_s)
    gain = vec[6:7]
    gain_sum = jnp.zeros((1, width), F32)
    shift_sum = jnp.zeros((1, width), F32)
    for r in range(seqs):
        rows = slice(r * chunk, (r + 1) * chunk)
        mid = mid_in[rows]
        out_o[r] = low(mid + (acc[rows] + outs[r]))
        unit, inv = norm_of(mid)
        gf = gf_in[rows] + grads[r]
        gain_sum += jnp.sum(gf * unit, axis=0, keepdims=True)
        shift_sum += jnp.sum(gf, axis=0, keepdims=True)
        gm = cot[r].astype(F32) + norm_back(gf * gain, unit, inv)
        gm_o[r] = gm
        gb = low(gm)
        gb_s[rows] = gb
        ga = low(mm(gb, ow[...], NT))
        half = width // 2
        gak_o[r] = jnp.where(first, ga[:, :half], ga[:, half:])
        gas_o[r] = jnp.where(first, ga[:, half:], ga[:, :half])
    gv_o[...] = jnp.concatenate([gain_sum, shift_sum, jnp.zeros((6, width), F32)], axis=0)
    big_s[:, 0:width] = low(mm(att[...], gb_s[...], TN))
    for mc, target in ((0, okeep_o), (1, osend_o)):
        for my in range(2):
            t = (pos[2] ^ my) * 2 + (pos[3] ^ mc)
            for mx in range(2):
                for mz in range(nz):
                    at = pl.multiple_of((dp_of(pos, mz, mx) * 4 + t) * 16, 16)
                    target[my, mx, mz] = big_s[pl.ds(at, 16), 0:width]


def adjoint_kernel(b, pos, gak, gar, inv_root, turn, fq, ccol, g_o, scaled_o, l1_o, pack_o):
    chunk = ccol.shape[1] // 2
    lane = lanes_of((chunk, 128))
    first = pos[3] == 0
    pairs = pairs_of(chunk)
    gas = []
    for j in range(2):
        for p in range(2):
            cols = slice(128 * p, 128 * p + 128)
            pair = jnp.where(first == (j == 0), gak[0, :, cols], gar[0, :, cols]).astype(F32)
            gas += [pair, swap_halves(pair)]
    gns = [low(ga * inv_root[0, h, rows]).astype(F32) for ga, (j, h, rows) in zip(gas, pairs)]
    gds = [
        jnp.sum(gn * turn[0, h, rows], axis=1, keepdims=True) for gn, (j, h, rows) in zip(gns, pairs)
    ]
    scaled = []
    for gn, gd, (j, h, rows) in zip(gns, gds, pairs):
        gd = jnp.broadcast_to(gd, gn.shape)
        high = low(gd).astype(F32)
        g = jnp.where(lane == 64, high, jnp.where(lane == 65, gd - high, gn))
        g_o[0, h, rows] = low(g)
        scaled.append(low(g * jnp.exp(ccol[0, rows, h : h + 1])))
        scaled_o[0, h, rows] = scaled[-1]
    parts = [mm(fq[0, h, rows], g, TN) for g, (j, h, rows) in zip(scaled, pairs)]
    states = []
    for h in range(4):
        l1_o[0, h] = parts[4 + h]
        states.append(parts[h] + jnp.exp(ccol[0, chunk - 1 : chunk, h : h + 1]) * parts[4 + h])
    pack_states(states, pack_o, b, pack_o.shape[0] - 1, split=True)


def local_back_kernel(b, fq, fk, va, g, scaled, st, ccol, crow, dfq_o, dfk_o, dva_o):
    chunk = crow.shape[3]
    row, col = lower_tri(chunk)
    pairs = pairs_of(chunk)
    for half in (pairs[:4], pairs[4:]):
        qk = [mm(fq[0, h, rows], fk[0, h, rows], NT) for j, h, rows in half]
        da = [mm(g[0, h, rows], va[0, h, rows], NT) for j, h, rows in half]
        inter = [mm(scaled[0, h, rows], st[0, h, j], NT) for j, h, rows in half]
        attn, dp = [], []
        for q, d, (j, h, rows) in zip(qk, da, half):
            w = weights_of(ccol[0, rows, h : h + 1], crow[0, j, 4 + h : 5 + h], crow[0, j, h : h + 1], row, col)
            attn.append(low(q * w))
            dp.append(low(d * w))
        dva = [mm(a, g[0, h, rows], TN) for a, (j, h, rows) in zip(attn, half)]
        dfk = [mm(d, fq[0, h, rows], TN) for d, (j, h, rows) in zip(dp, half)]
        dfq = [mm(d, fk[0, h, rows]) for d, (j, h, rows) in zip(dp, half)]
        for i, (j, h, rows) in enumerate(half):
            dfq_o[0, h, rows] = dfq[i] + inter[i]
            dfk_o[0, h, rows] = dfk[i]
            dva_o[0, h, rows] = dva[i]


def close_kernel(
    b, pos, units, attend, fq, fk, fqt, fkt, va, dfq, dfk, dva, ccol, ucol, pack, l1, st, wmix, gv, back,
    m00_o, m01_o, m10_o, m11_o, gnk_o, gns_o,
    acc_s, gm_s, gate_s, vsum_s, big_s,
    *, seqs_total,
):
    seqs = seqs_total
    chunk = units.shape[1] // 2
    nz = m00_o.shape[0]
    lane = lanes_of((chunk, 128))
    row, col = lower_tri(chunk)
    upper = jnp.where(row <= col, 1.0, 0.0).astype(BF16)
    zcols = pack[pack.shape[0] - 1].astype(F32)
    arrived = unpack_states(pack, b, zcols, last=64)
    wide = lanes_of((128, 128))

    @pl.when(b == 0)
    def _():
        gate_s[...] = jnp.zeros_like(gate_s)
        vsum_s[...] = jnp.zeros_like(vsum_s)

    pairs = pairs_of(chunk)
    spans = [slice(j * chunk, (j + 1) * chunk) for j in range(2)]
    cums = [ccol[0, rows] for rows in spans]
    freshs = [ucol[0, rows] for rows in spans]
    douts = [jnp.exp(cum[chunk - 1 : chunk] - cum) * fresh for cum, fresh in zip(cums, freshs)]
    nears = []
    for j, h, rows in pairs:
        adj = arrived[h]
        if j == 0:
            adj = l1[0, h] + jnp.exp(ccol[0, 2 * chunk - 1 : 2 * chunk, h : h + 1]) * adj
        zs = adj[:, 64:65] + adj[:, 65:66]
        high = low(zs).astype(F32)
        nears.append(low(jnp.where(wide == 64, high, jnp.where(wide == 65, zs - high, adj))))
    dk_fars = [mm(va[0, h, rows], near, NT) for near, (j, h, rows) in zip(nears, pairs)]
    dv_fars = [mm(fk[0, h, rows], near) for near, (j, h, rows) in zip(nears, pairs)]
    kds, qds, levels = [], [], []
    pqs, pks, dvs = [], [], []
    for i, (j, h, rows) in enumerate(pairs):
        d = douts[j][:, h : h + 1]
        keys, queries = fk[0, h, rows].astype(F32), fq[0, h, rows].astype(F32)
        dk_far = d * dk_fars[i]
        dk = dk_far + dfk[0, h, rows]
        dq = dfq[0, h, rows]
        kds.append(jnp.sum(keys * dk, axis=1, keepdims=True))
        qds.append(jnp.sum(queries * dq, axis=1, keepdims=True))
        passed = st[0, h, j].astype(F32) * nears[i].astype(F32)
        passed = jnp.sum(jnp.sum(passed, axis=0, keepdims=True), axis=1, keepdims=True)
        total = jnp.sum(jnp.sum(keys * dk_far, axis=0, keepdims=True), axis=1, keepdims=True)
        levels.append(total + jnp.exp(cums[j][chunk - 1 : chunk, h : h + 1]) * passed)
        dvs.append(dva[0, h, rows] + d * dv_fars[i])
        pks.append(low(dk * fkt[0, h, rows].astype(F32)))
        pqs.append(low(dq * fqt[0, h, rows].astype(F32)))
    grads = [
        [mm(jnp.concatenate(ps[4 * j + 2 * p : 4 * j + 2 * p + 2], axis=1), back[p]) for ps in (pqs, pks) for p in range(2)]
        for j in range(2)
    ]
    bias_sum = jnp.zeros((1, 128), F32)
    gms = []
    for j in range(2):
        kd = qd = jnp.zeros((chunk, 128), F32)
        level = jnp.zeros((1, 128), F32)
        for h in range(4):
            kd = jnp.where(lane == h, kds[4 * j + h], kd)
            qd = jnp.where(lane == h, qds[4 * j + h], qd)
            level = jnp.where(lanes_of((1, 128)) == h, levels[4 * j + h], level)
        dlog = tri_sum(upper, qd - kd) + level
        dlogit = jnp.where(lane < 4, freshs[j] * dlog - (1.0 - freshs[j]) * kd, 0.0)
        bias_sum += jnp.sum(dlogit, axis=0, keepdims=True)
        values = [jnp.where(lane < 64, dvs[4 * j + 2 * p], swap_halves(dvs[4 * j + 2 * p + 1])) for p in range(2)]
        gm = jnp.concatenate([low(x) for x in (*grads[j], *values, dlogit)], axis=1)
        gm_s[pl.ds(pl.multiple_of((2 * b + j) * chunk, chunk), chunk), :] = gm
        gms.append(gm)
    normed = [mm(gm, wmix[...], NT) for gm in gms]
    vsum_s[0:1] += sum(jnp.sum(n * units[0, rows], axis=0, keepdims=True) for n, rows in zip(normed, spans))
    vsum_s[1:2] += sum(jnp.sum(n, axis=0, keepdims=True) for n in normed)
    first = pos[3] == 0
    gnk_o[0] = jnp.where(first, normed[0], normed[1])
    gns_o[0] = low(jnp.where(first, normed[1], normed[0]))
    gate_s[0:1] += bias_sum

    @pl.when(b == seqs - 1)
    def _():
        width = acc_s.shape[0]
        acc_s[...] = mm(attend[...].reshape(gm_s.shape[0], width), gm_s[...], TN)
        table = jnp.concatenate(
            [jnp.zeros((4, width), F32), vsum_s[0:2], gv[0:2], jnp.zeros((120, width), F32)], axis=0
        ).T
        total = gate_s[0:1]
        high = low(total).astype(F32)
        rest = jnp.broadcast_to(total - high, (8, 128))
        both = pltpu.roll(jnp.broadcast_to(high, (8, 128)), 8, 1) + pltpu.roll(rest, 12, 1)
        biases = jnp.broadcast_to(both[0:1], (width, 128))
        side = jnp.where(lanes_of((width, 128)) < 4, acc_s[:, 768:896], table) + biases
        big_s[:, 0:768] = acc_s[:, 0:768].astype(BF16)
        big_s[:, 768:896] = side.astype(BF16)
        for my in range(2):
            for mx in range(2):
                for mz in range(nz):
                    at = pl.multiple_of(chip_row(pos, mz, mx, my), 32)
                    (m00_o, m01_o, m10_o, m11_o)[2 * my + mx][mz] = big_s[pl.ds(at, 32), :]


def final_kernel(pos, keep, recv, mix_o, gate_o, bias_o, *vec_o):
    first = pos[3] == 0
    mine, theirs = keep[...], recv[...]
    halves = (jnp.where(first, mine, theirs), jnp.where(first, theirs, mine))
    width = mix_o.shape[1] // 6
    for i in range(3):
        for s in range(2):
            mix_o[:, (2 * i + s) * width : (2 * i + s + 1) * width] = halves[s][:, i * width : (i + 1) * width]
    sides = [half[:, 3 * width :] for half in halves]
    lane = lanes_of(sides[0].shape)
    both = jnp.concatenate([sides[0] + sides[1], sides[0], sides[1], jnp.zeros((80, 128), F32)], axis=0).T
    gate_o[0:4] = both[0:4, 16:32]
    gate_o[4:8] = both[0:4, 32:48]
    for i, out in enumerate(vec_o):
        out[...] = both[4 + i, 0:16]
    sums = [side[0:8] + pltpu.roll(side[0:8], 124, 1) for side in sides]
    row = jnp.where(lane[0:8] < 4, pltpu.roll(sums[0], 120, 1), pltpu.roll(sums[1], 124, 1))
    bias_o[...] = row[0, 0:8]


def input_kernel(b, x, gm, keep, recv, vec, o, done_o):
    done_o[...] = jnp.zeros_like(done_o)
    unit, inv = norm_of(x[0].astype(F32))
    grad = keep[0] + recv[0].astype(F32)
    o[0] = gm[0] + norm_back(grad * vec[4:5], unit, inv)


def hold_kernel(*refs):
    sems = refs[-1]
    count = (len(refs) - 1) // 2
    copies = [
        pltpu.make_async_copy(refs[i], refs[count + i], sems.at[i]) for i in range(count)
    ]
    for copy in copies:
        copy.start()
    for copy in copies:
        copy.wait()


def halves_kernel(by_x, by_y, x_half, y_half, sems):
    half = x_half.shape[0]
    copies = [
        pltpu.make_async_copy(by_x.at[pl.ds(0, half)], x_half, sems.at[0]),
        pltpu.make_async_copy(by_y.at[pl.ds(half, half)], y_half, sems.at[1]),
    ]
    for copy in copies:
        copy.start()
    for copy in copies:
        copy.wait()


def gather_kernel(*refs):
    parts, out, sems = refs[:-2], refs[-2], refs[-1]
    copies, at = [], 0
    for i, part in enumerate(parts):
        copies.append(pltpu.make_async_copy(part, out.at[pl.ds(at, part.shape[0])], sems.at[i]))
        at += part.shape[0]
    for copy in copies:
        copy.start()
    for copy in copies:
        copy.wait()


def pause_kernel(out):
    out[...] = jnp.zeros_like(out)


def join_kernel(pos, *refs, axis):
    parts, out, sems = refs[:-2], refs[-2], refs[-1]
    copies = [
        pltpu.make_async_copy(part, out.at[pos[axis] ^ i], sems.at[i]) for i, part in enumerate(parts)
    ]
    for copy in copies:
        copy.start()
    for copy in copies:
        copy.wait()


def pair_sum_kernel(keep, recv, okeep, orecv, x_keep, x_send, y_keep, y_send):
    half = x_keep.shape[1]
    rows = keep.shape[3]
    first, second = slice(0, half), slice(half, 2 * half)
    for i in range(2):
        for my, mx, zs, out in ((i, 0, first, x_keep), (i, 1, first, x_send), (0, i, second, y_keep), (1, i, second, y_send)):
            out[i, :, 0:rows] = low(keep[my, mx, zs].astype(F32) + recv[my, mx, zs].astype(F32))
            out[i, :, rows:] = low(okeep[my, mx, zs].astype(F32) + orecv[my, mx, zs].astype(F32))


def half_sum_kernel(x_keep, x_recv, y_keep, y_recv, x_own, x_far, y_own, y_far):
    for keep, recv, own, far in ((x_keep, x_recv, x_own, x_far), (y_keep, y_recv, y_own, y_far)):
        for i, out in ((0, own), (1, far)):
            out[...] = low(keep[i].astype(F32) + recv[i].astype(F32))


def line_sum_kernel(x_own, x_recv, y_own, y_recv, *outs):
    half = x_own.shape[0]
    for i in range(half):
        outs[i][...] = low(x_own[i].astype(F32) + x_recv[i].astype(F32))
        outs[half + i][...] = low(y_own[i].astype(F32) + y_recv[i].astype(F32))


def sum_of_four(refs):
    a, b, c, d = (ref[...].astype(F32) for ref in refs)
    return (a + b) + (c + d)


def mix_sum_kernel(m0, m1, m2, m3, *outs):
    total = sum_of_four((m0, m1, m2, m3))
    side = total[..., 768:896]
    rest = side - low(side).astype(F32)
    lane = lanes_of(side.shape)
    moved = jnp.where((lane >= 12) & (lane < 16), side + pltpu.roll(rest, 4, side.ndim - 1), side)
    for i, out in enumerate(outs):
        out[:, 0:768] = low(total[i, :, 0:768])
        out[:, 768:896] = low(moved[i])


def feed_last_kernel(a, b, c, d, up_o, down_o, out_o, done_o):
    done_o[...] = jnp.zeros_like(done_o)
    total = sum_of_four((a, b, c, d))
    rows = up_o.shape[0]
    up_o[...] = total[0:rows]
    down_o[...] = total[rows : 2 * rows]
    out_o[...] = total[2 * rows :]


def mix_last_kernel(pos, a, b, c, d, keep_o, send_o):
    total = sum_of_four((a, b, c, d))
    rows = keep_o.shape[0]
    first = pos[3] == 0
    keep_o[...] = jnp.where(first, total[:rows], total[rows:])
    send_o[...] = jnp.where(first, total[rows:], total[:rows])


def call(kernel, steps, ins, outs, scratch=(), us=1.0, name=None, limit=12, unroll=True):
    def spec(kind):
        if kind in "da":
            return pl.BlockSpec(memory_space=pl.ANY)
        return pl.BlockSpec(memory_space=pltpu.SMEM if kind == "m" else pltpu.VMEM)

    kinds = [kind for kind, _ in ins]
    out_kinds = [kind for kind, _, _ in outs]
    all_kinds = kinds + out_kinds + ["w"] * len(scratch)

    def run(*refs):
        used = [(kind, ref) for kind, ref in zip(all_kinds, refs) if kind != "d"]
        if not steps:
            kernel(*[ref for _, ref in used])
            return

        def one(b, carry):
            kernel(b, *[ref.at[pl.ds(b, 1)] if kind == "s" else ref for kind, ref in used])
            return carry

        lax.fori_loop(0, steps, one, 0, unroll=unroll)

    return pl.pallas_call(
        run,
        in_specs=[spec(kind) for kind in kinds],
        out_specs=[spec(kind) for kind in out_kinds],
        out_shape=[jax.ShapeDtypeStruct(shape, dtype) for _, shape, dtype in outs],
        scratch_shapes=list(scratch),
        compiler_params=pltpu.CompilerParams(vmem_limit_bytes=limit * 1024 * 1024),
        cost_estimate=pl.CostEstimate(flops=int(us * 1.15e9), bytes_accessed=0, transcendentals=0),
        name=name,
    )(*[a for _, a in ins])


def xor_with(a, mask, count):
    return lax.ppermute(a, BOTH, [(i, i ^ mask) for i in range(count)])


def body(
    inputs, cotangent, mix_weight, gate_weight, gate_bias, out_weight, gain_first, shift_first, gain_second,
    shift_second, up_weight, down_weight, random_maps,
):
    dp, tensor = lax.axis_size("dp"), lax.axis_size("tensor")
    count = dp * tensor
    place_dp, place_t = lax.axis_index("dp"), lax.axis_index("tensor")
    seqs, chunk, width = inputs.shape
    heads, head = random_maps.shape[0], random_maps.shape[1]
    hidden = up_weight.shape[1]
    core = place_t % 2
    first = core == 0
    direct = dp == 8
    nz = 4
    if direct:
        pos = jnp.stack([place_dp // 2, place_dp % 2, place_t // 2, core]).astype(jnp.int32)
    else:
        pos = jnp.stack([jnp.zeros_like(core)] * 3 + [core]).astype(jnp.int32)
    swap_core = functools.partial(xor_with, mask=1, count=count)

    def mix_pack(mix_w, gate_w, vecs):
        rows = mix_w.shape[0]
        split = mix_w.reshape(rows, 3, 2, width // 2)
        sides = [v[:, None] for v in vecs]
        pad = jnp.zeros((rows, 120), BF16)
        return [
            jnp.concatenate(
                [split[:, 0, s], split[:, 1, s], split[:, 2, s], gate_w[:, 4 * s : 4 * s + 4]] + sides + [pad], axis=1
            )
            for s in range(2)
        ]

    def join(parts, axis, after=()):
        (out,) = call(
            functools.partial(join_kernel, axis=axis), 0, [("m", pos)] + [("a", a) for a in parts] + [("d", a) for a in after],
            [("w", (len(parts), *parts[0].shape), parts[0].dtype)],
            scratch=[pltpu.SemaphoreType.DMA((len(parts),))], name="join",
        )
        return out

    def pause(after, us):
        (out,) = call(
            pause_kernel, 0, [("d", a) for a in after], [("w", (8, 128), F32)], us=us, name="pause",
        )
        return out

    def from_plane(pieces):
        return [pieces[0], xor_with(pieces[1], 4, count), xor_with(pieces[2], 2, count), xor_with(pieces[3], 6, count)]

    other_in = swap_core(inputs)
    vectors = (gain_first, shift_first, gain_second, shift_second)
    long = 2 * chunk
    unit, cot_t = call(
        prepare_kernel, seqs, [("m", pos), ("s", inputs), ("s", other_in), ("s", cotangent)],
        [("s", (seqs, long, width), F32), ("s", (seqs, width, chunk), BF16)], us=2.5, name="prepare",
    )
    if direct:
        rows = mix_weight.shape[0]
        columns = jnp.pad(gate_weight.T, ((0, 16 - heads), (0, 0)))
        place = lax.broadcasted_iota(jnp.int32, columns.shape, 0)
        for i, v in enumerate(vectors):
            columns = jnp.where(place == heads + i, lax.broadcast_in_dim(v, columns.shape, (1,)), columns)
        keep, send = call(
            pack_kernel, 0, [("m", pos), ("w", mix_weight), ("w", columns)], [("w", (rows, 896), BF16)] * 2, name="pack",
        )
        pair = join([keep, swap_core(send)], 3)
        line = join([pair] + [xor_with(pair, 8 * m, count) for m in range(1, nz)], 0, after=[unit])
        w_pieces = [line] + [xor_with(line, m, count) for m in (4, 2, 6)]
        block = jnp.concatenate([up_weight, down_weight.T, out_weight], axis=0)
        (block,) = call(
            hold_kernel, 0, [("a", block), ("d", unit)],
            [("w", block.shape, BF16)], scratch=[pltpu.SemaphoreType.DMA((1,))], name="hold",
        )
        ff_line = join([block] + [xor_with(block, 8 * m, count) for m in range(1, nz)], 0, after=[line])
        by_x, by_y = xor_with(ff_line, 4, count), xor_with(ff_line, 2, count)
    else:
        whole = [
            lax.all_gather(a, BOTH, axis=0, tiled=True) for a in (mix_weight, gate_weight, out_weight) + vectors
        ]
        p0, p1 = mix_pack(whole[0], whole[1], whole[3:])
        blocks = jnp.where(first, p0, p1).reshape(nz, 2, 2, 2, 16, 896)
        w_pieces = [blocks[:, mx, my] for my, mx in ((0, 0), (0, 1), (1, 0), (1, 1))]
        up_all = lax.all_gather(up_weight, BOTH, axis=0, tiled=False).reshape(dp, tensor, -1, hidden)
        dn_all = lax.all_gather(down_weight.T, BOTH, axis=0, tiled=False).reshape(dp, tensor, -1, hidden)
        up_all = jnp.moveaxis(up_all, 1, 0).reshape(2, 2, nz, 2, -1, hidden)
        dn_all = jnp.moveaxis(dn_all, 1, 0).reshape(2, 2, nz, 2, -1, hidden)
        out_all = whole[2].reshape(nz, 2, 2, 2, 16, width).transpose(2, 3, 0, 1, 4, 5)
        ff_all = jnp.concatenate([up_all, dn_all, out_all], axis=4)
        ff_all = jnp.where(first, ff_all, ff_all[:, ::-1])
        ff_own, ff_other = (
            jnp.concatenate([ff_all[my, mc, :, mx] for my in range(2) for mx in range(2)]) for mc in range(2)
        )

    maps = lax.dynamic_slice_in_dim(random_maps, core * 4, 4, 0)
    zero = jnp.zeros((head, head), BF16)
    maps_pair = jnp.stack(
        [
            jnp.concatenate(
                [jnp.concatenate([maps[2 * p], zero], 1), jnp.concatenate([zero, maps[2 * p + 1]], 1)], 0
            )
            for p in range(2)
        ]
    )
    flip = jnp.swapaxes(maps, 1, 2)
    maps_back = jnp.stack(
        [
            jnp.concatenate(
                [
                    jnp.concatenate([flip[2 * p], zero], 1),
                    jnp.concatenate([-flip[2 * p], zero], 1),
                    jnp.concatenate([zero, flip[2 * p + 1]], 1),
                    jnp.concatenate([zero, -flip[2 * p + 1]], 1),
                ],
                0,
            )
            for p in range(2)
        ]
    )
    bias = jnp.pad(lax.dynamic_slice_in_dim(gate_bias, core * 4, 4, 0), (0, 124))[None]

    tokens = seqs * long
    feats = (seqs, 4, long, 128)
    npack = 2 * seqs + 1
    attend, fk, fkl, fkt, va, ccol, ucol, crow, smid, pack, wmix, vec, vbar = call(
        project_kernel, seqs,
        [("m", pos), ("s", unit)] + [("a", w) for w in w_pieces] + [("w", bias), ("w", maps_pair)],
        [
            ("s", (seqs, long, width), BF16), ("s", feats, BF16), ("s", feats, BF16), ("s", feats, BF16), ("s", feats, BF16),
            ("s", (seqs, long, 128), F32), ("s", (seqs, long, 128), F32),
            ("s", (seqs, 2, 8, chunk), F32),
            ("s", (seqs, 4, 128, 128), F32),
            ("w", (npack, 128, 128), BF16), ("w", (width, 896), BF16), ("w", (8, width), F32),
            ("w", (8, width // 2), F32),
        ],
        scratch=[pltpu.VMEM((nz, 2, 2, 2, 16, 896), BF16), pltpu.SemaphoreType.DMA((4,))], us=12, name="project",
    )
    ahead = [(i, i + 2) for i in range(count) if (i % tensor) < 2]
    arrived = lax.ppermute(pack, BOTH, ahead)
    fq, fql, fqt = call(
        query_kernel, seqs, [("s", attend), ("w", wmix), ("w", maps_pair)], [("s", feats, BF16)] * 3, us=0.3, name="query",
    )
    (o_loc,) = call(
        local_kernel, seqs,
        [("s", fq), ("s", fk), ("s", fql), ("s", fkl), ("s", va), ("s", ccol), ("s", crow)],
        [("s", feats, F32)], us=0.3, name="local",
    )
    if direct:
        half_z = nz // 2
        far_shape = (half_z, *ff_line.shape[1:])
        x_half, y_half = call(
            halves_kernel, 0, [("a", by_x), ("a", by_y), ("d", arrived), ("d", o_loc)], [("w", far_shape, BF16)] * 2,
            scratch=[pltpu.SemaphoreType.DMA((2,))], us=0.3, name="halves",
        )
        near_parts = [ff_line, by_x, by_y]
        (ff_near,) = call(
            gather_kernel, 0, [("a", a) for a in near_parts] + [("d", x_half)],
            [("w", (3 * nz, *ff_line.shape[1:]), BF16)], scratch=[pltpu.SemaphoreType.DMA((3,))], us=0.5, name="near",
        )
        before_finish = [x_half]
    else:
        before_finish = []
    (inv_root, turn, st, att_keep, att_send) = call(
        finish_kernel, seqs,
        [("m", pos), ("s", o_loc), ("s", fq), ("s", ccol), ("w", arrived), ("s", smid), ("w", vbar)]
        + [("d", a) for a in before_finish],
        [
            ("s", feats, F32), ("s", feats, F32), ("s", (seqs, 4, 2, 128, 128), BF16),
            ("s", (seqs, chunk, width // 2), BF16), ("s", (seqs, chunk, width // 2), BF16),
        ],
        us=0.3, name="finish",
    )
    att_recv = swap_core(att_send)
    if direct:
        near_other = swap_core(ff_near)
        far_parts = [xor_with(x_half, 2, count), xor_with(y_half, 4, count)]
        (ff_far,) = call(
            gather_kernel, 0, [("a", a) for a in far_parts] + [("d", att_keep)],
            [("w", ff_line.shape, BF16)], scratch=[pltpu.SemaphoreType.DMA((2,))], name="gather",
        )
        far_other = swap_core(ff_far)
    else:
        ff_near, ff_far, near_other, far_other = ff_own[: 3 * nz], ff_own[3 * nz :], ff_other[: 3 * nz], ff_other[3 * nz :]

    own = seqs * chunk
    nrows = ff_near.shape[1]
    payload, out_payload = (2, 2, nz, nrows - 16, hidden), (2, 2, nz, 16, hidden)
    rows_low, rows_full = ("w", (own, width), BF16), ("w", (own, width), F32)
    work = [
        pltpu.VMEM((width, 2 * hidden), BF16), pltpu.VMEM((width, 2 * hidden), BF16),
        pltpu.VMEM((own, 2 * hidden), BF16), pltpu.VMEM((own, 2 * hidden), BF16),
    ]
    big = pltpu.VMEM((width, 2 * hidden), BF16)
    g_send, *fed = call(
        feed_first_kernel, 0,
        [("m", pos)] + [
            ("w", a) for a in (
                att_keep, att_recv, inputs, cotangent, cot_t, vec, ff_near, ff_far, near_other, far_other
            )
        ],
        [
            ("w", payload, BF16), rows_full, rows_full, rows_full, rows_low, ("w", (width, own), BF16), rows_low,
            ("w", (width, width), BF16),
        ],
        scratch=[*work, big], us=10, name="feed_first", limit=18,
    )
    g_recv = swap_core(g_send)
    output, grad_middle, ga_keep, ga_send, g_keep, o_keep, o_send, grad_vec = call(
        feed_second_kernel, 0,
        [("m", pos)] + [("w", a) for a in (cotangent, cot_t, vec, ff_near, ff_far, *fed)],
        [
            ("w", (seqs, chunk, width), BF16), ("w", (seqs, chunk, width), F32),
            ("w", (seqs, chunk, width // 2), BF16), ("w", (seqs, chunk, width // 2), BF16),
            ("w", payload, BF16), ("w", out_payload, BF16), ("w", out_payload, BF16), ("w", (8, width), F32),
        ],
        scratch=[
            *work, pltpu.VMEM((own, width), BF16), big,
        ],
        us=10, name="feed_second", limit=18,
    )
    ga_recv = swap_core(ga_send)

    if direct:
        o_recv = swap_core(o_send)
        half_z = nz // 2
        two, one = (2, half_z, nrows, hidden), (half_z, nrows, hidden)
        x_keep, x_send, y_keep, y_send = call(
            pair_sum_kernel, 0, [("w", g_keep), ("w", g_recv), ("w", o_keep), ("w", o_recv)], [("w", two, BF16)] * 4,
            us=0.6, name="pair_sum",
        )
        x_recv, y_recv = xor_with(x_send, 4, count), xor_with(y_send, 2, count)
        before_adjoint = [x_keep]
    else:
        before_adjoint = []
        g_keep, g_send = (jnp.concatenate(parts, axis=3) for parts in ((g_keep, o_keep), (g_send, o_send)))
        by_core = jnp.where(first, jnp.stack([g_keep, g_send]), jnp.stack([g_send, g_keep]))
        by_rows = by_core.transpose(3, 2, 1, 0, 4, 5)
        rows_up = (nrows - 16) // 2
        ups = by_rows[..., :rows_up, :].reshape(nz * 2, 4, rows_up, hidden).transpose(1, 0, 2, 3)
        dns = by_rows[..., rows_up : 2 * rows_up, :].reshape(nz * 2, 4, rows_up, hidden).transpose(1, 0, 2, 3)
        ups = ups.reshape(4, dp, -1, hidden).transpose(1, 0, 2, 3)
        dns = dns.reshape(4, dp, -1, hidden).transpose(1, 0, 2, 3)
        outs = by_rows[..., 2 * rows_up :, :].reshape(width, width)

        def reduced(a):
            return lax.psum_scatter(a.astype(F32).reshape(count, -1, a.shape[-1]), BOTH, scatter_dimension=0)

        up_grad, down_grad, out_grad = reduced(ups), reduced(dns).T, reduced(outs)

    g, scaled, l1, pack_b = call(
        adjoint_kernel, seqs,
        [("m", pos), ("s", ga_keep), ("s", ga_recv), ("s", inv_root), ("s", turn), ("s", fq), ("s", ccol)]
        + [("d", a) for a in before_adjoint],
        [
            ("s", feats, BF16), ("s", feats, BF16), ("s", (seqs, 4, 128, 128), F32), ("w", (npack, 128, 128), BF16),
        ],
        us=0.3, name="adjoint",
    )
    behind = [(i, i - 2) for i in range(count) if (i % tensor) >= 2]
    arrived_b = lax.ppermute(pack_b, BOTH, behind)
    dfq, dfk, dva = call(
        local_back_kernel, seqs,
        [("s", fq), ("s", fk), ("s", va), ("s", g), ("s", scaled), ("s", st), ("s", ccol), ("s", crow)],
        [("s", feats, F32), ("s", feats, F32), ("s", feats, F32)],
        us=0.3, name="local_back",
    )
    before_close = []
    if direct:
        x_own, x_far, y_own, y_far = call(
            half_sum_kernel, 0, [("w", a) for a in (x_keep, x_recv, y_keep, y_recv)] + [("d", dfq)],
            [("w", one, BF16)] * 4, us=0.4, name="half_sum",
        )
        x_recv, y_recv = xor_with(x_far, 2, count), xor_with(y_far, 4, count)
        before_close = [x_own]
    *m_pieces, gn_keep, gn_send = call(
        functools.partial(close_kernel, seqs_total=seqs), seqs,
        [("m", pos), ("s", unit), ("w", attend), ("s", fq), ("s", fk), ("s", fqt), ("s", fkt), ("s", va), ("s", dfq),
         ("s", dfk), ("s", dva), ("s", ccol), ("s", ucol), ("w", arrived_b), ("s", l1), ("s", st),
         ("w", wmix), ("w", grad_vec), ("w", maps_back)] + [("d", a) for a in before_close],
        [*[("w", (nz, 32, 896), BF16)] * 4, ("s", (seqs, chunk, width), F32), ("s", (seqs, chunk, width), BF16)],
        scratch=[
            pltpu.VMEM((width, 896), F32), pltpu.VMEM((tokens, 896), BF16), pltpu.VMEM((8, 128), F32),
            pltpu.VMEM((8, width), F32), pltpu.VMEM((width, 896), BF16),
        ],
        us=14.7, name="close", unroll=False,
    )
    if direct:
        g_line = call(
            line_sum_kernel, 0, [("w", a) for a in (x_own, x_recv, y_own, y_recv)] + [("d", gn_keep)],
            [("w", (nrows, hidden), BF16)] * nz, us=0.4, name="line_sum",
        )
        m_parts = from_plane(m_pieces)
    gn_recv = swap_core(gn_send)
    def finish_input(after):
        return call(
            input_kernel, seqs,
            [("s", inputs), ("s", grad_middle), ("s", gn_keep), ("s", gn_recv), ("w", vec)] + [("d", a) for a in after],
            [("s", (seqs, chunk, width), F32), ("w", (8, 128), F32)], us=0.3, name="input_grad",
        )

    if direct:
        m_plane = call(
            mix_sum_kernel, 0, [("w", a) for a in m_parts] + [("d", pause([g_line[0]], 40)), ("d", gn_recv)],
            [("w", (32, 896), BF16)] * nz, us=0.4, name="mix_sum",
        )
        input_grad, input_done = finish_input([m_plane[0]])
        g_parts = [g_line[0]] + [xor_with(g_line[m], 8 * m, count) for m in range(1, nz)]
        up_grad, down_back, out_grad, feed_done = call(
            feed_last_kernel, 0, [("w", a) for a in g_parts],
            [("w", shape, F32) for shape in (up_weight.shape, down_weight.shape[::-1], out_weight.shape, (8, 128))],
            us=0.3, name="feed_last",
        )
        down_grad = down_back.T
        mix_parts = [m_plane[0]] + [xor_with(m_plane[m], 8 * m, count) for m in range(1, nz)]
        m_keep, m_send = call(
            mix_last_kernel, 0, [("m", pos)] + [("w", a) for a in mix_parts] + [("d", feed_done), ("d", input_done)],
            [("w", (mix_weight.shape[0], 896), F32)] * 2, name="mix_last",
        )
        m_recv = swap_core(m_send)
    else:
        input_grad, input_done = finish_input([])
        m_all = jnp.stack(m_pieces).astype(F32).reshape(2, 2, nz, 32, 896)
        mine_rows = m_all.transpose(2, 1, 0, 3, 4).reshape(count, -1, 896)
        keep_part = lax.psum_scatter(mine_rows * jnp.where(first, 1.0, 0.0), BOTH, scatter_dimension=0)
        far_part = lax.psum_scatter(mine_rows * jnp.where(first, 0.0, 1.0), BOTH, scatter_dimension=0)
        m_keep = jnp.where(first, keep_part, far_part)
        m_recv = jnp.where(first, far_part, keep_part)
    if direct:
        mix_grad, gate_back, bias_grad, *per_row = call(
            final_kernel, 0, [("m", pos), ("w", m_keep), ("w", m_recv)],
            [("w", mix_weight.shape, F32), ("w", gate_weight.shape[::-1], F32), ("w", (heads,), F32)]
            + [("w", gain_first.shape, F32)] * 4,
            us=1.2, name="final",
        )
        gate_grad = gate_back.T
    else:
        m_low = jnp.where(first, m_keep, m_recv)
        m_high = jnp.where(first, m_recv, m_keep)
        mix_grad = jnp.concatenate(
            [part[:, 256 * i : 256 * i + 256] for i in range(3) for part in (m_low, m_high)], axis=1
        )
        gate_grad = jnp.concatenate([m_low[:, 768:772], m_high[:, 768:772]], axis=1)
        bias_grad = jnp.concatenate([m[0, 776:780] + m[0, 780:784] for m in (m_low, m_high)])
        per_row = [m_keep[:, 772 + i] + m_recv[:, 772 + i] for i in range(4)]
    return (
        output, input_grad, mix_grad, gate_grad, bias_grad, out_grad,
        *per_row, up_grad, down_grad,
    )


def solution(mesh):
    rows, spread = P(("dp", "tensor"), None), P(("dp", "tensor"))
    tokens = P("dp", "tensor", None)
    in_specs = (
        tokens, tokens, rows, rows, P(), rows, spread, spread, spread, spread, P("dp", "tensor"), P("tensor", "dp"), P(),
    )
    out_specs = (
        tokens, tokens, rows, rows, P(), rows, spread, spread, spread, spread, P("dp", "tensor"), P("tensor", "dp"),
    )
    return jax.shard_map(body, mesh=mesh, in_specs=in_specs, out_specs=out_specs, check_vma=False)
```

```python
import functools

import jax
import jax.numpy as jnp
from jax import lax
from jax.experimental import pallas as pl
from jax.experimental.pallas import tpu as pltpu
from jax.sharding import PartitionSpec as P

BOTH = ("dp", "tensor")
F32 = jnp.float32
BF16 = jnp.bfloat16
EPSILON = 1e-05
DENSITY = 0.3989422804014327
SIN = (9.9999999998e-01, -1.6666666617e-01, 8.3333309689e-03, -1.9840860382e-04, 2.7525224003e-06, -2.3888330913e-08)
COS = (9.9999999978e-01, -4.9999999354e-01, 4.1666636104e-02, -1.3888359409e-03, 2.4760057595e-05, -2.6049626765e-07)

NN = (((1,), (0,)), ((), ()))
NT = (((1,), (1,)), ((), ()))
TN = (((0,), (0,)), ((), ()))


def mm(a, b, dims=NN):
    return lax.dot_general(a, b, dims, preferred_element_type=F32)


def low(a):
    return a.astype(BF16)


def lanes_of(shape):
    return lax.broadcasted_iota(jnp.int32, shape, len(shape) - 1)


def swap_halves(a):
    return pltpu.roll(a, 64, 1)


def sincos(a):
    turns = jnp.floor(a * 0.3183098861837907 + 0.5)
    r = (a - turns * 3.140625) - turns * 9.676535897932e-4
    half = turns * 0.5
    sign = 1.0 - 4.0 * (half - jnp.floor(half))
    r2 = r * r
    s = r * (SIN[0] + r2 * (SIN[1] + r2 * (SIN[2] + r2 * (SIN[3] + r2 * (SIN[4] + r2 * SIN[5])))))
    c = COS[0] + r2 * (COS[1] + r2 * (COS[2] + r2 * (COS[3] + r2 * (COS[4] + r2 * COS[5]))))
    return sign * s, sign * c


def normal_parts(v):
    t = pl.reciprocal(1.0 + 0.23164189 * jnp.abs(v), approx=True)
    bell = jnp.exp(-0.5 * (v * v))
    poly = t * (0.127414796 + t * (-0.142248368 + t * (0.7107068705 + t * (-0.7265760135 + t * 0.5307027145))))
    tail = poly * bell
    return jnp.where(v >= 0.0, 1.0 - tail, tail), DENSITY * bell


def three_parts(a):
    high = a.astype(BF16)
    rest = a - high.astype(F32)
    mid = rest.astype(BF16)
    return high, mid, (rest - mid.astype(F32)).astype(BF16)


def tri_sum(tri, a):
    high, mid, rest = (part.astype(F32) for part in three_parts(a))
    packed = mm(tri, low(high + pltpu.roll(mid, 4, 1) + pltpu.roll(rest, 8, 1)))
    return packed + pltpu.roll(packed, 124, 1) + pltpu.roll(packed, 120, 1)


def norm_of(x):
    mean = jnp.mean(x, axis=-1, keepdims=True)
    centered = x - mean
    inv = lax.rsqrt(jnp.mean(centered * centered, axis=-1, keepdims=True) + EPSILON)
    return centered * inv, inv


def norm_back(s, unit, inv):
    return inv * (
        s
        - jnp.mean(s, axis=-1, keepdims=True)
        - unit * jnp.mean(s * unit, axis=-1, keepdims=True)
    )


def chip_row(pos, mz, mx, my):
    return (((pos[0] ^ mz) * 2 + (pos[1] ^ mx)) * 2 + (pos[2] ^ my)) * 32


def lower_tri(n):
    row = lax.broadcasted_iota(jnp.int32, (n, n), 0)
    col = lax.broadcasted_iota(jnp.int32, (n, n), 1)
    return row, col


def unpack_states(pack, b, zcols, last=65):
    lane = lanes_of((128, 128))
    out = []
    for p in range(2):
        both = pack[2 * b + p].astype(F32)
        for h, mat in ((2 * p, both), (2 * p + 1, swap_halves(both))):
            z = jnp.sum(jnp.where(lane == 4 * b + h, zcols, 0.0), axis=1, keepdims=True)
            out.append(jnp.where(lane < 64, mat, jnp.where(lane <= last, z, 0.0)))
    return out


def pack_states(states, pack_o, b, last, split=False):
    lane = lanes_of((128, 128))
    zcols = jnp.where(b == 0, 0.0, pack_o[last].astype(F32))

    def sum_of(s):
        return s[:, 64:65] + s[:, 65:66] if split else s[:, 64:65]

    for p in range(2):
        s0, s1 = states[2 * p], states[2 * p + 1]
        pack_o[2 * b + p] = jnp.where(lane < 64, s0, swap_halves(s1)).astype(BF16)
        zcols = jnp.where(lane == 4 * b + 2 * p, sum_of(s0), zcols)
        zcols = jnp.where(lane == 4 * b + 2 * p + 1, sum_of(s1), zcols)
    pack_o[last] = zcols.astype(BF16)


def pack_kernel(pos, mix, columns, keep_o, send_o):
    width = mix.shape[1] // 6
    rows = mix.shape[0]
    table = jnp.concatenate(
        [columns[...].astype(F32), jnp.zeros((128 - columns.shape[0], rows), F32)], axis=0
    )
    sides = jnp.concatenate([table, jnp.zeros((128, 128 - rows), F32)], axis=1).T[0:rows]
    lane = lanes_of(sides.shape)
    moved = pltpu.roll(sides, 124, 1)
    halves = []
    for s, block in ((0, jnp.where(lane < 4, sides, moved)), (1, moved)):
        parts = [mix[:, (2 * i + s) * width : (2 * i + s + 1) * width] for i in range(3)]
        halves.append(jnp.concatenate(parts + [low(jnp.where(lane < 8, block, 0.0))], axis=1))
    first = pos[3] == 0
    keep_o[...] = jnp.where(first, halves[0], halves[1])
    send_o[...] = jnp.where(first, halves[1], halves[0])


def prepare_kernel(b, pos, own, oth, cot, unit_o, cott_o):
    chunk = own.shape[1]
    first = pos[3] == 0
    mine, theirs = own[0], oth[0]
    for j in range(2):
        unit, _ = norm_of(jnp.where(first == (j == 0), mine, theirs).astype(F32))
        unit_o[0, j * chunk : (j + 1) * chunk] = unit
    cott_o[0] = low(cot[0].astype(F32).T)


def feature_parts(angles, lane):
    s, c = sincos(angles)
    out = []
    turned_s, turned_c = swap_halves(s), swap_halves(c)
    for f, turned in (
        (jnp.where(lane < 64, s, turned_c), jnp.where(lane < 64, c, turned_s)),
        (jnp.where(lane < 64, turned_s, c), jnp.where(lane < 64, turned_c, s)),
    ):
        high = low(f)
        out.append((high, low(f - high.astype(F32)), low(turned)))
    return out


def query_kernel(b, a, wmix, maps, fq_o, fql_o, fqt_o):
    chunk = a.shape[1] // 2
    lane = lanes_of((chunk, 128))
    spans = [slice(j * chunk, (j + 1) * chunk) for j in range(2)]
    mixed = [low(mm(a[0, rows], wmix[:, 0:256])) for rows in spans]
    angles = [[mm(m[:, 128 * p : 128 * p + 128], maps[p]) for p in range(2)] for m in mixed]
    for j, rows in enumerate(spans):
        for p in range(2):
            for i, (high, rest, turned) in enumerate(feature_parts(angles[j][p], lane)):
                fq_o[0, 2 * p + i, rows], fql_o[0, 2 * p + i, rows], fqt_o[0, 2 * p + i, rows] = high, rest, turned


def project_kernel(
    b, pos, units, w0, w1, w2, w3, bias, maps,
    a_o, fk_o, fkl_o, fkt_o, va_o, ccol_o, ucol_o, crow_o, smid_o, pack_o, wmix_o, vec_o, vbar_o,
    w_s, sems,
):
    chunk = units.shape[1] // 2

    @pl.when(b == 0)
    def _():
        copies = [
            pltpu.make_async_copy(piece, w_s.at[:, pos[1] ^ mx, pos[2] ^ my], sems.at[2 * my + mx])
            for piece, (my, mx) in ((w0, (0, 0)), (w1, (0, 1)), (w2, (1, 0)), (w3, (1, 1)))
        ]
        for copy in copies:
            copy.start()
        for copy in copies:
            copy.wait()
        wmix_o[...] = w_s[...].reshape(wmix_o.shape)
        vec_o[...] = wmix_o[:, 768:896].astype(F32).T[0:8]
        vbar_o[...] = mm(jnp.broadcast_to(vec_o[5:6], vec_o.shape).astype(BF16), wmix_o[:, 512:768])

    gain, shift = vec_o[4:5], vec_o[5:6]
    row, col = lower_tri(chunk)
    tri = jnp.where(row >= col, 1.0, 0.0).astype(BF16)
    lane = lanes_of((chunk, 128))
    spans = [slice(j * chunk, (j + 1) * chunk) for j in range(2)]
    attends = [low(units[0, rows] * gain + shift) for rows in spans]
    for a, rows in zip(attends, spans):
        a_o[0, rows] = a
    wide = [mm(a, wmix_o[:, 256:896]) for a in attends]
    mixed = [low(m[:, 0:512]) for m in wide]
    angles = [[mm(m[:, 128 * p : 128 * p + 128], maps[p]) for p in range(2)] for m in mixed]
    douts, ends = [], []
    for j, rows in enumerate(spans):
        logits = wide[j][:, 512:640] + bias[...]
        e = jnp.exp(-jnp.abs(logits))
        w = 1.0 + e
        log1 = jnp.where(w == 1.0, e, jnp.log(w) * (e / jnp.where(w == 1.0, 1.0, w - 1.0)))
        log_gate = jnp.where(lane < 4, jnp.minimum(logits, 0.0) - log1, 0.0)
        fresh = jnp.where(lane < 4, jnp.where(logits >= 0.0, e, 1.0) / w, 0.0)
        cum = jnp.where(lane < 4, tri_sum(tri, log_gate), 0.0)
        ccol_o[0, rows] = cum
        ucol_o[0, rows] = fresh
        crow_o[0, j] = (cum + pltpu.roll(fresh, 4, 1)).T[0:8]
        ends.append(cum[chunk - 1 : chunk])
        douts.append(jnp.exp(ends[j] - cum) * fresh)
    one = jnp.where((lane == 64) | (lane == 65), 1.0, 0.0)
    shares = [[None] * 4, [None] * 4]
    for j, rows in enumerate(spans):
        for p in range(2):
            v = mixed[j][:, 256 + 128 * p : 384 + 128 * p].astype(F32) - vbar_o[0:1, 128 * p : 128 * p + 128]
            for h, vh in ((2 * p, v), (2 * p + 1, swap_halves(v))):
                aug = jnp.where(lane < 64, vh, one)
                va_o[0, h, rows] = low(aug)
                shares[j][h] = low(aug * douts[j][:, h : h + 1])
    locals_ = [[None] * 4, [None] * 4]
    for j, rows in enumerate(spans):
        for p in range(2):
            parts = feature_parts(angles[j][p], lane)
            for h in (2 * p, 2 * p + 1):
                fk_o[0, h, rows], fkl_o[0, h, rows], fkt_o[0, h, rows] = parts[h - 2 * p]
                locals_[j][h] = mm(parts[h - 2 * p][0], shares[j][h], TN)
    states = []
    for h in range(4):
        smid_o[0, h] = locals_[0][h]
        states.append(locals_[0][h] * jnp.exp(ends[1][:, h : h + 1]) + locals_[1][h])
    pack_states(states, pack_o, b, pack_o.shape[0] - 1)


def weights_of(ccol, ucol_row, crow, row, col):
    gap = jnp.minimum(ccol - crow, 0.0)
    return jnp.where(row >= col, jnp.exp(gap), 0.0) * ucol_row


def pairs_of(chunk):
    return [(j, h, slice(j * chunk, (j + 1) * chunk)) for j in range(2) for h in range(4)]


def scores(fq, fk, fql, fkl, h, rows):
    q, k = fq[0, h, rows], fk[0, h, rows]
    return mm(
        jnp.concatenate([q, fql[0, h, rows], q], axis=1), jnp.concatenate([k, k, fkl[0, h, rows]], axis=1), NT
    )


def local_kernel(b, fq, fk, fql, fkl, va, ccol, crow, o_o):
    chunk = crow.shape[3]
    row, col = lower_tri(chunk)
    pairs = pairs_of(chunk)
    qk = [scores(fq, fk, fql, fkl, h, rows) for j, h, rows in pairs]
    attn = [
        low(q * weights_of(ccol[0, rows, h : h + 1], crow[0, j, 4 + h : 5 + h], crow[0, j, h : h + 1], row, col))
        for q, (j, h, rows) in zip(qk, pairs)
    ]
    outs = [mm(a, va[0, h, rows]) for a, (j, h, rows) in zip(attn, pairs)]
    for out, (j, h, rows) in zip(outs, pairs):
        o_o[0, h, rows] = out


def mean_of(vbar, h):
    pair = vbar[:, 128 * (h // 2) : 128 * (h // 2) + 128]
    return (pair if h % 2 == 0 else swap_halves(pair))[0:1]


def finish_kernel(b, pos, o_loc, fq, ccol, pack, smid, vbar, inv_o, turn_o, st_o, keep_o, send_o):
    chunk = ccol.shape[1] // 2
    zcols = pack[pack.shape[0] - 1].astype(F32)
    states = unpack_states(pack, b, zcols)
    lane = lanes_of((chunk, 128))
    cend = ccol[0, chunk - 1 : chunk]
    pairs = pairs_of(chunk)
    near = []
    for h in range(4):
        near.append(low(states[h]))
        near.append(low(jnp.exp(cend[:, h : h + 1]) * states[h] + smid[0, h]))
        for j in range(2):
            st_o[0, h, j] = near[2 * h + j]
    inter = [mm(fq[0, h, rows], near[2 * h + j]) for j, h, rows in pairs]
    outs = [
        o_loc[0, h, rows] + jnp.exp(ccol[0, rows, h : h + 1]) * part for part, (j, h, rows) in zip(inter, pairs)
    ]
    dens = [jnp.broadcast_to(o[:, 64:65], o.shape) for o in outs]
    invs = [lax.rsqrt(den * den + 1.0) for den in dens]
    att = [[None] * 4, [None] * 4]
    for o, den, inv, (j, h, rows) in zip(outs, dens, invs, pairs):
        mean = mean_of(vbar, h)
        att[j][h] = (o + den * mean) * inv
        inv_o[0, h, rows] = jnp.where(lane < 64, inv, 0.0)
        turn_o[0, h, rows] = mean - den * inv * att[j][h]
    first = pos[3] == 0
    for p in range(2):
        both = [
            jnp.where(lane < 64, att[j][2 * p], swap_halves(att[j][2 * p + 1])) for j in range(2)
        ]
        keep_o[0, :, 128 * p : 128 * p + 128] = jnp.where(first, both[0], both[1]).astype(BF16)
        send_o[0, :, 128 * p : 128 * p + 128] = jnp.where(first, both[1], both[0]).astype(BF16)


def dp_of(pos, mz, mx):
    return (pos[0] ^ mz) * 2 + (pos[1] ^ mx)


def feed_chunks(pos, near, far, cot, cott, feed, feedt, target, up_s, dn_s, hid_s, gp_s, big_s):
    seqs, chunk, _ = cot.shape
    nz = far.shape[0]
    width, both = up_s.shape
    hidden = both // 2
    rows_up = width // (2 * nz)
    for my in range(2):
        cols = slice(my * hidden, (my + 1) * hidden)
        for mx in range(2):
            k = 2 * my + mx
            piece = far if k == 3 else near.at[pl.ds(k * nz, nz)]
            for z in range(nz):
                at = pl.multiple_of((2 * z + (pos[1] ^ mx)) * rows_up, rows_up)
                up_s[pl.ds(at, rows_up), cols] = piece[z, 0:rows_up]
                dn_s[pl.ds(at, rows_up), cols] = piece[z, rows_up : 2 * rows_up]

    def scatter(offset):
        for my in range(2):
            cols = slice(my * hidden, (my + 1) * hidden)
            for mx in range(2):
                for mz in range(nz):
                    at = pl.multiple_of(dp_of(pos, mz, mx) * rows_up, rows_up)
                    target[my, mx, mz, offset : offset + rows_up, :] = big_s[pl.ds(at, rows_up), cols]

    spans = [slice(r * chunk, (r + 1) * chunk) for r in range(seqs)]
    outs, grads = [], []
    pres = [mm(feed[rows], up_s[...]) for rows in spans]
    ghs = [mm(cot[r], dn_s[...]) for r in range(seqs)]
    for r, rows in enumerate(spans):
        cdf, pdf = normal_parts(pres[r])
        hid_s[rows] = low(pres[r] * cdf)
        gp_s[rows] = low(ghs[r] * (cdf + pres[r] * pdf))
    for rows in spans:
        outs.append(mm(hid_s[rows], dn_s[...], NT))
        grads.append(mm(gp_s[rows], up_s[...], NT))
    big_s[...] = low(mm(feedt[...], gp_s[...]))
    scatter(0)
    big_s[...] = low(mm(jnp.concatenate([cott[r] for r in range(seqs)], axis=1), hid_s[...]))
    scatter(rows_up)
    return outs, grads


def feed_first_kernel(
    pos, akeep, arecv, x, cot, cott, vec, near_own, far_own, near, far,
    gsend_o, acc_o, gf_o, mid_o, feed_o, feedt_o, att_o, ow_o,
    up_s, dn_s, hid_s, gp_s, big_s,
):
    seqs, chunk, _ = x.shape
    nz = far.shape[0]
    rows_up = up_s.shape[0] // (2 * nz)
    first = pos[3] == 0
    for mc, (some, rest) in enumerate(((near_own, far_own), (near, far))):
        for my in range(2):
            t = (pos[2] ^ my) * 2 + (pos[3] ^ mc)
            for mx in range(2):
                k = 2 * my + mx
                for z in range(nz):
                    at = pl.multiple_of(((2 * z + (pos[1] ^ mx)) * 4 + t) * 16, 16)
                    source = rest if k == 3 else some.at[pl.ds(k * nz, nz)]
                    ow_o[pl.ds(at, 16), :] = source[z, 2 * rows_up :]
    gain, shift = vec[6:7], vec[7:8]
    for r in range(seqs):
        rows = slice(r * chunk, (r + 1) * chunk)
        mine, theirs = akeep[r], arecv[r]
        att = jnp.concatenate([jnp.where(first, mine, theirs), jnp.where(first, theirs, mine)], axis=1)
        att_o[rows] = att
        mid = x[r].astype(F32) + mm(att, ow_o[...])
        mid_o[rows] = mid
        unit, _ = norm_of(mid)
        feed = unit * gain + shift
        feed_o[rows] = low(feed)
        feedt_o[:, rows] = low(feed.T)
    outs, grads = feed_chunks(pos, near, far, cot, cott, feed_o, feedt_o, gsend_o, up_s, dn_s, hid_s, gp_s, big_s)
    for r, (out, grad) in enumerate(zip(outs, grads)):
        acc_o[r * chunk : (r + 1) * chunk] = out
        gf_o[r * chunk : (r + 1) * chunk] = grad


def feed_second_kernel(
    pos, cot, cott, vec, near, far, acc, gf_in, mid_in, feed, feedt, att, ow,
    out_o, gm_o, gak_o, gas_o, gkeep_o, okeep_o, osend_o, gv_o,
    up_s, dn_s, hid_s, gp_s, gb_s, big_s,
):
    seqs, chunk, width = cot.shape
    nz = far.shape[0]
    first = pos[3] == 0
    outs, grads = feed_chunks(pos, near, far, cot, cott, feed, feedt, gkeep_o, up_s, dn_s, hid_s, gp_s, big_s)
    gain = vec[6:7]
    gain_sum = jnp.zeros((1, width), F32)
    shift_sum = jnp.zeros((1, width), F32)
    for r in range(seqs):
        rows = slice(r * chunk, (r + 1) * chunk)
        mid = mid_in[rows]
        out_o[r] = low(mid + (acc[rows] + outs[r]))
        unit, inv = norm_of(mid)
        gf = gf_in[rows] + grads[r]
        gain_sum += jnp.sum(gf * unit, axis=0, keepdims=True)
        shift_sum += jnp.sum(gf, axis=0, keepdims=True)
        gm = cot[r].astype(F32) + norm_back(gf * gain, unit, inv)
        gm_o[r] = gm
        gb = low(gm)
        gb_s[rows] = gb
        ga = low(mm(gb, ow[...], NT))
        half = width // 2
        gak_o[r] = jnp.where(first, ga[:, :half], ga[:, half:])
        gas_o[r] = jnp.where(first, ga[:, half:], ga[:, :half])
    gv_o[...] = jnp.concatenate([gain_sum, shift_sum, jnp.zeros((6, width), F32)], axis=0)
    big_s[:, 0:width] = low(mm(att[...], gb_s[...], TN))
    for mc, target in ((0, okeep_o), (1, osend_o)):
        for my in range(2):
            t = (pos[2] ^ my) * 2 + (pos[3] ^ mc)
            for mx in range(2):
                for mz in range(nz):
                    at = pl.multiple_of((dp_of(pos, mz, mx) * 4 + t) * 16, 16)
                    target[my, mx, mz] = big_s[pl.ds(at, 16), 0:width]


def adjoint_kernel(b, pos, gak, gar, inv_root, turn, fq, ccol, g_o, scaled_o, l1_o, pack_o):
    chunk = ccol.shape[1] // 2
    lane = lanes_of((chunk, 128))
    first = pos[3] == 0
    pairs = pairs_of(chunk)
    gas = []
    for j in range(2):
        for p in range(2):
            cols = slice(128 * p, 128 * p + 128)
            pair = jnp.where(first == (j == 0), gak[0, :, cols], gar[0, :, cols]).astype(F32)
            gas += [pair, swap_halves(pair)]
    gns = [low(ga * inv_root[0, h, rows]).astype(F32) for ga, (j, h, rows) in zip(gas, pairs)]
    gds = [
        jnp.sum(gn * turn[0, h, rows], axis=1, keepdims=True) for gn, (j, h, rows) in zip(gns, pairs)
    ]
    scaled = []
    for gn, gd, (j, h, rows) in zip(gns, gds, pairs):
        gd = jnp.broadcast_to(gd, gn.shape)
        high = low(gd).astype(F32)
        g = jnp.where(lane == 64, high, jnp.where(lane == 65, gd - high, gn))
        g_o[0, h, rows] = low(g)
        scaled.append(low(g * jnp.exp(ccol[0, rows, h : h + 1])))
        scaled_o[0, h, rows] = scaled[-1]
    parts = [mm(fq[0, h, rows], g, TN) for g, (j, h, rows) in zip(scaled, pairs)]
    states = []
    for h in range(4):
        l1_o[0, h] = parts[4 + h]
        states.append(parts[h] + jnp.exp(ccol[0, chunk - 1 : chunk, h : h + 1]) * parts[4 + h])
    pack_states(states, pack_o, b, pack_o.shape[0] - 1, split=True)


def local_back_kernel(b, fq, fk, va, g, scaled, st, ccol, crow, dfq_o, dfk_o, dva_o):
    chunk = crow.shape[3]
    row, col = lower_tri(chunk)
    pairs = pairs_of(chunk)
    for half in (pairs[:4], pairs[4:]):
        qk = [mm(fq[0, h, rows], fk[0, h, rows], NT) for j, h, rows in half]
        da = [mm(g[0, h, rows], va[0, h, rows], NT) for j, h, rows in half]
        inter = [mm(scaled[0, h, rows], st[0, h, j], NT) for j, h, rows in half]
        attn, dp = [], []
        for q, d, (j, h, rows) in zip(qk, da, half):
            w = weights_of(ccol[0, rows, h : h + 1], crow[0, j, 4 + h : 5 + h], crow[0, j, h : h + 1], row, col)
            attn.append(low(q * w))
            dp.append(low(d * w))
        dva = [mm(a, g[0, h, rows], TN) for a, (j, h, rows) in zip(attn, half)]
        dfk = [mm(d, fq[0, h, rows], TN) for d, (j, h, rows) in zip(dp, half)]
        dfq = [mm(d, fk[0, h, rows]) for d, (j, h, rows) in zip(dp, half)]
        for i, (j, h, rows) in enumerate(half):
            dfq_o[0, h, rows] = dfq[i] + inter[i]
            dfk_o[0, h, rows] = dfk[i]
            dva_o[0, h, rows] = dva[i]


def close_kernel(
    b, pos, units, attend, fq, fk, fqt, fkt, va, dfq, dfk, dva, ccol, ucol, pack, l1, st, wmix, gv, back,
    m00_o, m01_o, m10_o, m11_o, gnk_o, gns_o,
    acc_s, gm_s, gate_s, vsum_s, big_s,
    *, seqs_total,
):
    seqs = seqs_total
    chunk = units.shape[1] // 2
    nz = m00_o.shape[0]
    lane = lanes_of((chunk, 128))
    row, col = lower_tri(chunk)
    upper = jnp.where(row <= col, 1.0, 0.0).astype(BF16)
    zcols = pack[pack.shape[0] - 1].astype(F32)
    arrived = unpack_states(pack, b, zcols, last=64)
    wide = lanes_of((128, 128))

    @pl.when(b == 0)
    def _():
        gate_s[...] = jnp.zeros_like(gate_s)
        vsum_s[...] = jnp.zeros_like(vsum_s)

    pairs = pairs_of(chunk)
    spans = [slice(j * chunk, (j + 1) * chunk) for j in range(2)]
    cums = [ccol[0, rows] for rows in spans]
    freshs = [ucol[0, rows] for rows in spans]
    douts = [jnp.exp(cum[chunk - 1 : chunk] - cum) * fresh for cum, fresh in zip(cums, freshs)]
    nears = []
    for j, h, rows in pairs:
        adj = arrived[h]
        if j == 0:
            adj = l1[0, h] + jnp.exp(ccol[0, 2 * chunk - 1 : 2 * chunk, h : h + 1]) * adj
        zs = adj[:, 64:65] + adj[:, 65:66]
        high = low(zs).astype(F32)
        nears.append(low(jnp.where(wide == 64, high, jnp.where(wide == 65, zs - high, adj))))
    dk_fars = [mm(va[0, h, rows], near, NT) for near, (j, h, rows) in zip(nears, pairs)]
    dv_fars = [mm(fk[0, h, rows], near) for near, (j, h, rows) in zip(nears, pairs)]
    kds, qds, levels = [], [], []
    pqs, pks, dvs = [], [], []
    for i, (j, h, rows) in enumerate(pairs):
        d = douts[j][:, h : h + 1]
        keys, queries = fk[0, h, rows].astype(F32), fq[0, h, rows].astype(F32)
        dk_far = d * dk_fars[i]
        dk = dk_far + dfk[0, h, rows]
        dq = dfq[0, h, rows]
        kds.append(jnp.sum(keys * dk, axis=1, keepdims=True))
        qds.append(jnp.sum(queries * dq, axis=1, keepdims=True))
        passed = st[0, h, j].astype(F32) * nears[i].astype(F32)
        passed = jnp.sum(jnp.sum(passed, axis=0, keepdims=True), axis=1, keepdims=True)
        total = jnp.sum(jnp.sum(keys * dk_far, axis=0, keepdims=True), axis=1, keepdims=True)
        levels.append(total + jnp.exp(cums[j][chunk - 1 : chunk, h : h + 1]) * passed)
        dvs.append(dva[0, h, rows] + d * dv_fars[i])
        pks.append(low(dk * fkt[0, h, rows].astype(F32)))
        pqs.append(low(dq * fqt[0, h, rows].astype(F32)))
    grads = [
        [mm(jnp.concatenate(ps[4 * j + 2 * p : 4 * j + 2 * p + 2], axis=1), back[p]) for ps in (pqs, pks) for p in range(2)]
        for j in range(2)
    ]
    bias_sum = jnp.zeros((1, 128), F32)
    gms = []
    for j in range(2):
        kd = qd = jnp.zeros((chunk, 128), F32)
        level = jnp.zeros((1, 128), F32)
        for h in range(4):
            kd = jnp.where(lane == h, kds[4 * j + h], kd)
            qd = jnp.where(lane == h, qds[4 * j + h], qd)
            level = jnp.where(lanes_of((1, 128)) == h, levels[4 * j + h], level)
        dlog = tri_sum(upper, qd - kd) + level
        dlogit = jnp.where(lane < 4, freshs[j] * dlog - (1.0 - freshs[j]) * kd, 0.0)
        bias_sum += jnp.sum(dlogit, axis=0, keepdims=True)
        values = [jnp.where(lane < 64, dvs[4 * j + 2 * p], swap_halves(dvs[4 * j + 2 * p + 1])) for p in range(2)]
        gm = jnp.concatenate([low(x) for x in (*grads[j], *values, dlogit)], axis=1)
        gm_s[pl.ds(pl.multiple_of((2 * b + j) * chunk, chunk), chunk), :] = gm
        gms.append(gm)
    normed = [mm(gm, wmix[...], NT) for gm in gms]
    vsum_s[0:1] += sum(jnp.sum(n * units[0, rows], axis=0, keepdims=True) for n, rows in zip(normed, spans))
    vsum_s[1:2] += sum(jnp.sum(n, axis=0, keepdims=True) for n in normed)
    first = pos[3] == 0
    gnk_o[0] = jnp.where(first, normed[0], normed[1])
    gns_o[0] = low(jnp.where(first, normed[1], normed[0]))
    gate_s[0:1] += bias_sum

    @pl.when(b == seqs - 1)
    def _():
        width = acc_s.shape[0]
        acc_s[...] = mm(attend[...].reshape(gm_s.shape[0], width), gm_s[...], TN)
        table = jnp.concatenate(
            [jnp.zeros((4, width), F32), vsum_s[0:2], gv[0:2], jnp.zeros((120, width), F32)], axis=0
        ).T
        total = gate_s[0:1]
        high = low(total).astype(F32)
        rest = jnp.broadcast_to(total - high, (8, 128))
        both = pltpu.roll(jnp.broadcast_to(high, (8, 128)), 8, 1) + pltpu.roll(rest, 12, 1)
        biases = jnp.broadcast_to(both[0:1], (width, 128))
        side = jnp.where(lanes_of((width, 128)) < 4, acc_s[:, 768:896], table) + biases
        big_s[:, 0:768] = acc_s[:, 0:768].astype(BF16)
        big_s[:, 768:896] = side.astype(BF16)
        for my in range(2):
            for mx in range(2):
                for mz in range(nz):
                    at = pl.multiple_of(chip_row(pos, mz, mx, my), 32)
                    (m00_o, m01_o, m10_o, m11_o)[2 * my + mx][mz] = big_s[pl.ds(at, 32), :]


def final_kernel(pos, keep, recv, mix_o, gate_o, bias_o, *vec_o):
    first = pos[3] == 0
    mine, theirs = keep[...], recv[...]
    halves = (jnp.where(first, mine, theirs), jnp.where(first, theirs, mine))
    width = mix_o.shape[1] // 6
    for i in range(3):
        for s in range(2):
            mix_o[:, (2 * i + s) * width : (2 * i + s + 1) * width] = halves[s][:, i * width : (i + 1) * width]
    sides = [half[:, 3 * width :] for half in halves]
    lane = lanes_of(sides[0].shape)
    both = jnp.concatenate([sides[0] + sides[1], sides[0], sides[1], jnp.zeros((80, 128), F32)], axis=0).T
    gate_o[0:4] = both[0:4, 16:32]
    gate_o[4:8] = both[0:4, 32:48]
    for i, out in enumerate(vec_o):
        out[...] = both[4 + i, 0:16]
    sums = [side[0:8] + pltpu.roll(side[0:8], 124, 1) for side in sides]
    row = jnp.where(lane[0:8] < 4, pltpu.roll(sums[0], 120, 1), pltpu.roll(sums[1], 124, 1))
    bias_o[...] = row[0, 0:8]


def input_kernel(b, x, gm, keep, recv, vec, o, done_o):
    done_o[...] = jnp.zeros_like(done_o)
    unit, inv = norm_of(x[0].astype(F32))
    grad = keep[0] + recv[0].astype(F32)
    o[0] = gm[0] + norm_back(grad * vec[4:5], unit, inv)


def hold_kernel(*refs):
    sems = refs[-1]
    count = (len(refs) - 1) // 2
    copies = [
        pltpu.make_async_copy(refs[i], refs[count + i], sems.at[i]) for i in range(count)
    ]
    for copy in copies:
        copy.start()
    for copy in copies:
        copy.wait()


def halves_kernel(by_x, by_y, x_half, y_half, sems):
    half = x_half.shape[0]
    copies = [
        pltpu.make_async_copy(by_x.at[pl.ds(0, half)], x_half, sems.at[0]),
        pltpu.make_async_copy(by_y.at[pl.ds(half, half)], y_half, sems.at[1]),
    ]
    for copy in copies:
        copy.start()
    for copy in copies:
        copy.wait()


def gather_kernel(*refs):
    parts, out, sems = refs[:-2], refs[-2], refs[-1]
    copies, at = [], 0
    for i, part in enumerate(parts):
        copies.append(pltpu.make_async_copy(part, out.at[pl.ds(at, part.shape[0])], sems.at[i]))
        at += part.shape[0]
    for copy in copies:
        copy.start()
    for copy in copies:
        copy.wait()


def pause_kernel(out):
    out[...] = jnp.zeros_like(out)


def join_kernel(pos, *refs, axis):
    parts, out, sems = refs[:-2], refs[-2], refs[-1]
    copies = [
        pltpu.make_async_copy(part, out.at[pos[axis] ^ i], sems.at[i]) for i, part in enumerate(parts)
    ]
    for copy in copies:
        copy.start()
    for copy in copies:
        copy.wait()


def pair_sum_kernel(keep, recv, okeep, orecv, x_keep, x_send, y_keep, y_send):
    half = x_keep.shape[1]
    rows = keep.shape[3]
    first, second = slice(0, half), slice(half, 2 * half)
    for i in range(2):
        for my, mx, zs, out in ((i, 0, first, x_keep), (i, 1, first, x_send), (0, i, second, y_keep), (1, i, second, y_send)):
            out[i, :, 0:rows] = low(keep[my, mx, zs].astype(F32) + recv[my, mx, zs].astype(F32))
            out[i, :, rows:] = low(okeep[my, mx, zs].astype(F32) + orecv[my, mx, zs].astype(F32))


def half_sum_kernel(x_keep, x_recv, y_keep, y_recv, x_own, x_far, y_own, y_far):
    for keep, recv, own, far in ((x_keep, x_recv, x_own, x_far), (y_keep, y_recv, y_own, y_far)):
        for i, out in ((0, own), (1, far)):
            out[...] = low(keep[i].astype(F32) + recv[i].astype(F32))


def line_sum_kernel(x_own, x_recv, y_own, y_recv, *outs):
    half = x_own.shape[0]
    for i in range(half):
        outs[i][...] = low(x_own[i].astype(F32) + x_recv[i].astype(F32))
        outs[half + i][...] = low(y_own[i].astype(F32) + y_recv[i].astype(F32))


def sum_of_four(refs):
    a, b, c, d = (ref[...].astype(F32) for ref in refs)
    return (a + b) + (c + d)


def mix_sum_kernel(m0, m1, m2, m3, *outs):
    total = sum_of_four((m0, m1, m2, m3))
    side = total[..., 768:896]
    rest = side - low(side).astype(F32)
    lane = lanes_of(side.shape)
    moved = jnp.where((lane >= 12) & (lane < 16), side + pltpu.roll(rest, 4, side.ndim - 1), side)
    for i, out in enumerate(outs):
        out[:, 0:768] = low(total[i, :, 0:768])
        out[:, 768:896] = low(moved[i])


def feed_last_kernel(a, b, c, d, up_o, down_o, out_o, done_o):
    done_o[...] = jnp.zeros_like(done_o)
    total = sum_of_four((a, b, c, d))
    rows = up_o.shape[0]
    up_o[...] = total[0:rows]
    down_o[...] = total[rows : 2 * rows]
    out_o[...] = total[2 * rows :]


def mix_last_kernel(pos, a, b, c, d, keep_o, send_o):
    total = sum_of_four((a, b, c, d))
    rows = keep_o.shape[0]
    first = pos[3] == 0
    keep_o[...] = jnp.where(first, total[:rows], total[rows:])
    send_o[...] = jnp.where(first, total[rows:], total[:rows])


def call(kernel, steps, ins, outs, scratch=(), us=1.0, name=None, limit=12, unroll=False):
    def spec(kind):
        if kind in "da":
            return pl.BlockSpec(memory_space=pl.ANY)
        return pl.BlockSpec(memory_space=pltpu.SMEM if kind == "m" else pltpu.VMEM)

    kinds = [kind for kind, _ in ins]
    out_kinds = [kind for kind, _, _ in outs]
    all_kinds = kinds + out_kinds + ["w"] * len(scratch)

    def run(*refs):
        used = [(kind, ref) for kind, ref in zip(all_kinds, refs) if kind != "d"]
        if not steps:
            kernel(*[ref for _, ref in used])
            return

        def one(b, carry):
            kernel(b, *[ref.at[pl.ds(b, 1)] if kind == "s" else ref for kind, ref in used])
            return carry

        lax.fori_loop(0, steps, one, 0, unroll=unroll)

    return pl.pallas_call(
        run,
        in_specs=[spec(kind) for kind in kinds],
        out_specs=[spec(kind) for kind in out_kinds],
        out_shape=[jax.ShapeDtypeStruct(shape, dtype) for _, shape, dtype in outs],
        scratch_shapes=list(scratch),
        compiler_params=pltpu.CompilerParams(vmem_limit_bytes=limit * 1024 * 1024),
        cost_estimate=pl.CostEstimate(flops=int(us * 1.15e9), bytes_accessed=0, transcendentals=0),
        name=name,
    )(*[a for _, a in ins])


def xor_with(a, mask, count):
    return lax.ppermute(a, BOTH, [(i, i ^ mask) for i in range(count)])


def body(
    inputs, cotangent, mix_weight, gate_weight, gate_bias, out_weight, gain_first, shift_first, gain_second,
    shift_second, up_weight, down_weight, random_maps,
):
    dp, tensor = lax.axis_size("dp"), lax.axis_size("tensor")
    count = dp * tensor
    place_dp, place_t = lax.axis_index("dp"), lax.axis_index("tensor")
    seqs, chunk, width = inputs.shape
    heads, head = random_maps.shape[0], random_maps.shape[1]
    hidden = up_weight.shape[1]
    core = place_t % 2
    first = core == 0
    direct = dp == 8
    nz = 4
    if direct:
        pos = jnp.stack([place_dp // 2, place_dp % 2, place_t // 2, core]).astype(jnp.int32)
    else:
        pos = jnp.stack([jnp.zeros_like(core)] * 3 + [core]).astype(jnp.int32)
    swap_core = functools.partial(xor_with, mask=1, count=count)

    def mix_pack(mix_w, gate_w, vecs):
        rows = mix_w.shape[0]
        split = mix_w.reshape(rows, 3, 2, width // 2)
        sides = [v[:, None] for v in vecs]
        pad = jnp.zeros((rows, 120), BF16)
        return [
            jnp.concatenate(
                [split[:, 0, s], split[:, 1, s], split[:, 2, s], gate_w[:, 4 * s : 4 * s + 4]] + sides + [pad], axis=1
            )
            for s in range(2)
        ]

    def join(parts, axis, after=()):
        (out,) = call(
            functools.partial(join_kernel, axis=axis), 0, [("m", pos)] + [("a", a) for a in parts] + [("d", a) for a in after],
            [("w", (len(parts), *parts[0].shape), parts[0].dtype)],
            scratch=[pltpu.SemaphoreType.DMA((len(parts),))], name="join",
        )
        return out

    def pause(after, us):
        (out,) = call(
            pause_kernel, 0, [("d", a) for a in after], [("w", (8, 128), F32)], us=us, name="pause",
        )
        return out

    def from_plane(pieces):
        return [pieces[0], xor_with(pieces[1], 4, count), xor_with(pieces[2], 2, count), xor_with(pieces[3], 6, count)]

    other_in = swap_core(inputs)
    vectors = (gain_first, shift_first, gain_second, shift_second)
    long = 2 * chunk
    unit, cot_t = call(
        prepare_kernel, seqs, [("m", pos), ("s", inputs), ("s", other_in), ("s", cotangent)],
        [("s", (seqs, long, width), F32), ("s", (seqs, width, chunk), BF16)], us=2.5, name="prepare",
    )
    if direct:
        rows = mix_weight.shape[0]
        columns = jnp.pad(gate_weight.T, ((0, 16 - heads), (0, 0)))
        place = lax.broadcasted_iota(jnp.int32, columns.shape, 0)
        for i, v in enumerate(vectors):
            columns = jnp.where(place == heads + i, lax.broadcast_in_dim(v, columns.shape, (1,)), columns)
        keep, send = call(
            pack_kernel, 0, [("m", pos), ("w", mix_weight), ("w", columns)], [("w", (rows, 896), BF16)] * 2, name="pack",
        )
        pair = join([keep, swap_core(send)], 3)
        line = join([pair] + [xor_with(pair, 8 * m, count) for m in range(1, nz)], 0, after=[unit])
        w_pieces = [line] + [xor_with(line, m, count) for m in (4, 2, 6)]
        block = jnp.concatenate([up_weight, down_weight.T, out_weight], axis=0)
        (block,) = call(
            hold_kernel, 0, [("a", block), ("d", unit)],
            [("w", block.shape, BF16)], scratch=[pltpu.SemaphoreType.DMA((1,))], name="hold",
        )
        ff_line = join([block] + [xor_with(block, 8 * m, count) for m in range(1, nz)], 0, after=[line])
        by_x, by_y = xor_with(ff_line, 4, count), xor_with(ff_line, 2, count)
    else:
        whole = [
            lax.all_gather(a, BOTH, axis=0, tiled=True) for a in (mix_weight, gate_weight, out_weight) + vectors
        ]
        p0, p1 = mix_pack(whole[0], whole[1], whole[3:])
        blocks = jnp.where(first, p0, p1).reshape(nz, 2, 2, 2, 16, 896)
        w_pieces = [blocks[:, mx, my] for my, mx in ((0, 0), (0, 1), (1, 0), (1, 1))]
        up_all = lax.all_gather(up_weight, BOTH, axis=0, tiled=False).reshape(dp, tensor, -1, hidden)
        dn_all = lax.all_gather(down_weight.T, BOTH, axis=0, tiled=False).reshape(dp, tensor, -1, hidden)
        up_all = jnp.moveaxis(up_all, 1, 0).reshape(2, 2, nz, 2, -1, hidden)
        dn_all = jnp.moveaxis(dn_all, 1, 0).reshape(2, 2, nz, 2, -1, hidden)
        out_all = whole[2].reshape(nz, 2, 2, 2, 16, width).transpose(2, 3, 0, 1, 4, 5)
        ff_all = jnp.concatenate([up_all, dn_all, out_all], axis=4)
        ff_all = jnp.where(first, ff_all, ff_all[:, ::-1])
        ff_own, ff_other = (
            jnp.concatenate([ff_all[my, mc, :, mx] for my in range(2) for mx in range(2)]) for mc in range(2)
        )

    maps = lax.dynamic_slice_in_dim(random_maps, core * 4, 4, 0)
    zero = jnp.zeros((head, head), BF16)
    maps_pair = jnp.stack(
        [
            jnp.concatenate(
                [jnp.concatenate([maps[2 * p], zero], 1), jnp.concatenate([zero, maps[2 * p + 1]], 1)], 0
            )
            for p in range(2)
        ]
    )
    flip = jnp.swapaxes(maps, 1, 2)
    maps_back = jnp.stack(
        [
            jnp.concatenate(
                [
                    jnp.concatenate([flip[2 * p], zero], 1),
                    jnp.concatenate([-flip[2 * p], zero], 1),
                    jnp.concatenate([zero, flip[2 * p + 1]], 1),
                    jnp.concatenate([zero, -flip[2 * p + 1]], 1),
                ],
                0,
            )
            for p in range(2)
        ]
    )
    bias = jnp.pad(lax.dynamic_slice_in_dim(gate_bias, core * 4, 4, 0), (0, 124))[None]

    tokens = seqs * long
    feats = (seqs, 4, long, 128)
    npack = 2 * seqs + 1
    attend, fk, fkl, fkt, va, ccol, ucol, crow, smid, pack, wmix, vec, vbar = call(
        project_kernel, seqs,
        [("m", pos), ("s", unit)] + [("a", w) for w in w_pieces] + [("w", bias), ("w", maps_pair)],
        [
            ("s", (seqs, long, width), BF16), ("s", feats, BF16), ("s", feats, BF16), ("s", feats, BF16), ("s", feats, BF16),
            ("s", (seqs, long, 128), F32), ("s", (seqs, long, 128), F32),
            ("s", (seqs, 2, 8, chunk), F32),
            ("s", (seqs, 4, 128, 128), F32),
            ("w", (npack, 128, 128), BF16), ("w", (width, 896), BF16), ("w", (8, width), F32),
            ("w", (8, width // 2), F32),
        ],
        scratch=[pltpu.VMEM((nz, 2, 2, 2, 16, 896), BF16), pltpu.SemaphoreType.DMA((4,))], us=12, name="project",
    )
    ahead = [(i, i + 2) for i in range(count) if (i % tensor) < 2]
    arrived = lax.ppermute(pack, BOTH, ahead)
    fq, fql, fqt = call(
        query_kernel, seqs, [("s", attend), ("w", wmix), ("w", maps_pair)], [("s", feats, BF16)] * 3, us=0.3, name="query",
    )
    (o_loc,) = call(
        local_kernel, seqs,
        [("s", fq), ("s", fk), ("s", fql), ("s", fkl), ("s", va), ("s", ccol), ("s", crow)],
        [("s", feats, F32)], us=0.3, name="local",
    )
    if direct:
        half_z = nz // 2
        far_shape = (half_z, *ff_line.shape[1:])
        x_half, y_half = call(
            halves_kernel, 0, [("a", by_x), ("a", by_y), ("d", arrived), ("d", o_loc)], [("w", far_shape, BF16)] * 2,
            scratch=[pltpu.SemaphoreType.DMA((2,))], us=0.3, name="halves",
        )
        near_parts = [ff_line, by_x, by_y]
        (ff_near,) = call(
            gather_kernel, 0, [("a", a) for a in near_parts] + [("d", x_half)],
            [("w", (3 * nz, *ff_line.shape[1:]), BF16)], scratch=[pltpu.SemaphoreType.DMA((3,))], us=0.5, name="near",
        )
        before_finish = [x_half]
    else:
        before_finish = []
    (inv_root, turn, st, att_keep, att_send) = call(
        finish_kernel, seqs,
        [("m", pos), ("s", o_loc), ("s", fq), ("s", ccol), ("w", arrived), ("s", smid), ("w", vbar)]
        + [("d", a) for a in before_finish],
        [
            ("s", feats, F32), ("s", feats, F32), ("s", (seqs, 4, 2, 128, 128), BF16),
            ("s", (seqs, chunk, width // 2), BF16), ("s", (seqs, chunk, width // 2), BF16),
        ],
        us=0.3, name="finish",
    )
    att_recv = swap_core(att_send)
    if direct:
        near_other = swap_core(ff_near)
        far_parts = [xor_with(x_half, 2, count), xor_with(y_half, 4, count)]
        (ff_far,) = call(
            gather_kernel, 0, [("a", a) for a in far_parts] + [("d", att_keep)],
            [("w", ff_line.shape, BF16)], scratch=[pltpu.SemaphoreType.DMA((2,))], name="gather",
        )
        far_other = swap_core(ff_far)
    else:
        ff_near, ff_far, near_other, far_other = ff_own[: 3 * nz], ff_own[3 * nz :], ff_other[: 3 * nz], ff_other[3 * nz :]

    own = seqs * chunk
    nrows = ff_near.shape[1]
    payload, out_payload = (2, 2, nz, nrows - 16, hidden), (2, 2, nz, 16, hidden)
    rows_low, rows_full = ("w", (own, width), BF16), ("w", (own, width), F32)
    work = [
        pltpu.VMEM((width, 2 * hidden), BF16), pltpu.VMEM((width, 2 * hidden), BF16),
        pltpu.VMEM((own, 2 * hidden), BF16), pltpu.VMEM((own, 2 * hidden), BF16),
    ]
    big = pltpu.VMEM((width, 2 * hidden), BF16)
    g_send, *fed = call(
        feed_first_kernel, 0,
        [("m", pos)] + [
            ("w", a) for a in (
                att_keep, att_recv, inputs, cotangent, cot_t, vec, ff_near, ff_far, near_other, far_other
            )
        ],
        [
            ("w", payload, BF16), rows_full, rows_full, rows_full, rows_low, ("w", (width, own), BF16), rows_low,
            ("w", (width, width), BF16),
        ],
        scratch=[*work, big], us=10, name="feed_first", limit=18,
    )
    g_recv = swap_core(g_send)
    output, grad_middle, ga_keep, ga_send, g_keep, o_keep, o_send, grad_vec = call(
        feed_second_kernel, 0,
        [("m", pos)] + [("w", a) for a in (cotangent, cot_t, vec, ff_near, ff_far, *fed)],
        [
            ("w", (seqs, chunk, width), BF16), ("w", (seqs, chunk, width), F32),
            ("w", (seqs, chunk, width // 2), BF16), ("w", (seqs, chunk, width // 2), BF16),
            ("w", payload, BF16), ("w", out_payload, BF16), ("w", out_payload, BF16), ("w", (8, width), F32),
        ],
        scratch=[
            *work, pltpu.VMEM((own, width), BF16), big,
        ],
        us=10, name="feed_second", limit=18,
    )
    ga_recv = swap_core(ga_send)

    if direct:
        o_recv = swap_core(o_send)
        half_z = nz // 2
        two, one = (2, half_z, nrows, hidden), (half_z, nrows, hidden)
        x_keep, x_send, y_keep, y_send = call(
            pair_sum_kernel, 0, [("w", g_keep), ("w", g_recv), ("w", o_keep), ("w", o_recv)], [("w", two, BF16)] * 4,
            us=0.6, name="pair_sum",
        )
        x_recv, y_recv = xor_with(x_send, 4, count), xor_with(y_send, 2, count)
        before_adjoint = [x_keep]
    else:
        before_adjoint = []
        g_keep, g_send = (jnp.concatenate(parts, axis=3) for parts in ((g_keep, o_keep), (g_send, o_send)))
        by_core = jnp.where(first, jnp.stack([g_keep, g_send]), jnp.stack([g_send, g_keep]))
        by_rows = by_core.transpose(3, 2, 1, 0, 4, 5)
        rows_up = (nrows - 16) // 2
        ups = by_rows[..., :rows_up, :].reshape(nz * 2, 4, rows_up, hidden).transpose(1, 0, 2, 3)
        dns = by_rows[..., rows_up : 2 * rows_up, :].reshape(nz * 2, 4, rows_up, hidden).transpose(1, 0, 2, 3)
        ups = ups.reshape(4, dp, -1, hidden).transpose(1, 0, 2, 3)
        dns = dns.reshape(4, dp, -1, hidden).transpose(1, 0, 2, 3)
        outs = by_rows[..., 2 * rows_up :, :].reshape(width, width)

        def reduced(a):
            return lax.psum_scatter(a.astype(F32).reshape(count, -1, a.shape[-1]), BOTH, scatter_dimension=0)

        up_grad, down_grad, out_grad = reduced(ups), reduced(dns).T, reduced(outs)

    g, scaled, l1, pack_b = call(
        adjoint_kernel, seqs,
        [("m", pos), ("s", ga_keep), ("s", ga_recv), ("s", inv_root), ("s", turn), ("s", fq), ("s", ccol)]
        + [("d", a) for a in before_adjoint],
        [
            ("s", feats, BF16), ("s", feats, BF16), ("s", (seqs, 4, 128, 128), F32), ("w", (npack, 128, 128), BF16),
        ],
        us=0.3, name="adjoint",
    )
    behind = [(i, i - 2) for i in range(count) if (i % tensor) >= 2]
    arrived_b = lax.ppermute(pack_b, BOTH, behind)
    dfq, dfk, dva = call(
        local_back_kernel, seqs,
        [("s", fq), ("s", fk), ("s", va), ("s", g), ("s", scaled), ("s", st), ("s", ccol), ("s", crow)],
        [("s", feats, F32), ("s", feats, F32), ("s", feats, F32)],
        us=0.3, name="local_back",
    )
    before_close = []
    if direct:
        x_own, x_far, y_own, y_far = call(
            half_sum_kernel, 0, [("w", a) for a in (x_keep, x_recv, y_keep, y_recv)] + [("d", dfq)],
            [("w", one, BF16)] * 4, us=0.4, name="half_sum",
        )
        x_recv, y_recv = xor_with(x_far, 2, count), xor_with(y_far, 4, count)
        before_close = [x_own]
    *m_pieces, gn_keep, gn_send = call(
        functools.partial(close_kernel, seqs_total=seqs), seqs,
        [("m", pos), ("s", unit), ("w", attend), ("s", fq), ("s", fk), ("s", fqt), ("s", fkt), ("s", va), ("s", dfq),
         ("s", dfk), ("s", dva), ("s", ccol), ("s", ucol), ("w", arrived_b), ("s", l1), ("s", st),
         ("w", wmix), ("w", grad_vec), ("w", maps_back)] + [("d", a) for a in before_close],
        [*[("w", (nz, 32, 896), BF16)] * 4, ("s", (seqs, chunk, width), F32), ("s", (seqs, chunk, width), BF16)],
        scratch=[
            pltpu.VMEM((width, 896), F32), pltpu.VMEM((tokens, 896), BF16), pltpu.VMEM((8, 128), F32),
            pltpu.VMEM((8, width), F32), pltpu.VMEM((width, 896), BF16),
        ],
        us=14.7, name="close", unroll=False,
    )
    if direct:
        g_line = call(
            line_sum_kernel, 0, [("w", a) for a in (x_own, x_recv, y_own, y_recv)] + [("d", gn_keep)],
            [("w", (nrows, hidden), BF16)] * nz, us=0.4, name="line_sum",
        )
        m_parts = from_plane(m_pieces)
    gn_recv = swap_core(gn_send)
    def finish_input(after):
        return call(
            input_kernel, seqs,
            [("s", inputs), ("s", grad_middle), ("s", gn_keep), ("s", gn_recv), ("w", vec)] + [("d", a) for a in after],
            [("s", (seqs, chunk, width), F32), ("w", (8, 128), F32)], us=0.3, name="input_grad",
        )

    if direct:
        m_plane = call(
            mix_sum_kernel, 0, [("w", a) for a in m_parts] + [("d", pause([g_line[0]], 40)), ("d", gn_recv)],
            [("w", (32, 896), BF16)] * nz, us=0.4, name="mix_sum",
        )
        input_grad, input_done = finish_input([m_plane[0]])
        g_parts = [g_line[0]] + [xor_with(g_line[m], 8 * m, count) for m in range(1, nz)]
        up_grad, down_back, out_grad, feed_done = call(
            feed_last_kernel, 0, [("w", a) for a in g_parts],
            [("w", shape, F32) for shape in (up_weight.shape, down_weight.shape[::-1], out_weight.shape, (8, 128))],
            us=0.3, name="feed_last",
        )
        down_grad = down_back.T
        mix_parts = [m_plane[0]] + [xor_with(m_plane[m], 8 * m, count) for m in range(1, nz)]
        m_keep, m_send = call(
            mix_last_kernel, 0, [("m", pos)] + [("w", a) for a in mix_parts] + [("d", feed_done), ("d", input_done)],
            [("w", (mix_weight.shape[0], 896), F32)] * 2, name="mix_last",
        )
        m_recv = swap_core(m_send)
    else:
        input_grad, input_done = finish_input([])
        m_all = jnp.stack(m_pieces).astype(F32).reshape(2, 2, nz, 32, 896)
        mine_rows = m_all.transpose(2, 1, 0, 3, 4).reshape(count, -1, 896)
        keep_part = lax.psum_scatter(mine_rows * jnp.where(first, 1.0, 0.0), BOTH, scatter_dimension=0)
        far_part = lax.psum_scatter(mine_rows * jnp.where(first, 0.0, 1.0), BOTH, scatter_dimension=0)
        m_keep = jnp.where(first, keep_part, far_part)
        m_recv = jnp.where(first, far_part, keep_part)
    if direct:
        mix_grad, gate_back, bias_grad, *per_row = call(
            final_kernel, 0, [("m", pos), ("w", m_keep), ("w", m_recv)],
            [("w", mix_weight.shape, F32), ("w", gate_weight.shape[::-1], F32), ("w", (heads,), F32)]
            + [("w", gain_first.shape, F32)] * 4,
            us=1.2, name="final",
        )
        gate_grad = gate_back.T
    else:
        m_low = jnp.where(first, m_keep, m_recv)
        m_high = jnp.where(first, m_recv, m_keep)
        mix_grad = jnp.concatenate(
            [part[:, 256 * i : 256 * i + 256] for i in range(3) for part in (m_low, m_high)], axis=1
        )
        gate_grad = jnp.concatenate([m_low[:, 768:772], m_high[:, 768:772]], axis=1)
        bias_grad = jnp.concatenate([m[0, 776:780] + m[0, 780:784] for m in (m_low, m_high)])
        per_row = [m_keep[:, 772 + i] + m_recv[:, 772 + i] for i in range(4)]
    return (
        output, input_grad, mix_grad, gate_grad, bias_grad, out_grad,
        *per_row, up_grad, down_grad,
    )


def solution(mesh):
    rows, spread = P(("dp", "tensor"), None), P(("dp", "tensor"))
    tokens = P("dp", "tensor", None)
    in_specs = (
        tokens, tokens, rows, rows, P(), rows, spread, spread, spread, spread, P("dp", "tensor"), P("tensor", "dp"), P(),
    )
    out_specs = (
        tokens, tokens, rows, rows, P(), rows, spread, spread, spread, spread, P("dp", "tensor"), P("tensor", "dp"),
    )
    return jax.shard_map(body, mesh=mesh, in_specs=in_specs, out_specs=out_specs, check_vma=False)
```

```python
import functools

import jax
import jax.numpy as jnp
from jax import lax
from jax.experimental import pallas as pl
from jax.experimental.pallas import tpu as pltpu
from jax.sharding import PartitionSpec as P

BOTH = ("dp", "tensor")
F32 = jnp.float32
BF16 = jnp.bfloat16
EPSILON = 1e-05
DENSITY = 0.3989422804014327
SIN = (9.9999999998e-01, -1.6666666617e-01, 8.3333309689e-03, -1.9840860382e-04, 2.7525224003e-06, -2.3888330913e-08)
COS = (9.9999999978e-01, -4.9999999354e-01, 4.1666636104e-02, -1.3888359409e-03, 2.4760057595e-05, -2.6049626765e-07)

NN = (((1,), (0,)), ((), ()))
NT = (((1,), (1,)), ((), ()))
TN = (((0,), (0,)), ((), ()))


def mm(a, b, dims=NN):
    return lax.dot_general(a, b, dims, preferred_element_type=F32)


def low(a):
    return a.astype(BF16)


def lanes_of(shape):
    return lax.broadcasted_iota(jnp.int32, shape, len(shape) - 1)


def swap_halves(a):
    return pltpu.roll(a, 64, 1)


def sincos(a):
    turns = jnp.floor(a * 0.3183098861837907 + 0.5)
    r = (a - turns * 3.140625) - turns * 9.676535897932e-4
    half = turns * 0.5
    sign = 1.0 - 4.0 * (half - jnp.floor(half))
    r2 = r * r
    s = r * (SIN[0] + r2 * (SIN[1] + r2 * (SIN[2] + r2 * (SIN[3] + r2 * (SIN[4] + r2 * SIN[5])))))
    c = COS[0] + r2 * (COS[1] + r2 * (COS[2] + r2 * (COS[3] + r2 * (COS[4] + r2 * COS[5]))))
    return sign * s, sign * c


def normal_parts(v):
    t = pl.reciprocal(1.0 + 0.23164189 * jnp.abs(v), approx=True)
    bell = jnp.exp(-0.5 * (v * v))
    poly = t * (0.127414796 + t * (-0.142248368 + t * (0.7107068705 + t * (-0.7265760135 + t * 0.5307027145))))
    tail = poly * bell
    return jnp.where(v >= 0.0, 1.0 - tail, tail), DENSITY * bell


def three_parts(a):
    high = a.astype(BF16)
    rest = a - high.astype(F32)
    mid = rest.astype(BF16)
    return high, mid, (rest - mid.astype(F32)).astype(BF16)


def tri_sum(tri, a):
    high, mid, rest = (part.astype(F32) for part in three_parts(a))
    packed = mm(tri, low(high + pltpu.roll(mid, 4, 1) + pltpu.roll(rest, 8, 1)))
    return packed + pltpu.roll(packed, 124, 1) + pltpu.roll(packed, 120, 1)


def norm_of(x):
    mean = jnp.mean(x, axis=-1, keepdims=True)
    centered = x - mean
    inv = lax.rsqrt(jnp.mean(centered * centered, axis=-1, keepdims=True) + EPSILON)
    return centered * inv, inv


def norm_back(s, unit, inv):
    return inv * (
        s
        - jnp.mean(s, axis=-1, keepdims=True)
        - unit * jnp.mean(s * unit, axis=-1, keepdims=True)
    )


def chip_row(pos, mz, mx, my):
    return (((pos[0] ^ mz) * 2 + (pos[1] ^ mx)) * 2 + (pos[2] ^ my)) * 32


def lower_tri(n):
    row = lax.broadcasted_iota(jnp.int32, (n, n), 0)
    col = lax.broadcasted_iota(jnp.int32, (n, n), 1)
    return row, col


def unpack_states(pack, b, zcols, last=65):
    lane = lanes_of((128, 128))
    out = []
    for p in range(2):
        both = pack[2 * b + p].astype(F32)
        for h, mat in ((2 * p, both), (2 * p + 1, swap_halves(both))):
            z = jnp.sum(jnp.where(lane == 4 * b + h, zcols, 0.0), axis=1, keepdims=True)
            out.append(jnp.where(lane < 64, mat, jnp.where(lane <= last, z, 0.0)))
    return out


def pack_states(states, pack_o, b, last, split=False):
    lane = lanes_of((128, 128))
    zcols = jnp.where(b == 0, 0.0, pack_o[last].astype(F32))

    def sum_of(s):
        return s[:, 64:65] + s[:, 65:66] if split else s[:, 64:65]

    for p in range(2):
        s0, s1 = states[2 * p], states[2 * p + 1]
        pack_o[2 * b + p] = jnp.where(lane < 64, s0, swap_halves(s1)).astype(BF16)
        zcols = jnp.where(lane == 4 * b + 2 * p, sum_of(s0), zcols)
        zcols = jnp.where(lane == 4 * b + 2 * p + 1, sum_of(s1), zcols)
    pack_o[last] = zcols.astype(BF16)


def pack_kernel(pos, mix, columns, keep_o, send_o):
    width = mix.shape[1] // 6
    rows = mix.shape[0]
    table = jnp.concatenate(
        [columns[...].astype(F32), jnp.zeros((128 - columns.shape[0], rows), F32)], axis=0
    )
    sides = jnp.concatenate([table, jnp.zeros((128, 128 - rows), F32)], axis=1).T[0:rows]
    lane = lanes_of(sides.shape)
    moved = pltpu.roll(sides, 124, 1)
    halves = []
    for s, block in ((0, jnp.where(lane < 4, sides, moved)), (1, moved)):
        parts = [mix[:, (2 * i + s) * width : (2 * i + s + 1) * width] for i in range(3)]
        halves.append(jnp.concatenate(parts + [low(jnp.where(lane < 8, block, 0.0))], axis=1))
    first = pos[3] == 0
    keep_o[...] = jnp.where(first, halves[0], halves[1])
    send_o[...] = jnp.where(first, halves[1], halves[0])


def prepare_kernel(b, pos, own, oth, cot, unit_o, cott_o):
    chunk = own.shape[1]
    first = pos[3] == 0
    mine, theirs = own[0], oth[0]
    for j in range(2):
        unit, _ = norm_of(jnp.where(first == (j == 0), mine, theirs).astype(F32))
        unit_o[0, j * chunk : (j + 1) * chunk] = unit
    cott_o[0] = low(cot[0].astype(F32).T)


def feature_parts(angles, lane):
    s, c = sincos(angles)
    out = []
    turned_s, turned_c = swap_halves(s), swap_halves(c)
    for f, turned in (
        (jnp.where(lane < 64, s, turned_c), jnp.where(lane < 64, c, turned_s)),
        (jnp.where(lane < 64, turned_s, c), jnp.where(lane < 64, turned_c, s)),
    ):
        high = low(f)
        out.append((high, low(f - high.astype(F32)), low(turned)))
    return out


def query_kernel(b, a, wmix, maps, fq_o, fql_o, fqt_o):
    chunk = a.shape[1] // 2
    lane = lanes_of((chunk, 128))
    spans = [slice(j * chunk, (j + 1) * chunk) for j in range(2)]
    mixed = [low(mm(a[0, rows], wmix[:, 0:256])) for rows in spans]
    angles = [[mm(m[:, 128 * p : 128 * p + 128], maps[p]) for p in range(2)] for m in mixed]
    for j, rows in enumerate(spans):
        for p in range(2):
            for i, (high, rest, turned) in enumerate(feature_parts(angles[j][p], lane)):
                fq_o[0, 2 * p + i, rows], fql_o[0, 2 * p + i, rows], fqt_o[0, 2 * p + i, rows] = high, rest, turned


def project_kernel(
    b, pos, units, w0, w1, w2, w3, bias, maps,
    a_o, fk_o, fkl_o, fkt_o, va_o, ccol_o, ucol_o, crow_o, smid_o, pack_o, wmix_o, vec_o, vbar_o,
    w_s, sems,
):
    chunk = units.shape[1] // 2

    @pl.when(b == 0)
    def _():
        copies = [
            pltpu.make_async_copy(piece, w_s.at[:, pos[1] ^ mx, pos[2] ^ my], sems.at[2 * my + mx])
            for piece, (my, mx) in ((w0, (0, 0)), (w1, (0, 1)), (w2, (1, 0)), (w3, (1, 1)))
        ]
        for copy in copies:
            copy.start()
        for copy in copies:
            copy.wait()
        wmix_o[...] = w_s[...].reshape(wmix_o.shape)
        vec_o[...] = wmix_o[:, 768:896].astype(F32).T[0:8]
        vbar_o[...] = mm(jnp.broadcast_to(vec_o[5:6], vec_o.shape).astype(BF16), wmix_o[:, 512:768])

    gain, shift = vec_o[4:5], vec_o[5:6]
    row, col = lower_tri(chunk)
    tri = jnp.where(row >= col, 1.0, 0.0).astype(BF16)
    lane = lanes_of((chunk, 128))
    spans = [slice(j * chunk, (j + 1) * chunk) for j in range(2)]
    attends = [low(units[0, rows] * gain + shift) for rows in spans]
    for a, rows in zip(attends, spans):
        a_o[0, rows] = a
    wide = [mm(a, wmix_o[:, 256:896]) for a in attends]
    mixed = [low(m[:, 0:512]) for m in wide]
    angles = [[mm(m[:, 128 * p : 128 * p + 128], maps[p]) for p in range(2)] for m in mixed]
    douts, ends = [], []
    for j, rows in enumerate(spans):
        logits = wide[j][:, 512:640] + bias[...]
        e = jnp.exp(-jnp.abs(logits))
        w = 1.0 + e
        log1 = jnp.where(w == 1.0, e, jnp.log(w) * (e / jnp.where(w == 1.0, 1.0, w - 1.0)))
        log_gate = jnp.where(lane < 4, jnp.minimum(logits, 0.0) - log1, 0.0)
        fresh = jnp.where(lane < 4, jnp.where(logits >= 0.0, e, 1.0) / w, 0.0)
        cum = jnp.where(lane < 4, tri_sum(tri, log_gate), 0.0)
        ccol_o[0, rows] = cum
        ucol_o[0, rows] = fresh
        crow_o[0, j] = (cum + pltpu.roll(fresh, 4, 1)).T[0:8]
        ends.append(cum[chunk - 1 : chunk])
        douts.append(jnp.exp(ends[j] - cum) * fresh)
    one = jnp.where((lane == 64) | (lane == 65), 1.0, 0.0)
    shares = [[None] * 4, [None] * 4]
    for j, rows in enumerate(spans):
        for p in range(2):
            v = mixed[j][:, 256 + 128 * p : 384 + 128 * p].astype(F32) - vbar_o[0:1, 128 * p : 128 * p + 128]
            for h, vh in ((2 * p, v), (2 * p + 1, swap_halves(v))):
                aug = jnp.where(lane < 64, vh, one)
                va_o[0, h, rows] = low(aug)
                shares[j][h] = low(aug * douts[j][:, h : h + 1])
    locals_ = [[None] * 4, [None] * 4]
    for j, rows in enumerate(spans):
        for p in range(2):
            parts = feature_parts(angles[j][p], lane)
            for h in (2 * p, 2 * p + 1):
                fk_o[0, h, rows], fkl_o[0, h, rows], fkt_o[0, h, rows] = parts[h - 2 * p]
                locals_[j][h] = mm(parts[h - 2 * p][0], shares[j][h], TN)
    states = []
    for h in range(4):
        smid_o[0, h] = locals_[0][h]
        states.append(locals_[0][h] * jnp.exp(ends[1][:, h : h + 1]) + locals_[1][h])
    pack_states(states, pack_o, b, pack_o.shape[0] - 1)


def weights_of(ccol, ucol_row, crow, row, col):
    gap = jnp.minimum(ccol - crow, 0.0)
    return jnp.where(row >= col, jnp.exp(gap), 0.0) * ucol_row


def pairs_of(chunk):
    return [(j, h, slice(j * chunk, (j + 1) * chunk)) for j in range(2) for h in range(4)]


def scores(fq, fk, fql, fkl, h, rows):
    q, k = fq[0, h, rows], fk[0, h, rows]
    return mm(
        jnp.concatenate([q, fql[0, h, rows], q], axis=1), jnp.concatenate([k, k, fkl[0, h, rows]], axis=1), NT
    )


def local_kernel(b, fq, fk, fql, fkl, va, ccol, crow, o_o):
    chunk = crow.shape[3]
    row, col = lower_tri(chunk)
    pairs = pairs_of(chunk)
    qk = [scores(fq, fk, fql, fkl, h, rows) for j, h, rows in pairs]
    attn = [
        low(q * weights_of(ccol[0, rows, h : h + 1], crow[0, j, 4 + h : 5 + h], crow[0, j, h : h + 1], row, col))
        for q, (j, h, rows) in zip(qk, pairs)
    ]
    outs = [mm(a, va[0, h, rows]) for a, (j, h, rows) in zip(attn, pairs)]
    for out, (j, h, rows) in zip(outs, pairs):
        o_o[0, h, rows] = out


def mean_of(vbar, h):
    pair = vbar[:, 128 * (h // 2) : 128 * (h // 2) + 128]
    return (pair if h % 2 == 0 else swap_halves(pair))[0:1]


def finish_kernel(b, pos, o_loc, fq, ccol, pack, smid, vbar, inv_o, turn_o, st_o, keep_o, send_o):
    chunk = ccol.shape[1] // 2
    zcols = pack[pack.shape[0] - 1].astype(F32)
    states = unpack_states(pack, b, zcols)
    lane = lanes_of((chunk, 128))
    cend = ccol[0, chunk - 1 : chunk]
    pairs = pairs_of(chunk)
    near = []
    for h in range(4):
        near.append(low(states[h]))
        near.append(low(jnp.exp(cend[:, h : h + 1]) * states[h] + smid[0, h]))
        for j in range(2):
            st_o[0, h, j] = near[2 * h + j]
    inter = [mm(fq[0, h, rows], near[2 * h + j]) for j, h, rows in pairs]
    outs = [
        o_loc[0, h, rows] + jnp.exp(ccol[0, rows, h : h + 1]) * part for part, (j, h, rows) in zip(inter, pairs)
    ]
    dens = [jnp.broadcast_to(o[:, 64:65], o.shape) for o in outs]
    invs = [lax.rsqrt(den * den + 1.0) for den in dens]
    att = [[None] * 4, [None] * 4]
    for o, den, inv, (j, h, rows) in zip(outs, dens, invs, pairs):
        mean = mean_of(vbar, h)
        att[j][h] = (o + den * mean) * inv
        inv_o[0, h, rows] = jnp.where(lane < 64, inv, 0.0)
        turn_o[0, h, rows] = mean - den * inv * att[j][h]
    first = pos[3] == 0
    for p in range(2):
        both = [
            jnp.where(lane < 64, att[j][2 * p], swap_halves(att[j][2 * p + 1])) for j in range(2)
        ]
        keep_o[0, :, 128 * p : 128 * p + 128] = jnp.where(first, both[0], both[1]).astype(BF16)
        send_o[0, :, 128 * p : 128 * p + 128] = jnp.where(first, both[1], both[0]).astype(BF16)


def dp_of(pos, mz, mx):
    return (pos[0] ^ mz) * 2 + (pos[1] ^ mx)


def feed_chunks(pos, near, far, cot, cott, feed, feedt, target, up_s, dn_s, hid_s, gp_s, big_s):
    seqs, chunk, _ = cot.shape
    nz = far.shape[0]
    width, both = up_s.shape
    hidden = both // 2
    rows_up = width // (2 * nz)
    for my in range(2):
        cols = slice(my * hidden, (my + 1) * hidden)
        for mx in range(2):
            k = 2 * my + mx
            piece = far if k == 3 else near.at[pl.ds(k * nz, nz)]
            for z in range(nz):
                at = pl.multiple_of((2 * z + (pos[1] ^ mx)) * rows_up, rows_up)
                up_s[pl.ds(at, rows_up), cols] = piece[z, 0:rows_up]
                dn_s[pl.ds(at, rows_up), cols] = piece[z, rows_up : 2 * rows_up]

    def scatter(offset):
        for my in range(2):
            cols = slice(my * hidden, (my + 1) * hidden)
            for mx in range(2):
                for mz in range(nz):
                    at = pl.multiple_of(dp_of(pos, mz, mx) * rows_up, rows_up)
                    target[my, mx, mz, offset : offset + rows_up, :] = big_s[pl.ds(at, rows_up), cols]

    spans = [slice(r * chunk, (r + 1) * chunk) for r in range(seqs)]
    outs, grads = [], []
    pres = [mm(feed[rows], up_s[...]) for rows in spans]
    ghs = [mm(cot[r], dn_s[...]) for r in range(seqs)]
    for r, rows in enumerate(spans):
        cdf, pdf = normal_parts(pres[r])
        hid_s[rows] = low(pres[r] * cdf)
        gp_s[rows] = low(ghs[r] * (cdf + pres[r] * pdf))
    for rows in spans:
        outs.append(mm(hid_s[rows], dn_s[...], NT))
        grads.append(mm(gp_s[rows], up_s[...], NT))
    big_s[...] = low(mm(feedt[...], gp_s[...]))
    scatter(0)
    big_s[...] = low(mm(jnp.concatenate([cott[r] for r in range(seqs)], axis=1), hid_s[...]))
    scatter(rows_up)
    return outs, grads


def feed_first_kernel(
    pos, akeep, arecv, x, cot, cott, vec, near_own, far_own, near, far,
    gsend_o, acc_o, gf_o, mid_o, feed_o, feedt_o, att_o, ow_o,
    up_s, dn_s, hid_s, gp_s, big_s,
):
    seqs, chunk, _ = x.shape
    nz = far.shape[0]
    rows_up = up_s.shape[0] // (2 * nz)
    first = pos[3] == 0
    for mc, (some, rest) in enumerate(((near_own, far_own), (near, far))):
        for my in range(2):
            t = (pos[2] ^ my) * 2 + (pos[3] ^ mc)
            for mx in range(2):
                k = 2 * my + mx
                for z in range(nz):
                    at = pl.multiple_of(((2 * z + (pos[1] ^ mx)) * 4 + t) * 16, 16)
                    source = rest if k == 3 else some.at[pl.ds(k * nz, nz)]
                    ow_o[pl.ds(at, 16), :] = source[z, 2 * rows_up :]
    gain, shift = vec[6:7], vec[7:8]
    for r in range(seqs):
        rows = slice(r * chunk, (r + 1) * chunk)
        mine, theirs = akeep[r], arecv[r]
        att = jnp.concatenate([jnp.where(first, mine, theirs), jnp.where(first, theirs, mine)], axis=1)
        att_o[rows] = att
        mid = x[r].astype(F32) + mm(att, ow_o[...])
        mid_o[rows] = mid
        unit, _ = norm_of(mid)
        feed = unit * gain + shift
        feed_o[rows] = low(feed)
        feedt_o[:, rows] = low(feed.T)
    outs, grads = feed_chunks(pos, near, far, cot, cott, feed_o, feedt_o, gsend_o, up_s, dn_s, hid_s, gp_s, big_s)
    for r, (out, grad) in enumerate(zip(outs, grads)):
        acc_o[r * chunk : (r + 1) * chunk] = out
        gf_o[r * chunk : (r + 1) * chunk] = grad


def feed_second_kernel(
    pos, cot, cott, vec, near, far, acc, gf_in, mid_in, feed, feedt, att, ow,
    out_o, gm_o, gak_o, gas_o, gkeep_o, okeep_o, osend_o, gv_o,
    up_s, dn_s, hid_s, gp_s, gb_s, big_s,
):
    seqs, chunk, width = cot.shape
    nz = far.shape[0]
    first = pos[3] == 0
    outs, grads = feed_chunks(pos, near, far, cot, cott, feed, feedt, gkeep_o, up_s, dn_s, hid_s, gp_s, big_s)
    gain = vec[6:7]
    gain_sum = jnp.zeros((1, width), F32)
    shift_sum = jnp.zeros((1, width), F32)
    for r in range(seqs):
        rows = slice(r * chunk, (r + 1) * chunk)
        mid = mid_in[rows]
        out_o[r] = low(mid + (acc[rows] + outs[r]))
        unit, inv = norm_of(mid)
        gf = gf_in[rows] + grads[r]
        gain_sum += jnp.sum(gf * unit, axis=0, keepdims=True)
        shift_sum += jnp.sum(gf, axis=0, keepdims=True)
        gm = cot[r].astype(F32) + norm_back(gf * gain, unit, inv)
        gm_o[r] = gm
        gb = low(gm)
        gb_s[rows] = gb
        ga = low(mm(gb, ow[...], NT))
        half = width // 2
        gak_o[r] = jnp.where(first, ga[:, :half], ga[:, half:])
        gas_o[r] = jnp.where(first, ga[:, half:], ga[:, :half])
    gv_o[...] = jnp.concatenate([gain_sum, shift_sum, jnp.zeros((6, width), F32)], axis=0)
    big_s[:, 0:width] = low(mm(att[...], gb_s[...], TN))
    for mc, target in ((0, okeep_o), (1, osend_o)):
        for my in range(2):
            t = (pos[2] ^ my) * 2 + (pos[3] ^ mc)
            for mx in range(2):
                for mz in range(nz):
                    at = pl.multiple_of((dp_of(pos, mz, mx) * 4 + t) * 16, 16)
                    target[my, mx, mz] = big_s[pl.ds(at, 16), 0:width]


def adjoint_kernel(b, pos, gak, gar, inv_root, turn, fq, ccol, g_o, scaled_o, l1_o, pack_o):
    chunk = ccol.shape[1] // 2
    lane = lanes_of((chunk, 128))
    first = pos[3] == 0
    pairs = pairs_of(chunk)
    gas = []
    for j in range(2):
        for p in range(2):
            cols = slice(128 * p, 128 * p + 128)
            pair = jnp.where(first == (j == 0), gak[0, :, cols], gar[0, :, cols]).astype(F32)
            gas += [pair, swap_halves(pair)]
    gns = [low(ga * inv_root[0, h, rows]).astype(F32) for ga, (j, h, rows) in zip(gas, pairs)]
    gds = [
        jnp.sum(gn * turn[0, h, rows], axis=1, keepdims=True) for gn, (j, h, rows) in zip(gns, pairs)
    ]
    scaled = []
    for gn, gd, (j, h, rows) in zip(gns, gds, pairs):
        gd = jnp.broadcast_to(gd, gn.shape)
        high = low(gd).astype(F32)
        g = jnp.where(lane == 64, high, jnp.where(lane == 65, gd - high, gn))
        g_o[0, h, rows] = low(g)
        scaled.append(low(g * jnp.exp(ccol[0, rows, h : h + 1])))
        scaled_o[0, h, rows] = scaled[-1]
    parts = [mm(fq[0, h, rows], g, TN) for g, (j, h, rows) in zip(scaled, pairs)]
    states = []
    for h in range(4):
        l1_o[0, h] = parts[4 + h]
        states.append(parts[h] + jnp.exp(ccol[0, chunk - 1 : chunk, h : h + 1]) * parts[4 + h])
    pack_states(states, pack_o, b, pack_o.shape[0] - 1, split=True)


def local_back_kernel(b, fq, fk, va, g, scaled, st, ccol, crow, dfq_o, dfk_o, dva_o):
    chunk = crow.shape[3]
    row, col = lower_tri(chunk)
    pairs = pairs_of(chunk)
    for half in (pairs[:4], pairs[4:]):
        qk = [mm(fq[0, h, rows], fk[0, h, rows], NT) for j, h, rows in half]
        da = [mm(g[0, h, rows], va[0, h, rows], NT) for j, h, rows in half]
        inter = [mm(scaled[0, h, rows], st[0, h, j], NT) for j, h, rows in half]
        attn, dp = [], []
        for q, d, (j, h, rows) in zip(qk, da, half):
            w = weights_of(ccol[0, rows, h : h + 1], crow[0, j, 4 + h : 5 + h], crow[0, j, h : h + 1], row, col)
            attn.append(low(q * w))
            dp.append(low(d * w))
        dva = [mm(a, g[0, h, rows], TN) for a, (j, h, rows) in zip(attn, half)]
        dfk = [mm(d, fq[0, h, rows], TN) for d, (j, h, rows) in zip(dp, half)]
        dfq = [mm(d, fk[0, h, rows]) for d, (j, h, rows) in zip(dp, half)]
        for i, (j, h, rows) in enumerate(half):
            dfq_o[0, h, rows] = dfq[i] + inter[i]
            dfk_o[0, h, rows] = dfk[i]
            dva_o[0, h, rows] = dva[i]


def close_kernel(
    b, pos, units, attend, fq, fk, fqt, fkt, va, dfq, dfk, dva, ccol, ucol, pack, l1, st, wmix, gv, back,
    m00_o, m01_o, m10_o, m11_o, gnk_o, gns_o,
    acc_s, gm_s, gate_s, vsum_s, big_s,
    *, seqs_total,
):
    seqs = seqs_total
    chunk = units.shape[1] // 2
    nz = m00_o.shape[0]
    lane = lanes_of((chunk, 128))
    row, col = lower_tri(chunk)
    upper = jnp.where(row <= col, 1.0, 0.0).astype(BF16)
    zcols = pack[pack.shape[0] - 1].astype(F32)
    arrived = unpack_states(pack, b, zcols, last=64)
    wide = lanes_of((128, 128))

    @pl.when(b == 0)
    def _():
        gate_s[...] = jnp.zeros_like(gate_s)
        vsum_s[...] = jnp.zeros_like(vsum_s)

    pairs = pairs_of(chunk)
    spans = [slice(j * chunk, (j + 1) * chunk) for j in range(2)]
    cums = [ccol[0, rows] for rows in spans]
    freshs = [ucol[0, rows] for rows in spans]
    douts = [jnp.exp(cum[chunk - 1 : chunk] - cum) * fresh for cum, fresh in zip(cums, freshs)]
    nears = []
    for j, h, rows in pairs:
        adj = arrived[h]
        if j == 0:
            adj = l1[0, h] + jnp.exp(ccol[0, 2 * chunk - 1 : 2 * chunk, h : h + 1]) * adj
        zs = adj[:, 64:65] + adj[:, 65:66]
        high = low(zs).astype(F32)
        nears.append(low(jnp.where(wide == 64, high, jnp.where(wide == 65, zs - high, adj))))
    dk_fars = [mm(va[0, h, rows], near, NT) for near, (j, h, rows) in zip(nears, pairs)]
    dv_fars = [mm(fk[0, h, rows], near) for near, (j, h, rows) in zip(nears, pairs)]
    kds, qds, levels = [], [], []
    pqs, pks, dvs = [], [], []
    for i, (j, h, rows) in enumerate(pairs):
        d = douts[j][:, h : h + 1]
        keys, queries = fk[0, h, rows].astype(F32), fq[0, h, rows].astype(F32)
        dk_far = d * dk_fars[i]
        dk = dk_far + dfk[0, h, rows]
        dq = dfq[0, h, rows]
        kds.append(jnp.sum(keys * dk, axis=1, keepdims=True))
        qds.append(jnp.sum(queries * dq, axis=1, keepdims=True))
        passed = st[0, h, j].astype(F32) * nears[i].astype(F32)
        passed = jnp.sum(jnp.sum(passed, axis=0, keepdims=True), axis=1, keepdims=True)
        total = jnp.sum(jnp.sum(keys * dk_far, axis=0, keepdims=True), axis=1, keepdims=True)
        levels.append(total + jnp.exp(cums[j][chunk - 1 : chunk, h : h + 1]) * passed)
        dvs.append(dva[0, h, rows] + d * dv_fars[i])
        pks.append(low(dk * fkt[0, h, rows].astype(F32)))
        pqs.append(low(dq * fqt[0, h, rows].astype(F32)))
    grads = [
        [mm(jnp.concatenate(ps[4 * j + 2 * p : 4 * j + 2 * p + 2], axis=1), back[p]) for ps in (pqs, pks) for p in range(2)]
        for j in range(2)
    ]
    bias_sum = jnp.zeros((1, 128), F32)
    gms = []
    for j in range(2):
        kd = qd = jnp.zeros((chunk, 128), F32)
        level = jnp.zeros((1, 128), F32)
        for h in range(4):
            kd = jnp.where(lane == h, kds[4 * j + h], kd)
            qd = jnp.where(lane == h, qds[4 * j + h], qd)
            level = jnp.where(lanes_of((1, 128)) == h, levels[4 * j + h], level)
        dlog = tri_sum(upper, qd - kd) + level
        dlogit = jnp.where(lane < 4, freshs[j] * dlog - (1.0 - freshs[j]) * kd, 0.0)
        bias_sum += jnp.sum(dlogit, axis=0, keepdims=True)
        values = [jnp.where(lane < 64, dvs[4 * j + 2 * p], swap_halves(dvs[4 * j + 2 * p + 1])) for p in range(2)]
        gm = jnp.concatenate([low(x) for x in (*grads[j], *values, dlogit)], axis=1)
        gm_s[pl.ds(pl.multiple_of((2 * b + j) * chunk, chunk), chunk), :] = gm
        gms.append(gm)
    normed = [mm(gm, wmix[...], NT) for gm in gms]
    vsum_s[0:1] += sum(jnp.sum(n * units[0, rows], axis=0, keepdims=True) for n, rows in zip(normed, spans))
    vsum_s[1:2] += sum(jnp.sum(n, axis=0, keepdims=True) for n in normed)
    first = pos[3] == 0
    gnk_o[0] = jnp.where(first, normed[0], normed[1])
    gns_o[0] = low(jnp.where(first, normed[1], normed[0]))
    gate_s[0:1] += bias_sum

    @pl.when(b == seqs - 1)
    def _():
        width = acc_s.shape[0]
        acc_s[...] = mm(attend[...].reshape(gm_s.shape[0], width), gm_s[...], TN)
        table = jnp.concatenate(
            [jnp.zeros((4, width), F32), vsum_s[0:2], gv[0:2], jnp.zeros((120, width), F32)], axis=0
        ).T
        total = gate_s[0:1]
        high = low(total).astype(F32)
        rest = jnp.broadcast_to(total - high, (8, 128))
        both = pltpu.roll(jnp.broadcast_to(high, (8, 128)), 8, 1) + pltpu.roll(rest, 12, 1)
        biases = jnp.broadcast_to(both[0:1], (width, 128))
        side = jnp.where(lanes_of((width, 128)) < 4, acc_s[:, 768:896], table) + biases
        big_s[:, 0:768] = acc_s[:, 0:768].astype(BF16)
        big_s[:, 768:896] = side.astype(BF16)
        for my in range(2):
            for mx in range(2):
                for mz in range(nz):
                    at = pl.multiple_of(chip_row(pos, mz, mx, my), 32)
                    (m00_o, m01_o, m10_o, m11_o)[2 * my + mx][mz] = big_s[pl.ds(at, 32), :]


def final_kernel(pos, keep, recv, mix_o, gate_o, bias_o, *vec_o):
    first = pos[3] == 0
    mine, theirs = keep[...], recv[...]
    halves = (jnp.where(first, mine, theirs), jnp.where(first, theirs, mine))
    width = mix_o.shape[1] // 6
    for i in range(3):
        for s in range(2):
            mix_o[:, (2 * i + s) * width : (2 * i + s + 1) * width] = halves[s][:, i * width : (i + 1) * width]
    sides = [half[:, 3 * width :] for half in halves]
    lane = lanes_of(sides[0].shape)
    both = jnp.concatenate([sides[0] + sides[1], sides[0], sides[1], jnp.zeros((80, 128), F32)], axis=0).T
    gate_o[0:4] = both[0:4, 16:32]
    gate_o[4:8] = both[0:4, 32:48]
    for i, out in enumerate(vec_o):
        out[...] = both[4 + i, 0:16]
    sums = [side[0:8] + pltpu.roll(side[0:8], 124, 1) for side in sides]
    row = jnp.where(lane[0:8] < 4, pltpu.roll(sums[0], 120, 1), pltpu.roll(sums[1], 124, 1))
    bias_o[...] = row[0, 0:8]


def input_kernel(b, x, gm, keep, recv, vec, o, done_o):
    done_o[...] = jnp.zeros_like(done_o)
    unit, inv = norm_of(x[0].astype(F32))
    grad = keep[0] + recv[0].astype(F32)
    o[0] = gm[0] + norm_back(grad * vec[4:5], unit, inv)


def hold_kernel(*refs):
    sems = refs[-1]
    count = (len(refs) - 1) // 2
    copies = [
        pltpu.make_async_copy(refs[i], refs[count + i], sems.at[i]) for i in range(count)
    ]
    for copy in copies:
        copy.start()
    for copy in copies:
        copy.wait()


def halves_kernel(by_x, by_y, x_half, y_half, sems):
    half = x_half.shape[0]
    copies = [
        pltpu.make_async_copy(by_x.at[pl.ds(0, half)], x_half, sems.at[0]),
        pltpu.make_async_copy(by_y.at[pl.ds(half, half)], y_half, sems.at[1]),
    ]
    for copy in copies:
        copy.start()
    for copy in copies:
        copy.wait()


def gather_kernel(*refs):
    parts, out, sems = refs[:-2], refs[-2], refs[-1]
    copies, at = [], 0
    for i, part in enumerate(parts):
        copies.append(pltpu.make_async_copy(part, out.at[pl.ds(at, part.shape[0])], sems.at[i]))
        at += part.shape[0]
    for copy in copies:
        copy.start()
    for copy in copies:
        copy.wait()


def pause_kernel(out):
    out[...] = jnp.zeros_like(out)


def join_kernel(pos, *refs, axis):
    parts, out, sems = refs[:-2], refs[-2], refs[-1]
    copies = [
        pltpu.make_async_copy(part, out.at[pos[axis] ^ i], sems.at[i]) for i, part in enumerate(parts)
    ]
    for copy in copies:
        copy.start()
    for copy in copies:
        copy.wait()


def pair_sum_kernel(keep, recv, okeep, orecv, x_keep, x_send, y_keep, y_send):
    half = x_keep.shape[1]
    rows = keep.shape[3]
    first, second = slice(0, half), slice(half, 2 * half)
    for i in range(2):
        for my, mx, zs, out in ((i, 0, first, x_keep), (i, 1, first, x_send), (0, i, second, y_keep), (1, i, second, y_send)):
            out[i, :, 0:rows] = low(keep[my, mx, zs].astype(F32) + recv[my, mx, zs].astype(F32))
            out[i, :, rows:] = low(okeep[my, mx, zs].astype(F32) + orecv[my, mx, zs].astype(F32))


def half_sum_kernel(x_keep, x_recv, y_keep, y_recv, x_own, x_far, y_own, y_far):
    for keep, recv, own, far in ((x_keep, x_recv, x_own, x_far), (y_keep, y_recv, y_own, y_far)):
        for i, out in ((0, own), (1, far)):
            out[...] = low(keep[i].astype(F32) + recv[i].astype(F32))


def line_sum_kernel(x_own, x_recv, y_own, y_recv, *outs):
    half = x_own.shape[0]
    for i in range(half):
        outs[i][...] = low(x_own[i].astype(F32) + x_recv[i].astype(F32))
        outs[half + i][...] = low(y_own[i].astype(F32) + y_recv[i].astype(F32))


def sum_of_four(refs):
    a, b, c, d = (ref[...].astype(F32) for ref in refs)
    return (a + b) + (c + d)


def mix_sum_kernel(m0, m1, m2, m3, *outs):
    total = sum_of_four((m0, m1, m2, m3))
    side = total[..., 768:896]
    rest = side - low(side).astype(F32)
    lane = lanes_of(side.shape)
    moved = jnp.where((lane >= 12) & (lane < 16), side + pltpu.roll(rest, 4, side.ndim - 1), side)
    for i, out in enumerate(outs):
        out[:, 0:768] = low(total[i, :, 0:768])
        out[:, 768:896] = low(moved[i])


def feed_last_kernel(a, b, c, d, up_o, down_o, out_o, done_o):
    done_o[...] = jnp.zeros_like(done_o)
    total = sum_of_four((a, b, c, d))
    rows = up_o.shape[0]
    up_o[...] = total[0:rows]
    down_o[...] = total[rows : 2 * rows]
    out_o[...] = total[2 * rows :]


def mix_last_kernel(pos, a, b, c, d, keep_o, send_o):
    total = sum_of_four((a, b, c, d))
    rows = keep_o.shape[0]
    first = pos[3] == 0
    keep_o[...] = jnp.where(first, total[:rows], total[rows:])
    send_o[...] = jnp.where(first, total[rows:], total[:rows])


def call(kernel, steps, ins, outs, scratch=(), us=1.0, name=None, limit=12, unroll=False):
    def spec(kind):
        if kind in "da":
            return pl.BlockSpec(memory_space=pl.ANY)
        return pl.BlockSpec(memory_space=pltpu.SMEM if kind == "m" else pltpu.VMEM)

    kinds = [kind for kind, _ in ins]
    out_kinds = [kind for kind, _, _ in outs]
    all_kinds = kinds + out_kinds + ["w"] * len(scratch)

    def run(*refs):
        used = [(kind, ref) for kind, ref in zip(all_kinds, refs) if kind != "d"]
        if not steps:
            kernel(*[ref for _, ref in used])
            return

        def one(b, carry):
            kernel(b, *[ref.at[pl.ds(b, 1)] if kind == "s" else ref for kind, ref in used])
            return carry

        lax.fori_loop(0, steps, one, 0, unroll=unroll)

    return pl.pallas_call(
        run,
        in_specs=[spec(kind) for kind in kinds],
        out_specs=[spec(kind) for kind in out_kinds],
        out_shape=[jax.ShapeDtypeStruct(shape, dtype) for _, shape, dtype in outs],
        scratch_shapes=list(scratch),
        compiler_params=pltpu.CompilerParams(vmem_limit_bytes=limit * 1024 * 1024),
        cost_estimate=pl.CostEstimate(flops=int(us * 1.15e9), bytes_accessed=0, transcendentals=0),
        name=name,
    )(*[a for _, a in ins])


def xor_with(a, mask, count):
    return lax.ppermute(a, BOTH, [(i, i ^ mask) for i in range(count)])


def body(
    inputs, cotangent, mix_weight, gate_weight, gate_bias, out_weight, gain_first, shift_first, gain_second,
    shift_second, up_weight, down_weight, random_maps,
):
    dp, tensor = lax.axis_size("dp"), lax.axis_size("tensor")
    count = dp * tensor
    place_dp, place_t = lax.axis_index("dp"), lax.axis_index("tensor")
    seqs, chunk, width = inputs.shape
    heads, head = random_maps.shape[0], random_maps.shape[1]
    hidden = up_weight.shape[1]
    core = place_t % 2
    first = core == 0
    direct = dp == 8
    nz = 4
    if direct:
        pos = jnp.stack([place_dp // 2, place_dp % 2, place_t // 2, core]).astype(jnp.int32)
    else:
        pos = jnp.stack([jnp.zeros_like(core)] * 3 + [core]).astype(jnp.int32)
    swap_core = functools.partial(xor_with, mask=1, count=count)

    def mix_pack(mix_w, gate_w, vecs):
        rows = mix_w.shape[0]
        split = mix_w.reshape(rows, 3, 2, width // 2)
        sides = [v[:, None] for v in vecs]
        pad = jnp.zeros((rows, 120), BF16)
        return [
            jnp.concatenate(
                [split[:, 0, s], split[:, 1, s], split[:, 2, s], gate_w[:, 4 * s : 4 * s + 4]] + sides + [pad], axis=1
            )
            for s in range(2)
        ]

    def join(parts, axis, after=()):
        (out,) = call(
            functools.partial(join_kernel, axis=axis), 0, [("m", pos)] + [("a", a) for a in parts] + [("d", a) for a in after],
            [("w", (len(parts), *parts[0].shape), parts[0].dtype)],
            scratch=[pltpu.SemaphoreType.DMA((len(parts),))], name="join",
        )
        return out

    def pause(after, us):
        (out,) = call(
            pause_kernel, 0, [("d", a) for a in after], [("w", (8, 128), F32)], us=us, name="pause",
        )
        return out

    def from_plane(pieces):
        return [pieces[0], xor_with(pieces[1], 4, count), xor_with(pieces[2], 2, count), xor_with(pieces[3], 6, count)]

    other_in = swap_core(inputs)
    vectors = (gain_first, shift_first, gain_second, shift_second)
    long = 2 * chunk
    unit, cot_t = call(
        prepare_kernel, seqs, [("m", pos), ("s", inputs), ("s", other_in), ("s", cotangent)],
        [("s", (seqs, long, width), F32), ("s", (seqs, width, chunk), BF16)], us=2.5, name="prepare",
    )
    if direct:
        rows = mix_weight.shape[0]
        columns = jnp.pad(gate_weight.T, ((0, 16 - heads), (0, 0)))
        place = lax.broadcasted_iota(jnp.int32, columns.shape, 0)
        for i, v in enumerate(vectors):
            columns = jnp.where(place == heads + i, lax.broadcast_in_dim(v, columns.shape, (1,)), columns)
        keep, send = call(
            pack_kernel, 0, [("m", pos), ("w", mix_weight), ("w", columns)], [("w", (rows, 896), BF16)] * 2, name="pack",
        )
        pair = join([keep, swap_core(send)], 3)
        line = join([pair] + [xor_with(pair, 8 * m, count) for m in range(1, nz)], 0, after=[unit])
        w_pieces = [line] + [xor_with(line, m, count) for m in (4, 2, 6)]
        block = jnp.concatenate([up_weight, down_weight.T, out_weight], axis=0)
        (block,) = call(
            hold_kernel, 0, [("a", block), ("d", unit)],
            [("w", block.shape, BF16)], scratch=[pltpu.SemaphoreType.DMA((1,))], name="hold",
        )
        ff_line = join([block] + [xor_with(block, 8 * m, count) for m in range(1, nz)], 0, after=[line])
        by_x, by_y = xor_with(ff_line, 4, count), xor_with(ff_line, 2, count)
    else:
        whole = [
            lax.all_gather(a, BOTH, axis=0, tiled=True) for a in (mix_weight, gate_weight, out_weight) + vectors
        ]
        p0, p1 = mix_pack(whole[0], whole[1], whole[3:])
        blocks = jnp.where(first, p0, p1).reshape(nz, 2, 2, 2, 16, 896)
        w_pieces = [blocks[:, mx, my] for my, mx in ((0, 0), (0, 1), (1, 0), (1, 1))]
        up_all = lax.all_gather(up_weight, BOTH, axis=0, tiled=False).reshape(dp, tensor, -1, hidden)
        dn_all = lax.all_gather(down_weight.T, BOTH, axis=0, tiled=False).reshape(dp, tensor, -1, hidden)
        up_all = jnp.moveaxis(up_all, 1, 0).reshape(2, 2, nz, 2, -1, hidden)
        dn_all = jnp.moveaxis(dn_all, 1, 0).reshape(2, 2, nz, 2, -1, hidden)
        out_all = whole[2].reshape(nz, 2, 2, 2, 16, width).transpose(2, 3, 0, 1, 4, 5)
        ff_all = jnp.concatenate([up_all, dn_all, out_all], axis=4)
        ff_all = jnp.where(first, ff_all, ff_all[:, ::-1])
        ff_own, ff_other = (
            jnp.concatenate([ff_all[my, mc, :, mx] for my in range(2) for mx in range(2)]) for mc in range(2)
        )

    maps = lax.dynamic_slice_in_dim(random_maps, core * 4, 4, 0)
    zero = jnp.zeros((head, head), BF16)
    maps_pair = jnp.stack(
        [
            jnp.concatenate(
                [jnp.concatenate([maps[2 * p], zero], 1), jnp.concatenate([zero, maps[2 * p + 1]], 1)], 0
            )
            for p in range(2)
        ]
    )
    flip = jnp.swapaxes(maps, 1, 2)
    maps_back = jnp.stack(
        [
            jnp.concatenate(
                [
                    jnp.concatenate([flip[2 * p], zero], 1),
                    jnp.concatenate([-flip[2 * p], zero], 1),
                    jnp.concatenate([zero, flip[2 * p + 1]], 1),
                    jnp.concatenate([zero, -flip[2 * p + 1]], 1),
                ],
                0,
            )
            for p in range(2)
        ]
    )
    bias = jnp.pad(lax.dynamic_slice_in_dim(gate_bias, core * 4, 4, 0), (0, 124))[None]

    tokens = seqs * long
    feats = (seqs, 4, long, 128)
    npack = 2 * seqs + 1
    attend, fk, fkl, fkt, va, ccol, ucol, crow, smid, pack, wmix, vec, vbar = call(
        project_kernel, seqs,
        [("m", pos), ("s", unit)] + [("a", w) for w in w_pieces] + [("w", bias), ("w", maps_pair)],
        [
            ("s", (seqs, long, width), BF16), ("s", feats, BF16), ("s", feats, BF16), ("s", feats, BF16), ("s", feats, BF16),
            ("s", (seqs, long, 128), F32), ("s", (seqs, long, 128), F32),
            ("s", (seqs, 2, 8, chunk), F32),
            ("s", (seqs, 4, 128, 128), F32),
            ("w", (npack, 128, 128), BF16), ("w", (width, 896), BF16), ("w", (8, width), F32),
            ("w", (8, width // 2), F32),
        ],
        scratch=[pltpu.VMEM((nz, 2, 2, 2, 16, 896), BF16), pltpu.SemaphoreType.DMA((4,))], us=12, name="project",
    )
    ahead = [(i, i + 2) for i in range(count) if (i % tensor) < 2]
    arrived = lax.ppermute(pack, BOTH, ahead)
    fq, fql, fqt = call(
        query_kernel, seqs, [("s", attend), ("w", wmix), ("w", maps_pair)], [("s", feats, BF16)] * 3, us=0.3, name="query",
    )
    (o_loc,) = call(
        local_kernel, seqs,
        [("s", fq), ("s", fk), ("s", fql), ("s", fkl), ("s", va), ("s", ccol), ("s", crow)],
        [("s", feats, F32)], us=0.3, name="local", unroll=True,
    )
    if direct:
        half_z = nz // 2
        far_shape = (half_z, *ff_line.shape[1:])
        x_half, y_half = call(
            halves_kernel, 0, [("a", by_x), ("a", by_y), ("d", arrived), ("d", o_loc)], [("w", far_shape, BF16)] * 2,
            scratch=[pltpu.SemaphoreType.DMA((2,))], us=0.3, name="halves",
        )
        near_parts = [ff_line, by_x, by_y]
        (ff_near,) = call(
            gather_kernel, 0, [("a", a) for a in near_parts] + [("d", x_half)],
            [("w", (3 * nz, *ff_line.shape[1:]), BF16)], scratch=[pltpu.SemaphoreType.DMA((3,))], us=0.5, name="near",
        )
        before_finish = [x_half]
    else:
        before_finish = []
    (inv_root, turn, st, att_keep, att_send) = call(
        finish_kernel, seqs,
        [("m", pos), ("s", o_loc), ("s", fq), ("s", ccol), ("w", arrived), ("s", smid), ("w", vbar)]
        + [("d", a) for a in before_finish],
        [
            ("s", feats, F32), ("s", feats, F32), ("s", (seqs, 4, 2, 128, 128), BF16),
            ("s", (seqs, chunk, width // 2), BF16), ("s", (seqs, chunk, width // 2), BF16),
        ],
        us=0.3, name="finish",
    )
    att_recv = swap_core(att_send)
    if direct:
        near_other = swap_core(ff_near)
        far_parts = [xor_with(x_half, 2, count), xor_with(y_half, 4, count)]
        (ff_far,) = call(
            gather_kernel, 0, [("a", a) for a in far_parts] + [("d", att_keep)],
            [("w", ff_line.shape, BF16)], scratch=[pltpu.SemaphoreType.DMA((2,))], name="gather",
        )
        far_other = swap_core(ff_far)
    else:
        ff_near, ff_far, near_other, far_other = ff_own[: 3 * nz], ff_own[3 * nz :], ff_other[: 3 * nz], ff_other[3 * nz :]

    own = seqs * chunk
    nrows = ff_near.shape[1]
    payload, out_payload = (2, 2, nz, nrows - 16, hidden), (2, 2, nz, 16, hidden)
    rows_low, rows_full = ("w", (own, width), BF16), ("w", (own, width), F32)
    work = [
        pltpu.VMEM((width, 2 * hidden), BF16), pltpu.VMEM((width, 2 * hidden), BF16),
        pltpu.VMEM((own, 2 * hidden), BF16), pltpu.VMEM((own, 2 * hidden), BF16),
    ]
    big = pltpu.VMEM((width, 2 * hidden), BF16)
    g_send, *fed = call(
        feed_first_kernel, 0,
        [("m", pos)] + [
            ("w", a) for a in (
                att_keep, att_recv, inputs, cotangent, cot_t, vec, ff_near, ff_far, near_other, far_other
            )
        ],
        [
            ("w", payload, BF16), rows_full, rows_full, rows_full, rows_low, ("w", (width, own), BF16), rows_low,
            ("w", (width, width), BF16),
        ],
        scratch=[*work, big], us=10, name="feed_first", limit=18,
    )
    g_recv = swap_core(g_send)
    output, grad_middle, ga_keep, ga_send, g_keep, o_keep, o_send, grad_vec = call(
        feed_second_kernel, 0,
        [("m", pos)] + [("w", a) for a in (cotangent, cot_t, vec, ff_near, ff_far, *fed)],
        [
            ("w", (seqs, chunk, width), BF16), ("w", (seqs, chunk, width), F32),
            ("w", (seqs, chunk, width // 2), BF16), ("w", (seqs, chunk, width // 2), BF16),
            ("w", payload, BF16), ("w", out_payload, BF16), ("w", out_payload, BF16), ("w", (8, width), F32),
        ],
        scratch=[
            *work, pltpu.VMEM((own, width), BF16), big,
        ],
        us=10, name="feed_second", limit=18,
    )
    ga_recv = swap_core(ga_send)

    if direct:
        o_recv = swap_core(o_send)
        half_z = nz // 2
        two, one = (2, half_z, nrows, hidden), (half_z, nrows, hidden)
        x_keep, x_send, y_keep, y_send = call(
            pair_sum_kernel, 0, [("w", g_keep), ("w", g_recv), ("w", o_keep), ("w", o_recv)], [("w", two, BF16)] * 4,
            us=0.6, name="pair_sum",
        )
        x_recv, y_recv = xor_with(x_send, 4, count), xor_with(y_send, 2, count)
        before_adjoint = [x_keep]
    else:
        before_adjoint = []
        g_keep, g_send = (jnp.concatenate(parts, axis=3) for parts in ((g_keep, o_keep), (g_send, o_send)))
        by_core = jnp.where(first, jnp.stack([g_keep, g_send]), jnp.stack([g_send, g_keep]))
        by_rows = by_core.transpose(3, 2, 1, 0, 4, 5)
        rows_up = (nrows - 16) // 2
        ups = by_rows[..., :rows_up, :].reshape(nz * 2, 4, rows_up, hidden).transpose(1, 0, 2, 3)
        dns = by_rows[..., rows_up : 2 * rows_up, :].reshape(nz * 2, 4, rows_up, hidden).transpose(1, 0, 2, 3)
        ups = ups.reshape(4, dp, -1, hidden).transpose(1, 0, 2, 3)
        dns = dns.reshape(4, dp, -1, hidden).transpose(1, 0, 2, 3)
        outs = by_rows[..., 2 * rows_up :, :].reshape(width, width)

        def reduced(a):
            return lax.psum_scatter(a.astype(F32).reshape(count, -1, a.shape[-1]), BOTH, scatter_dimension=0)

        up_grad, down_grad, out_grad = reduced(ups), reduced(dns).T, reduced(outs)

    g, scaled, l1, pack_b = call(
        adjoint_kernel, seqs,
        [("m", pos), ("s", ga_keep), ("s", ga_recv), ("s", inv_root), ("s", turn), ("s", fq), ("s", ccol)]
        + [("d", a) for a in before_adjoint],
        [
            ("s", feats, BF16), ("s", feats, BF16), ("s", (seqs, 4, 128, 128), F32), ("w", (npack, 128, 128), BF16),
        ],
        us=0.3, name="adjoint",
    )
    behind = [(i, i - 2) for i in range(count) if (i % tensor) >= 2]
    arrived_b = lax.ppermute(pack_b, BOTH, behind)
    dfq, dfk, dva = call(
        local_back_kernel, seqs,
        [("s", fq), ("s", fk), ("s", va), ("s", g), ("s", scaled), ("s", st), ("s", ccol), ("s", crow)],
        [("s", feats, F32), ("s", feats, F32), ("s", feats, F32)],
        us=0.3, name="local_back",
    )
    before_close = []
    if direct:
        x_own, x_far, y_own, y_far = call(
            half_sum_kernel, 0, [("w", a) for a in (x_keep, x_recv, y_keep, y_recv)] + [("d", dfq)],
            [("w", one, BF16)] * 4, us=0.4, name="half_sum",
        )
        x_recv, y_recv = xor_with(x_far, 2, count), xor_with(y_far, 4, count)
        before_close = [x_own]
    *m_pieces, gn_keep, gn_send = call(
        functools.partial(close_kernel, seqs_total=seqs), seqs,
        [("m", pos), ("s", unit), ("w", attend), ("s", fq), ("s", fk), ("s", fqt), ("s", fkt), ("s", va), ("s", dfq),
         ("s", dfk), ("s", dva), ("s", ccol), ("s", ucol), ("w", arrived_b), ("s", l1), ("s", st),
         ("w", wmix), ("w", grad_vec), ("w", maps_back)] + [("d", a) for a in before_close],
        [*[("w", (nz, 32, 896), BF16)] * 4, ("s", (seqs, chunk, width), F32), ("s", (seqs, chunk, width), BF16)],
        scratch=[
            pltpu.VMEM((width, 896), F32), pltpu.VMEM((tokens, 896), BF16), pltpu.VMEM((8, 128), F32),
            pltpu.VMEM((8, width), F32), pltpu.VMEM((width, 896), BF16),
        ],
        us=14.7, name="close", unroll=False,
    )
    if direct:
        g_line = call(
            line_sum_kernel, 0, [("w", a) for a in (x_own, x_recv, y_own, y_recv)] + [("d", gn_keep)],
            [("w", (nrows, hidden), BF16)] * nz, us=0.4, name="line_sum",
        )
        m_parts = from_plane(m_pieces)
    gn_recv = swap_core(gn_send)
    def finish_input(after):
        return call(
            input_kernel, seqs,
            [("s", inputs), ("s", grad_middle), ("s", gn_keep), ("s", gn_recv), ("w", vec)] + [("d", a) for a in after],
            [("s", (seqs, chunk, width), F32), ("w", (8, 128), F32)], us=0.3, name="input_grad",
        )

    if direct:
        m_plane = call(
            mix_sum_kernel, 0, [("w", a) for a in m_parts] + [("d", pause([g_line[0]], 40)), ("d", gn_recv)],
            [("w", (32, 896), BF16)] * nz, us=0.4, name="mix_sum",
        )
        input_grad, input_done = finish_input([g_line[0]])
        g_parts = [g_line[0]] + [xor_with(g_line[m], 8 * m, count) for m in range(1, nz)]
        up_grad, down_back, out_grad, feed_done = call(
            feed_last_kernel, 0, [("w", a) for a in g_parts],
            [("w", shape, F32) for shape in (up_weight.shape, down_weight.shape[::-1], out_weight.shape, (8, 128))],
            us=0.3, name="feed_last",
        )
        down_grad = down_back.T
        mix_parts = [m_plane[0]] + [xor_with(m_plane[m], 8 * m, count) for m in range(1, nz)]
        m_keep, m_send = call(
            mix_last_kernel, 0, [("m", pos)] + [("w", a) for a in mix_parts] + [("d", feed_done), ("d", input_done)],
            [("w", (mix_weight.shape[0], 896), F32)] * 2, name="mix_last",
        )
        m_recv = swap_core(m_send)
    else:
        input_grad, input_done = finish_input([])
        m_all = jnp.stack(m_pieces).astype(F32).reshape(2, 2, nz, 32, 896)
        mine_rows = m_all.transpose(2, 1, 0, 3, 4).reshape(count, -1, 896)
        keep_part = lax.psum_scatter(mine_rows * jnp.where(first, 1.0, 0.0), BOTH, scatter_dimension=0)
        far_part = lax.psum_scatter(mine_rows * jnp.where(first, 0.0, 1.0), BOTH, scatter_dimension=0)
        m_keep = jnp.where(first, keep_part, far_part)
        m_recv = jnp.where(first, far_part, keep_part)
    if direct:
        mix_grad, gate_back, bias_grad, *per_row = call(
            final_kernel, 0, [("m", pos), ("w", m_keep), ("w", m_recv)],
            [("w", mix_weight.shape, F32), ("w", gate_weight.shape[::-1], F32), ("w", (heads,), F32)]
            + [("w", gain_first.shape, F32)] * 4,
            us=1.2, name="final",
        )
        gate_grad = gate_back.T
    else:
        m_low = jnp.where(first, m_keep, m_recv)
        m_high = jnp.where(first, m_recv, m_keep)
        mix_grad = jnp.concatenate(
            [part[:, 256 * i : 256 * i + 256] for i in range(3) for part in (m_low, m_high)], axis=1
        )
        gate_grad = jnp.concatenate([m_low[:, 768:772], m_high[:, 768:772]], axis=1)
        bias_grad = jnp.concatenate([m[0, 776:780] + m[0, 780:784] for m in (m_low, m_high)])
        per_row = [m_keep[:, 772 + i] + m_recv[:, 772 + i] for i in range(4)]
    return (
        output, input_grad, mix_grad, gate_grad, bias_grad, out_grad,
        *per_row, up_grad, down_grad,
    )


def solution(mesh):
    rows, spread = P(("dp", "tensor"), None), P(("dp", "tensor"))
    tokens = P("dp", "tensor", None)
    in_specs = (
        tokens, tokens, rows, rows, P(), rows, spread, spread, spread, spread, P("dp", "tensor"), P("tensor", "dp"), P(),
    )
    out_specs = (
        tokens, tokens, rows, rows, P(), rows, spread, spread, spread, spread, P("dp", "tensor"), P("tensor", "dp"),
    )
    return jax.shard_map(body, mesh=mesh, in_specs=in_specs, out_specs=out_specs, check_vma=False)
```

```python
import functools

import jax
import jax.numpy as jnp
from jax import lax
from jax.experimental import pallas as pl
from jax.experimental.pallas import tpu as pltpu
from jax.sharding import PartitionSpec as P

BOTH = ("dp", "tensor")
F32 = jnp.float32
BF16 = jnp.bfloat16
EPSILON = 1e-05
DENSITY = 0.3989422804014327
SIN = (9.9999999998e-01, -1.6666666617e-01, 8.3333309689e-03, -1.9840860382e-04, 2.7525224003e-06, -2.3888330913e-08)
COS = (9.9999999978e-01, -4.9999999354e-01, 4.1666636104e-02, -1.3888359409e-03, 2.4760057595e-05, -2.6049626765e-07)

NN = (((1,), (0,)), ((), ()))
NT = (((1,), (1,)), ((), ()))
TN = (((0,), (0,)), ((), ()))


def mm(a, b, dims=NN):
    return lax.dot_general(a, b, dims, preferred_element_type=F32)


def low(a):
    return a.astype(BF16)


def lanes_of(shape):
    return lax.broadcasted_iota(jnp.int32, shape, len(shape) - 1)


def swap_halves(a):
    return pltpu.roll(a, 64, 1)


def sincos(a):
    turns = jnp.floor(a * 0.3183098861837907 + 0.5)
    r = (a - turns * 3.140625) - turns * 9.676535897932e-4
    half = turns * 0.5
    sign = 1.0 - 4.0 * (half - jnp.floor(half))
    r2 = r * r
    s = r * (SIN[0] + r2 * (SIN[1] + r2 * (SIN[2] + r2 * (SIN[3] + r2 * (SIN[4] + r2 * SIN[5])))))
    c = COS[0] + r2 * (COS[1] + r2 * (COS[2] + r2 * (COS[3] + r2 * (COS[4] + r2 * COS[5]))))
    return sign * s, sign * c


def normal_parts(v):
    t = pl.reciprocal(1.0 + 0.23164189 * jnp.abs(v), approx=True)
    bell = jnp.exp(-0.5 * (v * v))
    poly = t * (0.127414796 + t * (-0.142248368 + t * (0.7107068705 + t * (-0.7265760135 + t * 0.5307027145))))
    tail = poly * bell
    return jnp.where(v >= 0.0, 1.0 - tail, tail), DENSITY * bell


def three_parts(a):
    high = a.astype(BF16)
    rest = a - high.astype(F32)
    mid = rest.astype(BF16)
    return high, mid, (rest - mid.astype(F32)).astype(BF16)


def tri_sum(tri, a):
    high, mid, rest = (part.astype(F32) for part in three_parts(a))
    packed = mm(tri, low(high + pltpu.roll(mid, 4, 1) + pltpu.roll(rest, 8, 1)))
    return packed + pltpu.roll(packed, 124, 1) + pltpu.roll(packed, 120, 1)


def norm_of(x):
    mean = jnp.mean(x, axis=-1, keepdims=True)
    centered = x - mean
    inv = lax.rsqrt(jnp.mean(centered * centered, axis=-1, keepdims=True) + EPSILON)
    return centered * inv, inv


def norm_back(s, unit, inv):
    return inv * (
        s
        - jnp.mean(s, axis=-1, keepdims=True)
        - unit * jnp.mean(s * unit, axis=-1, keepdims=True)
    )


def chip_row(pos, mz, mx, my):
    return (((pos[0] ^ mz) * 2 + (pos[1] ^ mx)) * 2 + (pos[2] ^ my)) * 32


def lower_tri(n):
    row = lax.broadcasted_iota(jnp.int32, (n, n), 0)
    col = lax.broadcasted_iota(jnp.int32, (n, n), 1)
    return row, col


def unpack_states(pack, b, zcols, last=65):
    lane = lanes_of((128, 128))
    out = []
    for p in range(2):
        both = pack[2 * b + p].astype(F32)
        for h, mat in ((2 * p, both), (2 * p + 1, swap_halves(both))):
            z = jnp.sum(jnp.where(lane == 4 * b + h, zcols, 0.0), axis=1, keepdims=True)
            out.append(jnp.where(lane < 64, mat, jnp.where(lane <= last, z, 0.0)))
    return out


def pack_states(states, pack_o, b, last, split=False):
    lane = lanes_of((128, 128))
    zcols = jnp.where(b == 0, 0.0, pack_o[last].astype(F32))

    def sum_of(s):
        return s[:, 64:65] + s[:, 65:66] if split else s[:, 64:65]

    for p in range(2):
        s0, s1 = states[2 * p], states[2 * p + 1]
        pack_o[2 * b + p] = jnp.where(lane < 64, s0, swap_halves(s1)).astype(BF16)
        zcols = jnp.where(lane == 4 * b + 2 * p, sum_of(s0), zcols)
        zcols = jnp.where(lane == 4 * b + 2 * p + 1, sum_of(s1), zcols)
    pack_o[last] = zcols.astype(BF16)


def pack_kernel(pos, mix, columns, keep_o, send_o):
    width = mix.shape[1] // 6
    rows = mix.shape[0]
    table = jnp.concatenate(
        [columns[...].astype(F32), jnp.zeros((128 - columns.shape[0], rows), F32)], axis=0
    )
    sides = jnp.concatenate([table, jnp.zeros((128, 128 - rows), F32)], axis=1).T[0:rows]
    lane = lanes_of(sides.shape)
    moved = pltpu.roll(sides, 124, 1)
    halves = []
    for s, block in ((0, jnp.where(lane < 4, sides, moved)), (1, moved)):
        parts = [mix[:, (2 * i + s) * width : (2 * i + s + 1) * width] for i in range(3)]
        halves.append(jnp.concatenate(parts + [low(jnp.where(lane < 8, block, 0.0))], axis=1))
    first = pos[3] == 0
    keep_o[...] = jnp.where(first, halves[0], halves[1])
    send_o[...] = jnp.where(first, halves[1], halves[0])


def prepare_kernel(b, pos, own, oth, cot, unit_o, cott_o):
    chunk = own.shape[1]
    first = pos[3] == 0
    mine, theirs = own[0], oth[0]
    for j in range(2):
        unit, _ = norm_of(jnp.where(first == (j == 0), mine, theirs).astype(F32))
        unit_o[0, j * chunk : (j + 1) * chunk] = unit
    cott_o[0] = low(cot[0].astype(F32).T)


def feature_parts(angles, lane):
    s, c = sincos(angles)
    out = []
    turned_s, turned_c = swap_halves(s), swap_halves(c)
    for f, turned in (
        (jnp.where(lane < 64, s, turned_c), jnp.where(lane < 64, c, turned_s)),
        (jnp.where(lane < 64, turned_s, c), jnp.where(lane < 64, turned_c, s)),
    ):
        high = low(f)
        out.append((high, low(f - high.astype(F32)), low(turned)))
    return out


def query_kernel(b, a, wmix, maps, fq_o, fql_o, fqt_o):
    chunk = a.shape[1] // 2
    lane = lanes_of((chunk, 128))
    spans = [slice(j * chunk, (j + 1) * chunk) for j in range(2)]
    mixed = [low(mm(a[0, rows], wmix[:, 0:256])) for rows in spans]
    angles = [[mm(m[:, 128 * p : 128 * p + 128], maps[p]) for p in range(2)] for m in mixed]
    for j, rows in enumerate(spans):
        for p in range(2):
            for i, (high, rest, turned) in enumerate(feature_parts(angles[j][p], lane)):
                fq_o[0, 2 * p + i, rows], fql_o[0, 2 * p + i, rows], fqt_o[0, 2 * p + i, rows] = high, rest, turned


def project_kernel(
    b, pos, units, w0, w1, w2, w3, bias, maps,
    a_o, fk_o, fkl_o, fkt_o, va_o, ccol_o, ucol_o, crow_o, smid_o, pack_o, wmix_o, vec_o, vbar_o,
    w_s, sems,
):
    chunk = units.shape[1] // 2

    @pl.when(b == 0)
    def _():
        copies = [
            pltpu.make_async_copy(piece, w_s.at[:, pos[1] ^ mx, pos[2] ^ my], sems.at[2 * my + mx])
            for piece, (my, mx) in ((w0, (0, 0)), (w1, (0, 1)), (w2, (1, 0)), (w3, (1, 1)))
        ]
        for copy in copies:
            copy.start()
        for copy in copies:
            copy.wait()
        wmix_o[...] = w_s[...].reshape(wmix_o.shape)
        vec_o[...] = wmix_o[:, 768:896].astype(F32).T[0:8]
        vbar_o[...] = mm(jnp.broadcast_to(vec_o[5:6], vec_o.shape).astype(BF16), wmix_o[:, 512:768])

    gain, shift = vec_o[4:5], vec_o[5:6]
    row, col = lower_tri(chunk)
    tri = jnp.where(row >= col, 1.0, 0.0).astype(BF16)
    lane = lanes_of((chunk, 128))
    spans = [slice(j * chunk, (j + 1) * chunk) for j in range(2)]
    attends = [low(units[0, rows] * gain + shift) for rows in spans]
    for a, rows in zip(attends, spans):
        a_o[0, rows] = a
    wide = [mm(a, wmix_o[:, 256:896]) for a in attends]
    mixed = [low(m[:, 0:512]) for m in wide]
    angles = [[mm(m[:, 128 * p : 128 * p + 128], maps[p]) for p in range(2)] for m in mixed]
    douts, ends = [], []
    for j, rows in enumerate(spans):
        logits = wide[j][:, 512:640] + bias[...]
        e = jnp.exp(-jnp.abs(logits))
        w = 1.0 + e
        log1 = jnp.where(w == 1.0, e, jnp.log(w) * (e / jnp.where(w == 1.0, 1.0, w - 1.0)))
        log_gate = jnp.where(lane < 4, jnp.minimum(logits, 0.0) - log1, 0.0)
        fresh = jnp.where(lane < 4, jnp.where(logits >= 0.0, e, 1.0) / w, 0.0)
        cum = jnp.where(lane < 4, tri_sum(tri, log_gate), 0.0)
        ccol_o[0, rows] = cum
        ucol_o[0, rows] = fresh
        crow_o[0, j] = (cum + pltpu.roll(fresh, 4, 1)).T[0:8]
        ends.append(cum[chunk - 1 : chunk])
        douts.append(jnp.exp(ends[j] - cum) * fresh)
    one = jnp.where((lane == 64) | (lane == 65), 1.0, 0.0)
    shares = [[None] * 4, [None] * 4]
    for j, rows in enumerate(spans):
        for p in range(2):
            v = mixed[j][:, 256 + 128 * p : 384 + 128 * p].astype(F32) - vbar_o[0:1, 128 * p : 128 * p + 128]
            for h, vh in ((2 * p, v), (2 * p + 1, swap_halves(v))):
                aug = jnp.where(lane < 64, vh, one)
                va_o[0, h, rows] = low(aug)
                shares[j][h] = low(aug * douts[j][:, h : h + 1])
    locals_ = [[None] * 4, [None] * 4]
    for j, rows in enumerate(spans):
        for p in range(2):
            parts = feature_parts(angles[j][p], lane)
            for h in (2 * p, 2 * p + 1):
                fk_o[0, h, rows], fkl_o[0, h, rows], fkt_o[0, h, rows] = parts[h - 2 * p]
                locals_[j][h] = mm(parts[h - 2 * p][0], shares[j][h], TN)
    states = []
    for h in range(4):
        smid_o[0, h] = locals_[0][h]
        states.append(locals_[0][h] * jnp.exp(ends[1][:, h : h + 1]) + locals_[1][h])
    pack_states(states, pack_o, b, pack_o.shape[0] - 1)


def weights_of(ccol, ucol_row, crow, row, col):
    gap = jnp.minimum(ccol - crow, 0.0)
    return jnp.where(row >= col, jnp.exp(gap), 0.0) * ucol_row


def pairs_of(chunk):
    return [(j, h, slice(j * chunk, (j + 1) * chunk)) for j in range(2) for h in range(4)]


def scores(fq, fk, fql, fkl, h, rows):
    q, k = fq[0, h, rows], fk[0, h, rows]
    return mm(
        jnp.concatenate([q, fql[0, h, rows], q], axis=1), jnp.concatenate([k, k, fkl[0, h, rows]], axis=1), NT
    )


def local_kernel(b, fq, fk, fql, fkl, va, ccol, crow, o_o):
    chunk = crow.shape[3]
    row, col = lower_tri(chunk)
    pairs = pairs_of(chunk)
    qk = [scores(fq, fk, fql, fkl, h, rows) for j, h, rows in pairs]
    attn = [
        low(q * weights_of(ccol[0, rows, h : h + 1], crow[0, j, 4 + h : 5 + h], crow[0, j, h : h + 1], row, col))
        for q, (j, h, rows) in zip(qk, pairs)
    ]
    outs = [mm(a, va[0, h, rows]) for a, (j, h, rows) in zip(attn, pairs)]
    for out, (j, h, rows) in zip(outs, pairs):
        o_o[0, h, rows] = out


def mean_of(vbar, h):
    pair = vbar[:, 128 * (h // 2) : 128 * (h // 2) + 128]
    return (pair if h % 2 == 0 else swap_halves(pair))[0:1]


def finish_kernel(b, pos, o_loc, fq, ccol, pack, smid, vbar, inv_o, turn_o, st_o, keep_o, send_o):
    chunk = ccol.shape[1] // 2
    zcols = pack[pack.shape[0] - 1].astype(F32)
    states = unpack_states(pack, b, zcols)
    lane = lanes_of((chunk, 128))
    cend = ccol[0, chunk - 1 : chunk]
    pairs = pairs_of(chunk)
    near = []
    for h in range(4):
        near.append(low(states[h]))
        near.append(low(jnp.exp(cend[:, h : h + 1]) * states[h] + smid[0, h]))
        for j in range(2):
            st_o[0, h, j] = near[2 * h + j]
    inter = [mm(fq[0, h, rows], near[2 * h + j]) for j, h, rows in pairs]
    outs = [
        o_loc[0, h, rows] + jnp.exp(ccol[0, rows, h : h + 1]) * part for part, (j, h, rows) in zip(inter, pairs)
    ]
    dens = [jnp.broadcast_to(o[:, 64:65], o.shape) for o in outs]
    invs = [lax.rsqrt(den * den + 1.0) for den in dens]
    att = [[None] * 4, [None] * 4]
    for o, den, inv, (j, h, rows) in zip(outs, dens, invs, pairs):
        mean = mean_of(vbar, h)
        att[j][h] = (o + den * mean) * inv
        inv_o[0, h, rows] = jnp.where(lane < 64, inv, 0.0)
        turn_o[0, h, rows] = mean - den * inv * att[j][h]
    first = pos[3] == 0
    for p in range(2):
        both = [
            jnp.where(lane < 64, att[j][2 * p], swap_halves(att[j][2 * p + 1])) for j in range(2)
        ]
        keep_o[0, :, 128 * p : 128 * p + 128] = jnp.where(first, both[0], both[1]).astype(BF16)
        send_o[0, :, 128 * p : 128 * p + 128] = jnp.where(first, both[1], both[0]).astype(BF16)


def dp_of(pos, mz, mx):
    return (pos[0] ^ mz) * 2 + (pos[1] ^ mx)


def feed_chunks(pos, near, far, cot, cott, feed, feedt, target, up_s, dn_s, hid_s, gp_s, big_s):
    seqs, chunk, _ = cot.shape
    nz = far.shape[0]
    width, both = up_s.shape
    hidden = both // 2
    rows_up = width // (2 * nz)
    for my in range(2):
        cols = slice(my * hidden, (my + 1) * hidden)
        for mx in range(2):
            k = 2 * my + mx
            piece = far if k == 3 else near.at[pl.ds(k * nz, nz)]
            for z in range(nz):
                at = pl.multiple_of((2 * z + (pos[1] ^ mx)) * rows_up, rows_up)
                up_s[pl.ds(at, rows_up), cols] = piece[z, 0:rows_up]
                dn_s[pl.ds(at, rows_up), cols] = piece[z, rows_up : 2 * rows_up]

    def scatter(offset):
        for my in range(2):
            cols = slice(my * hidden, (my + 1) * hidden)
            for mx in range(2):
                for mz in range(nz):
                    at = pl.multiple_of(dp_of(pos, mz, mx) * rows_up, rows_up)
                    target[my, mx, mz, offset : offset + rows_up, :] = big_s[pl.ds(at, rows_up), cols]

    spans = [slice(r * chunk, (r + 1) * chunk) for r in range(seqs)]
    outs, grads = [], []
    pres = [mm(feed[rows], up_s[...]) for rows in spans]
    ghs = [mm(cot[r], dn_s[...]) for r in range(seqs)]
    for r, rows in enumerate(spans):
        cdf, pdf = normal_parts(pres[r])
        hid_s[rows] = low(pres[r] * cdf)
        gp_s[rows] = low(ghs[r] * (cdf + pres[r] * pdf))
    for rows in spans:
        outs.append(mm(hid_s[rows], dn_s[...], NT))
        grads.append(mm(gp_s[rows], up_s[...], NT))
    big_s[...] = low(mm(feedt[...], gp_s[...]))
    scatter(0)
    big_s[...] = low(mm(jnp.concatenate([cott[r] for r in range(seqs)], axis=1), hid_s[...]))
    scatter(rows_up)
    return outs, grads


def feed_first_kernel(
    pos, akeep, arecv, x, cot, cott, vec, near_own, far_own, near, far,
    gsend_o, acc_o, gf_o, mid_o, feed_o, feedt_o, att_o, ow_o,
    up_s, dn_s, hid_s, gp_s, big_s,
):
    seqs, chunk, _ = x.shape
    nz = far.shape[0]
    rows_up = up_s.shape[0] // (2 * nz)
    first = pos[3] == 0
    for mc, (some, rest) in enumerate(((near_own, far_own), (near, far))):
        for my in range(2):
            t = (pos[2] ^ my) * 2 + (pos[3] ^ mc)
            for mx in range(2):
                k = 2 * my + mx
                for z in range(nz):
                    at = pl.multiple_of(((2 * z + (pos[1] ^ mx)) * 4 + t) * 16, 16)
                    source = rest if k == 3 else some.at[pl.ds(k * nz, nz)]
                    ow_o[pl.ds(at, 16), :] = source[z, 2 * rows_up :]
    gain, shift = vec[6:7], vec[7:8]
    for r in range(seqs):
        rows = slice(r * chunk, (r + 1) * chunk)
        mine, theirs = akeep[r], arecv[r]
        att = jnp.concatenate([jnp.where(first, mine, theirs), jnp.where(first, theirs, mine)], axis=1)
        att_o[rows] = att
        mid = x[r].astype(F32) + mm(att, ow_o[...])
        mid_o[rows] = mid
        unit, _ = norm_of(mid)
        feed = unit * gain + shift
        feed_o[rows] = low(feed)
        feedt_o[:, rows] = low(feed.T)
    outs, grads = feed_chunks(pos, near, far, cot, cott, feed_o, feedt_o, gsend_o, up_s, dn_s, hid_s, gp_s, big_s)
    for r, (out, grad) in enumerate(zip(outs, grads)):
        acc_o[r * chunk : (r + 1) * chunk] = out
        gf_o[r * chunk : (r + 1) * chunk] = grad


def feed_second_kernel(
    pos, cot, cott, vec, near, far, acc, gf_in, mid_in, feed, feedt, att, ow,
    out_o, gm_o, gak_o, gas_o, gkeep_o, okeep_o, osend_o, gv_o,
    up_s, dn_s, hid_s, gp_s, gb_s, big_s,
):
    seqs, chunk, width = cot.shape
    nz = far.shape[0]
    first = pos[3] == 0
    outs, grads = feed_chunks(pos, near, far, cot, cott, feed, feedt, gkeep_o, up_s, dn_s, hid_s, gp_s, big_s)
    gain = vec[6:7]
    gain_sum = jnp.zeros((1, width), F32)
    shift_sum = jnp.zeros((1, width), F32)
    for r in range(seqs):
        rows = slice(r * chunk, (r + 1) * chunk)
        mid = mid_in[rows]
        out_o[r] = low(mid + (acc[rows] + outs[r]))
        unit, inv = norm_of(mid)
        gf = gf_in[rows] + grads[r]
        gain_sum += jnp.sum(gf * unit, axis=0, keepdims=True)
        shift_sum += jnp.sum(gf, axis=0, keepdims=True)
        gm = cot[r].astype(F32) + norm_back(gf * gain, unit, inv)
        gm_o[r] = gm
        gb = low(gm)
        gb_s[rows] = gb
        ga = low(mm(gb, ow[...], NT))
        half = width // 2
        gak_o[r] = jnp.where(first, ga[:, :half], ga[:, half:])
        gas_o[r] = jnp.where(first, ga[:, half:], ga[:, :half])
    gv_o[...] = jnp.concatenate([gain_sum, shift_sum, jnp.zeros((6, width), F32)], axis=0)
    big_s[:, 0:width] = low(mm(att[...], gb_s[...], TN))
    for mc, target in ((0, okeep_o), (1, osend_o)):
        for my in range(2):
            t = (pos[2] ^ my) * 2 + (pos[3] ^ mc)
            for mx in range(2):
                for mz in range(nz):
                    at = pl.multiple_of((dp_of(pos, mz, mx) * 4 + t) * 16, 16)
                    target[my, mx, mz] = big_s[pl.ds(at, 16), 0:width]


def adjoint_kernel(b, pos, gak, gar, inv_root, turn, fq, ccol, g_o, scaled_o, l1_o, pack_o):
    chunk = ccol.shape[1] // 2
    lane = lanes_of((chunk, 128))
    first = pos[3] == 0
    pairs = pairs_of(chunk)
    gas = []
    for j in range(2):
        for p in range(2):
            cols = slice(128 * p, 128 * p + 128)
            pair = jnp.where(first == (j == 0), gak[0, :, cols], gar[0, :, cols]).astype(F32)
            gas += [pair, swap_halves(pair)]
    gns = [low(ga * inv_root[0, h, rows]).astype(F32) for ga, (j, h, rows) in zip(gas, pairs)]
    gds = [
        jnp.sum(gn * turn[0, h, rows], axis=1, keepdims=True) for gn, (j, h, rows) in zip(gns, pairs)
    ]
    scaled = []
    for gn, gd, (j, h, rows) in zip(gns, gds, pairs):
        gd = jnp.broadcast_to(gd, gn.shape)
        high = low(gd).astype(F32)
        g = jnp.where(lane == 64, high, jnp.where(lane == 65, gd - high, gn))
        g_o[0, h, rows] = low(g)
        scaled.append(low(g * jnp.exp(ccol[0, rows, h : h + 1])))
        scaled_o[0, h, rows] = scaled[-1]
    parts = [mm(fq[0, h, rows], g, TN) for g, (j, h, rows) in zip(scaled, pairs)]
    states = []
    for h in range(4):
        l1_o[0, h] = parts[4 + h]
        states.append(parts[h] + jnp.exp(ccol[0, chunk - 1 : chunk, h : h + 1]) * parts[4 + h])
    pack_states(states, pack_o, b, pack_o.shape[0] - 1, split=True)


def local_back_kernel(b, fq, fk, va, g, scaled, st, ccol, crow, dfq_o, dfk_o, dva_o):
    chunk = crow.shape[3]
    row, col = lower_tri(chunk)
    pairs = pairs_of(chunk)
    for half in (pairs[:4], pairs[4:]):
        qk = [mm(fq[0, h, rows], fk[0, h, rows], NT) for j, h, rows in half]
        da = [mm(g[0, h, rows], va[0, h, rows], NT) for j, h, rows in half]
        inter = [mm(scaled[0, h, rows], st[0, h, j], NT) for j, h, rows in half]
        attn, dp = [], []
        for q, d, (j, h, rows) in zip(qk, da, half):
            w = weights_of(ccol[0, rows, h : h + 1], crow[0, j, 4 + h : 5 + h], crow[0, j, h : h + 1], row, col)
            attn.append(low(q * w))
            dp.append(low(d * w))
        dva = [mm(a, g[0, h, rows], TN) for a, (j, h, rows) in zip(attn, half)]
        dfk = [mm(d, fq[0, h, rows], TN) for d, (j, h, rows) in zip(dp, half)]
        dfq = [mm(d, fk[0, h, rows]) for d, (j, h, rows) in zip(dp, half)]
        for i, (j, h, rows) in enumerate(half):
            dfq_o[0, h, rows] = dfq[i] + inter[i]
            dfk_o[0, h, rows] = dfk[i]
            dva_o[0, h, rows] = dva[i]


def close_kernel(
    b, pos, units, attend, fq, fk, fqt, fkt, va, dfq, dfk, dva, ccol, ucol, pack, l1, st, wmix, gv, back,
    m00_o, m01_o, m10_o, m11_o, gnk_o, gns_o,
    acc_s, gm_s, gate_s, vsum_s, big_s,
    *, seqs_total,
):
    seqs = seqs_total
    chunk = units.shape[1] // 2
    nz = m00_o.shape[0]
    lane = lanes_of((chunk, 128))
    row, col = lower_tri(chunk)
    upper = jnp.where(row <= col, 1.0, 0.0).astype(BF16)
    zcols = pack[pack.shape[0] - 1].astype(F32)
    arrived = unpack_states(pack, b, zcols, last=64)
    wide = lanes_of((128, 128))

    @pl.when(b == 0)
    def _():
        gate_s[...] = jnp.zeros_like(gate_s)
        vsum_s[...] = jnp.zeros_like(vsum_s)

    pairs = pairs_of(chunk)
    spans = [slice(j * chunk, (j + 1) * chunk) for j in range(2)]
    cums = [ccol[0, rows] for rows in spans]
    freshs = [ucol[0, rows] for rows in spans]
    douts = [jnp.exp(cum[chunk - 1 : chunk] - cum) * fresh for cum, fresh in zip(cums, freshs)]
    nears = []
    for j, h, rows in pairs:
        adj = arrived[h]
        if j == 0:
            adj = l1[0, h] + jnp.exp(ccol[0, 2 * chunk - 1 : 2 * chunk, h : h + 1]) * adj
        zs = adj[:, 64:65] + adj[:, 65:66]
        high = low(zs).astype(F32)
        nears.append(low(jnp.where(wide == 64, high, jnp.where(wide == 65, zs - high, adj))))
    dk_fars = [mm(va[0, h, rows], near, NT) for near, (j, h, rows) in zip(nears, pairs)]
    dv_fars = [mm(fk[0, h, rows], near) for near, (j, h, rows) in zip(nears, pairs)]
    kds, qds, levels = [], [], []
    pqs, pks, dvs = [], [], []
    for i, (j, h, rows) in enumerate(pairs):
        d = douts[j][:, h : h + 1]
        keys, queries = fk[0, h, rows].astype(F32), fq[0, h, rows].astype(F32)
        dk_far = d * dk_fars[i]
        dk = dk_far + dfk[0, h, rows]
        dq = dfq[0, h, rows]
        kds.append(jnp.sum(keys * dk, axis=1, keepdims=True))
        qds.append(jnp.sum(queries * dq, axis=1, keepdims=True))
        passed = st[0, h, j].astype(F32) * nears[i].astype(F32)
        passed = jnp.sum(jnp.sum(passed, axis=0, keepdims=True), axis=1, keepdims=True)
        total = jnp.sum(jnp.sum(keys * dk_far, axis=0, keepdims=True), axis=1, keepdims=True)
        levels.append(total + jnp.exp(cums[j][chunk - 1 : chunk, h : h + 1]) * passed)
        dvs.append(dva[0, h, rows] + d * dv_fars[i])
        pks.append(low(dk * fkt[0, h, rows].astype(F32)))
        pqs.append(low(dq * fqt[0, h, rows].astype(F32)))
    grads = [
        [mm(jnp.concatenate(ps[4 * j + 2 * p : 4 * j + 2 * p + 2], axis=1), back[p]) for ps in (pqs, pks) for p in range(2)]
        for j in range(2)
    ]
    bias_sum = jnp.zeros((1, 128), F32)
    gms = []
    for j in range(2):
        kd = qd = jnp.zeros((chunk, 128), F32)
        level = jnp.zeros((1, 128), F32)
        for h in range(4):
            kd = jnp.where(lane == h, kds[4 * j + h], kd)
            qd = jnp.where(lane == h, qds[4 * j + h], qd)
            level = jnp.where(lanes_of((1, 128)) == h, levels[4 * j + h], level)
        dlog = tri_sum(upper, qd - kd) + level
        dlogit = jnp.where(lane < 4, freshs[j] * dlog - (1.0 - freshs[j]) * kd, 0.0)
        bias_sum += jnp.sum(dlogit, axis=0, keepdims=True)
        values = [jnp.where(lane < 64, dvs[4 * j + 2 * p], swap_halves(dvs[4 * j + 2 * p + 1])) for p in range(2)]
        gm = jnp.concatenate([low(x) for x in (*grads[j], *values, dlogit)], axis=1)
        gm_s[pl.ds(pl.multiple_of((2 * b + j) * chunk, chunk), chunk), :] = gm
        gms.append(gm)
    normed = [mm(gm, wmix[...], NT) for gm in gms]
    vsum_s[0:1] += sum(jnp.sum(n * units[0, rows], axis=0, keepdims=True) for n, rows in zip(normed, spans))
    vsum_s[1:2] += sum(jnp.sum(n, axis=0, keepdims=True) for n in normed)
    first = pos[3] == 0
    gnk_o[0] = jnp.where(first, normed[0], normed[1])
    gns_o[0] = low(jnp.where(first, normed[1], normed[0]))
    gate_s[0:1] += bias_sum

    @pl.when(b == seqs - 1)
    def _():
        width = acc_s.shape[0]
        acc_s[...] = mm(attend[...].reshape(gm_s.shape[0], width), gm_s[...], TN)
        table = jnp.concatenate(
            [jnp.zeros((4, width), F32), vsum_s[0:2], gv[0:2], jnp.zeros((120, width), F32)], axis=0
        ).T
        total = gate_s[0:1]
        high = low(total).astype(F32)
        rest = jnp.broadcast_to(total - high, (8, 128))
        both = pltpu.roll(jnp.broadcast_to(high, (8, 128)), 8, 1) + pltpu.roll(rest, 12, 1)
        biases = jnp.broadcast_to(both[0:1], (width, 128))
        side = jnp.where(lanes_of((width, 128)) < 4, acc_s[:, 768:896], table) + biases
        big_s[:, 0:768] = acc_s[:, 0:768].astype(BF16)
        big_s[:, 768:896] = side.astype(BF16)
        for my in range(2):
            for mx in range(2):
                for mz in range(nz):
                    at = pl.multiple_of(chip_row(pos, mz, mx, my), 32)
                    (m00_o, m01_o, m10_o, m11_o)[2 * my + mx][mz] = big_s[pl.ds(at, 32), :]


def final_kernel(pos, keep, recv, mix_o, gate_o, bias_o, *vec_o):
    first = pos[3] == 0
    mine, theirs = keep[...], recv[...]
    halves = (jnp.where(first, mine, theirs), jnp.where(first, theirs, mine))
    width = mix_o.shape[1] // 6
    for i in range(3):
        for s in range(2):
            mix_o[:, (2 * i + s) * width : (2 * i + s + 1) * width] = halves[s][:, i * width : (i + 1) * width]
    sides = [half[:, 3 * width :] for half in halves]
    lane = lanes_of(sides[0].shape)
    both = jnp.concatenate([sides[0] + sides[1], sides[0], sides[1], jnp.zeros((80, 128), F32)], axis=0).T
    gate_o[0:4] = both[0:4, 16:32]
    gate_o[4:8] = both[0:4, 32:48]
    for i, out in enumerate(vec_o):
        out[...] = both[4 + i, 0:16]
    sums = [side[0:8] + pltpu.roll(side[0:8], 124, 1) for side in sides]
    row = jnp.where(lane[0:8] < 4, pltpu.roll(sums[0], 120, 1), pltpu.roll(sums[1], 124, 1))
    bias_o[...] = row[0, 0:8]


def input_kernel(b, x, gm, keep, recv, vec, o, done_o):
    done_o[...] = jnp.zeros_like(done_o)
    unit, inv = norm_of(x[0].astype(F32))
    grad = keep[0] + recv[0].astype(F32)
    o[0] = gm[0] + norm_back(grad * vec[4:5], unit, inv)


def hold_kernel(*refs):
    sems = refs[-1]
    count = (len(refs) - 1) // 2
    copies = [
        pltpu.make_async_copy(refs[i], refs[count + i], sems.at[i]) for i in range(count)
    ]
    for copy in copies:
        copy.start()
    for copy in copies:
        copy.wait()


def halves_kernel(by_x, by_y, x_half, y_half, sems):
    half = x_half.shape[0]
    copies = [
        pltpu.make_async_copy(by_x.at[pl.ds(0, half)], x_half, sems.at[0]),
        pltpu.make_async_copy(by_y.at[pl.ds(half, half)], y_half, sems.at[1]),
    ]
    for copy in copies:
        copy.start()
    for copy in copies:
        copy.wait()


def gather_kernel(*refs):
    parts, out, sems = refs[:-2], refs[-2], refs[-1]
    copies, at = [], 0
    for i, part in enumerate(parts):
        copies.append(pltpu.make_async_copy(part, out.at[pl.ds(at, part.shape[0])], sems.at[i]))
        at += part.shape[0]
    for copy in copies:
        copy.start()
    for copy in copies:
        copy.wait()


def pause_kernel(out):
    out[...] = jnp.zeros_like(out)


def join_kernel(pos, *refs, axis):
    parts, out, sems = refs[:-2], refs[-2], refs[-1]
    copies = [
        pltpu.make_async_copy(part, out.at[pos[axis] ^ i], sems.at[i]) for i, part in enumerate(parts)
    ]
    for copy in copies:
        copy.start()
    for copy in copies:
        copy.wait()


def pair_sum_kernel(keep, recv, okeep, orecv, x_keep, x_send, y_keep, y_send):
    half = x_keep.shape[1]
    rows = keep.shape[3]
    first, second = slice(0, half), slice(half, 2 * half)
    for i in range(2):
        for my, mx, zs, out in ((i, 0, first, x_keep), (i, 1, first, x_send), (0, i, second, y_keep), (1, i, second, y_send)):
            out[i, :, 0:rows] = low(keep[my, mx, zs].astype(F32) + recv[my, mx, zs].astype(F32))
            out[i, :, rows:] = low(okeep[my, mx, zs].astype(F32) + orecv[my, mx, zs].astype(F32))


def half_sum_kernel(x_keep, x_recv, y_keep, y_recv, x_own, x_far, y_own, y_far):
    for keep, recv, own, far in ((x_keep, x_recv, x_own, x_far), (y_keep, y_recv, y_own, y_far)):
        for i, out in ((0, own), (1, far)):
            out[...] = low(keep[i].astype(F32) + recv[i].astype(F32))


def line_sum_kernel(x_own, x_recv, y_own, y_recv, *outs):
    half = x_own.shape[0]
    for i in range(half):
        outs[i][...] = low(x_own[i].astype(F32) + x_recv[i].astype(F32))
        outs[half + i][...] = low(y_own[i].astype(F32) + y_recv[i].astype(F32))


def sum_of_four(refs):
    a, b, c, d = (ref[...].astype(F32) for ref in refs)
    return (a + b) + (c + d)


def mix_sum_kernel(m0, m1, m2, m3, *outs):
    total = sum_of_four((m0, m1, m2, m3))
    side = total[..., 768:896]
    rest = side - low(side).astype(F32)
    lane = lanes_of(side.shape)
    moved = jnp.where((lane >= 12) & (lane < 16), side + pltpu.roll(rest, 4, side.ndim - 1), side)
    for i, out in enumerate(outs):
        out[:, 0:768] = low(total[i, :, 0:768])
        out[:, 768:896] = low(moved[i])


def feed_last_kernel(a, b, c, d, up_o, down_o, out_o, done_o):
    done_o[...] = jnp.zeros_like(done_o)
    total = sum_of_four((a, b, c, d))
    rows = up_o.shape[0]
    up_o[...] = total[0:rows]
    down_o[...] = total[rows : 2 * rows]
    out_o[...] = total[2 * rows :]


def mix_last_kernel(pos, a, b, c, d, keep_o, send_o):
    total = sum_of_four((a, b, c, d))
    rows = keep_o.shape[0]
    first = pos[3] == 0
    keep_o[...] = jnp.where(first, total[:rows], total[rows:])
    send_o[...] = jnp.where(first, total[rows:], total[:rows])


def call(kernel, steps, ins, outs, scratch=(), us=1.0, name=None, limit=12, unroll=False):
    def spec(kind):
        if kind in "da":
            return pl.BlockSpec(memory_space=pl.ANY)
        return pl.BlockSpec(memory_space=pltpu.SMEM if kind == "m" else pltpu.VMEM)

    kinds = [kind for kind, _ in ins]
    out_kinds = [kind for kind, _, _ in outs]
    all_kinds = kinds + out_kinds + ["w"] * len(scratch)

    def run(*refs):
        used = [(kind, ref) for kind, ref in zip(all_kinds, refs) if kind != "d"]
        if not steps:
            kernel(*[ref for _, ref in used])
            return

        def one(b, carry):
            kernel(b, *[ref.at[pl.ds(b, 1)] if kind == "s" else ref for kind, ref in used])
            return carry

        lax.fori_loop(0, steps, one, 0, unroll=unroll)

    return pl.pallas_call(
        run,
        in_specs=[spec(kind) for kind in kinds],
        out_specs=[spec(kind) for kind in out_kinds],
        out_shape=[jax.ShapeDtypeStruct(shape, dtype) for _, shape, dtype in outs],
        scratch_shapes=list(scratch),
        compiler_params=pltpu.CompilerParams(vmem_limit_bytes=limit * 1024 * 1024),
        cost_estimate=pl.CostEstimate(flops=int(us * 1.15e9), bytes_accessed=0, transcendentals=0),
        name=name,
    )(*[a for _, a in ins])


def xor_with(a, mask, count):
    return lax.ppermute(a, BOTH, [(i, i ^ mask) for i in range(count)])


def body(
    inputs, cotangent, mix_weight, gate_weight, gate_bias, out_weight, gain_first, shift_first, gain_second,
    shift_second, up_weight, down_weight, random_maps,
):
    dp, tensor = lax.axis_size("dp"), lax.axis_size("tensor")
    count = dp * tensor
    place_dp, place_t = lax.axis_index("dp"), lax.axis_index("tensor")
    seqs, chunk, width = inputs.shape
    heads, head = random_maps.shape[0], random_maps.shape[1]
    hidden = up_weight.shape[1]
    core = place_t % 2
    first = core == 0
    direct = dp == 8
    nz = 4
    if direct:
        pos = jnp.stack([place_dp // 2, place_dp % 2, place_t // 2, core]).astype(jnp.int32)
    else:
        pos = jnp.stack([jnp.zeros_like(core)] * 3 + [core]).astype(jnp.int32)
    swap_core = functools.partial(xor_with, mask=1, count=count)

    def mix_pack(mix_w, gate_w, vecs):
        rows = mix_w.shape[0]
        split = mix_w.reshape(rows, 3, 2, width // 2)
        sides = [v[:, None] for v in vecs]
        pad = jnp.zeros((rows, 120), BF16)
        return [
            jnp.concatenate(
                [split[:, 0, s], split[:, 1, s], split[:, 2, s], gate_w[:, 4 * s : 4 * s + 4]] + sides + [pad], axis=1
            )
            for s in range(2)
        ]

    def join(parts, axis, after=()):
        (out,) = call(
            functools.partial(join_kernel, axis=axis), 0, [("m", pos)] + [("a", a) for a in parts] + [("d", a) for a in after],
            [("w", (len(parts), *parts[0].shape), parts[0].dtype)],
            scratch=[pltpu.SemaphoreType.DMA((len(parts),))], name="join",
        )
        return out

    def pause(after, us):
        (out,) = call(
            pause_kernel, 0, [("d", a) for a in after], [("w", (8, 128), F32)], us=us, name="pause",
        )
        return out

    def from_plane(pieces):
        return [pieces[0], xor_with(pieces[1], 4, count), xor_with(pieces[2], 2, count), xor_with(pieces[3], 6, count)]

    other_in = swap_core(inputs)
    vectors = (gain_first, shift_first, gain_second, shift_second)
    long = 2 * chunk
    unit, cot_t = call(
        prepare_kernel, seqs, [("m", pos), ("s", inputs), ("s", other_in), ("s", cotangent)],
        [("s", (seqs, long, width), F32), ("s", (seqs, width, chunk), BF16)], us=2.5, name="prepare",
    )
    if direct:
        rows = mix_weight.shape[0]
        columns = jnp.pad(gate_weight.T, ((0, 16 - heads), (0, 0)))
        place = lax.broadcasted_iota(jnp.int32, columns.shape, 0)
        for i, v in enumerate(vectors):
            columns = jnp.where(place == heads + i, lax.broadcast_in_dim(v, columns.shape, (1,)), columns)
        keep, send = call(
            pack_kernel, 0, [("m", pos), ("w", mix_weight), ("w", columns)], [("w", (rows, 896), BF16)] * 2, name="pack",
        )
        pair = join([keep, swap_core(send)], 3)
        line = join([pair] + [xor_with(pair, 8 * m, count) for m in range(1, nz)], 0, after=[unit])
        w_pieces = [line] + [xor_with(line, m, count) for m in (4, 2, 6)]
        block = jnp.concatenate([up_weight, down_weight.T, out_weight], axis=0)
        (block,) = call(
            hold_kernel, 0, [("a", block), ("d", unit)],
            [("w", block.shape, BF16)], scratch=[pltpu.SemaphoreType.DMA((1,))], name="hold",
        )
        ff_line = join([block] + [xor_with(block, 8 * m, count) for m in range(1, nz)], 0, after=[line])
        by_x, by_y = xor_with(ff_line, 4, count), xor_with(ff_line, 2, count)
    else:
        whole = [
            lax.all_gather(a, BOTH, axis=0, tiled=True) for a in (mix_weight, gate_weight, out_weight) + vectors
        ]
        p0, p1 = mix_pack(whole[0], whole[1], whole[3:])
        blocks = jnp.where(first, p0, p1).reshape(nz, 2, 2, 2, 16, 896)
        w_pieces = [blocks[:, mx, my] for my, mx in ((0, 0), (0, 1), (1, 0), (1, 1))]
        up_all = lax.all_gather(up_weight, BOTH, axis=0, tiled=False).reshape(dp, tensor, -1, hidden)
        dn_all = lax.all_gather(down_weight.T, BOTH, axis=0, tiled=False).reshape(dp, tensor, -1, hidden)
        up_all = jnp.moveaxis(up_all, 1, 0).reshape(2, 2, nz, 2, -1, hidden)
        dn_all = jnp.moveaxis(dn_all, 1, 0).reshape(2, 2, nz, 2, -1, hidden)
        out_all = whole[2].reshape(nz, 2, 2, 2, 16, width).transpose(2, 3, 0, 1, 4, 5)
        ff_all = jnp.concatenate([up_all, dn_all, out_all], axis=4)
        ff_all = jnp.where(first, ff_all, ff_all[:, ::-1])
        ff_own, ff_other = (
            jnp.concatenate([ff_all[my, mc, :, mx] for my in range(2) for mx in range(2)]) for mc in range(2)
        )

    maps = lax.dynamic_slice_in_dim(random_maps, core * 4, 4, 0)
    zero = jnp.zeros((head, head), BF16)
    maps_pair = jnp.stack(
        [
            jnp.concatenate(
                [jnp.concatenate([maps[2 * p], zero], 1), jnp.concatenate([zero, maps[2 * p + 1]], 1)], 0
            )
            for p in range(2)
        ]
    )
    flip = jnp.swapaxes(maps, 1, 2)
    maps_back = jnp.stack(
        [
            jnp.concatenate(
                [
                    jnp.concatenate([flip[2 * p], zero], 1),
                    jnp.concatenate([-flip[2 * p], zero], 1),
                    jnp.concatenate([zero, flip[2 * p + 1]], 1),
                    jnp.concatenate([zero, -flip[2 * p + 1]], 1),
                ],
                0,
            )
            for p in range(2)
        ]
    )
    bias = jnp.pad(lax.dynamic_slice_in_dim(gate_bias, core * 4, 4, 0), (0, 124))[None]

    tokens = seqs * long
    feats = (seqs, 4, long, 128)
    npack = 2 * seqs + 1
    attend, fk, fkl, fkt, va, ccol, ucol, crow, smid, pack, wmix, vec, vbar = call(
        project_kernel, seqs,
        [("m", pos), ("s", unit)] + [("a", w) for w in w_pieces] + [("w", bias), ("w", maps_pair)],
        [
            ("s", (seqs, long, width), BF16), ("s", feats, BF16), ("s", feats, BF16), ("s", feats, BF16), ("s", feats, BF16),
            ("s", (seqs, long, 128), F32), ("s", (seqs, long, 128), F32),
            ("s", (seqs, 2, 8, chunk), F32),
            ("s", (seqs, 4, 128, 128), F32),
            ("w", (npack, 128, 128), BF16), ("w", (width, 896), BF16), ("w", (8, width), F32),
            ("w", (8, width // 2), F32),
        ],
        scratch=[pltpu.VMEM((nz, 2, 2, 2, 16, 896), BF16), pltpu.SemaphoreType.DMA((4,))], us=12, name="project",
    )
    ahead = [(i, i + 2) for i in range(count) if (i % tensor) < 2]
    arrived = lax.ppermute(pack, BOTH, ahead)
    fq, fql, fqt = call(
        query_kernel, seqs, [("s", attend), ("w", wmix), ("w", maps_pair)], [("s", feats, BF16)] * 3, us=0.3, name="query",
    )
    (o_loc,) = call(
        local_kernel, seqs,
        [("s", fq), ("s", fk), ("s", fql), ("s", fkl), ("s", va), ("s", ccol), ("s", crow)],
        [("s", feats, F32)], us=0.3, name="local", unroll=True,
    )
    if direct:
        half_z = nz // 2
        far_shape = (half_z, *ff_line.shape[1:])
        x_half, y_half = call(
            halves_kernel, 0, [("a", by_x), ("a", by_y), ("d", arrived), ("d", o_loc)], [("w", far_shape, BF16)] * 2,
            scratch=[pltpu.SemaphoreType.DMA((2,))], us=0.3, name="halves",
        )
        near_parts = [ff_line, by_x, by_y]
        (ff_near,) = call(
            gather_kernel, 0, [("a", a) for a in near_parts] + [("d", x_half)],
            [("w", (3 * nz, *ff_line.shape[1:]), BF16)], scratch=[pltpu.SemaphoreType.DMA((3,))], us=0.5, name="near",
        )
        before_finish = [x_half, ff_near]
    else:
        before_finish = []
    (inv_root, turn, st, att_keep, att_send) = call(
        finish_kernel, seqs,
        [("m", pos), ("s", o_loc), ("s", fq), ("s", ccol), ("w", arrived), ("s", smid), ("w", vbar)]
        + [("d", a) for a in before_finish],
        [
            ("s", feats, F32), ("s", feats, F32), ("s", (seqs, 4, 2, 128, 128), BF16),
            ("s", (seqs, chunk, width // 2), BF16), ("s", (seqs, chunk, width // 2), BF16),
        ],
        us=0.3, name="finish",
    )
    att_recv = swap_core(att_send)
    if direct:
        near_other = swap_core(ff_near)
        far_parts = [xor_with(x_half, 2, count), xor_with(y_half, 4, count)]
        (ff_far,) = call(
            gather_kernel, 0, [("a", a) for a in far_parts] + [("d", att_keep)],
            [("w", ff_line.shape, BF16)], scratch=[pltpu.SemaphoreType.DMA((2,))], name="gather",
        )
        far_other = swap_core(ff_far)
    else:
        ff_near, ff_far, near_other, far_other = ff_own[: 3 * nz], ff_own[3 * nz :], ff_other[: 3 * nz], ff_other[3 * nz :]

    own = seqs * chunk
    nrows = ff_near.shape[1]
    payload, out_payload = (2, 2, nz, nrows - 16, hidden), (2, 2, nz, 16, hidden)
    rows_low, rows_full = ("w", (own, width), BF16), ("w", (own, width), F32)
    work = [
        pltpu.VMEM((width, 2 * hidden), BF16), pltpu.VMEM((width, 2 * hidden), BF16),
        pltpu.VMEM((own, 2 * hidden), BF16), pltpu.VMEM((own, 2 * hidden), BF16),
    ]
    big = pltpu.VMEM((width, 2 * hidden), BF16)
    g_send, *fed = call(
        feed_first_kernel, 0,
        [("m", pos)] + [
            ("w", a) for a in (
                att_keep, att_recv, inputs, cotangent, cot_t, vec, ff_near, ff_far, near_other, far_other
            )
        ],
        [
            ("w", payload, BF16), rows_full, rows_full, rows_full, rows_low, ("w", (width, own), BF16), rows_low,
            ("w", (width, width), BF16),
        ],
        scratch=[*work, big], us=10, name="feed_first", limit=18,
    )
    g_recv = swap_core(g_send)
    output, grad_middle, ga_keep, ga_send, g_keep, o_keep, o_send, grad_vec = call(
        feed_second_kernel, 0,
        [("m", pos)] + [("w", a) for a in (cotangent, cot_t, vec, ff_near, ff_far, *fed)],
        [
            ("w", (seqs, chunk, width), BF16), ("w", (seqs, chunk, width), F32),
            ("w", (seqs, chunk, width // 2), BF16), ("w", (seqs, chunk, width // 2), BF16),
            ("w", payload, BF16), ("w", out_payload, BF16), ("w", out_payload, BF16), ("w", (8, width), F32),
        ],
        scratch=[
            *work, pltpu.VMEM((own, width), BF16), big,
        ],
        us=10, name="feed_second", limit=18,
    )
    ga_recv = swap_core(ga_send)

    if direct:
        o_recv = swap_core(o_send)
        half_z = nz // 2
        two, one = (2, half_z, nrows, hidden), (half_z, nrows, hidden)
        x_keep, x_send, y_keep, y_send = call(
            pair_sum_kernel, 0, [("w", g_keep), ("w", g_recv), ("w", o_keep), ("w", o_recv)], [("w", two, BF16)] * 4,
            us=0.6, name="pair_sum",
        )
        x_recv, y_recv = xor_with(x_send, 4, count), xor_with(y_send, 2, count)
        before_adjoint = [x_keep]
    else:
        before_adjoint = []
        g_keep, g_send = (jnp.concatenate(parts, axis=3) for parts in ((g_keep, o_keep), (g_send, o_send)))
        by_core = jnp.where(first, jnp.stack([g_keep, g_send]), jnp.stack([g_send, g_keep]))
        by_rows = by_core.transpose(3, 2, 1, 0, 4, 5)
        rows_up = (nrows - 16) // 2
        ups = by_rows[..., :rows_up, :].reshape(nz * 2, 4, rows_up, hidden).transpose(1, 0, 2, 3)
        dns = by_rows[..., rows_up : 2 * rows_up, :].reshape(nz * 2, 4, rows_up, hidden).transpose(1, 0, 2, 3)
        ups = ups.reshape(4, dp, -1, hidden).transpose(1, 0, 2, 3)
        dns = dns.reshape(4, dp, -1, hidden).transpose(1, 0, 2, 3)
        outs = by_rows[..., 2 * rows_up :, :].reshape(width, width)

        def reduced(a):
            return lax.psum_scatter(a.astype(F32).reshape(count, -1, a.shape[-1]), BOTH, scatter_dimension=0)

        up_grad, down_grad, out_grad = reduced(ups), reduced(dns).T, reduced(outs)

    g, scaled, l1, pack_b = call(
        adjoint_kernel, seqs,
        [("m", pos), ("s", ga_keep), ("s", ga_recv), ("s", inv_root), ("s", turn), ("s", fq), ("s", ccol)]
        + [("d", a) for a in before_adjoint],
        [
            ("s", feats, BF16), ("s", feats, BF16), ("s", (seqs, 4, 128, 128), F32), ("w", (npack, 128, 128), BF16),
        ],
        us=0.3, name="adjoint",
    )
    behind = [(i, i - 2) for i in range(count) if (i % tensor) >= 2]
    arrived_b = lax.ppermute(pack_b, BOTH, behind)
    dfq, dfk, dva = call(
        local_back_kernel, seqs,
        [("s", fq), ("s", fk), ("s", va), ("s", g), ("s", scaled), ("s", st), ("s", ccol), ("s", crow)],
        [("s", feats, F32), ("s", feats, F32), ("s", feats, F32)],
        us=0.3, name="local_back",
    )
    before_close = []
    if direct:
        x_own, x_far, y_own, y_far = call(
            half_sum_kernel, 0, [("w", a) for a in (x_keep, x_recv, y_keep, y_recv)] + [("d", dfq)],
            [("w", one, BF16)] * 4, us=0.4, name="half_sum",
        )
        x_recv, y_recv = xor_with(x_far, 2, count), xor_with(y_far, 4, count)
        before_close = [x_own]
    *m_pieces, gn_keep, gn_send = call(
        functools.partial(close_kernel, seqs_total=seqs), seqs,
        [("m", pos), ("s", unit), ("w", attend), ("s", fq), ("s", fk), ("s", fqt), ("s", fkt), ("s", va), ("s", dfq),
         ("s", dfk), ("s", dva), ("s", ccol), ("s", ucol), ("w", arrived_b), ("s", l1), ("s", st),
         ("w", wmix), ("w", grad_vec), ("w", maps_back)] + [("d", a) for a in before_close],
        [*[("w", (nz, 32, 896), BF16)] * 4, ("s", (seqs, chunk, width), F32), ("s", (seqs, chunk, width), BF16)],
        scratch=[
            pltpu.VMEM((width, 896), F32), pltpu.VMEM((tokens, 896), BF16), pltpu.VMEM((8, 128), F32),
            pltpu.VMEM((8, width), F32), pltpu.VMEM((width, 896), BF16),
        ],
        us=14.7, name="close", unroll=False,
    )
    if direct:
        g_line = call(
            line_sum_kernel, 0, [("w", a) for a in (x_own, x_recv, y_own, y_recv)] + [("d", gn_keep)],
            [("w", (nrows, hidden), BF16)] * nz, us=0.4, name="line_sum",
        )
        m_parts = from_plane(m_pieces)
    gn_recv = swap_core(gn_send)
    def finish_input(after):
        return call(
            input_kernel, seqs,
            [("s", inputs), ("s", grad_middle), ("s", gn_keep), ("s", gn_recv), ("w", vec)] + [("d", a) for a in after],
            [("s", (seqs, chunk, width), F32), ("w", (8, 128), F32)], us=0.3, name="input_grad",
        )

    if direct:
        m_plane = call(
            mix_sum_kernel, 0, [("w", a) for a in m_parts] + [("d", pause([g_line[0]], 15)), ("d", gn_recv)],
            [("w", (32, 896), BF16)] * nz, us=0.4, name="mix_sum",
        )
        input_grad, input_done = finish_input([g_line[0]])
        g_parts = [g_line[0]] + [xor_with(g_line[m], 8 * m, count) for m in range(1, nz)]
        up_grad, down_back, out_grad, feed_done = call(
            feed_last_kernel, 0, [("w", a) for a in g_parts],
            [("w", shape, F32) for shape in (up_weight.shape, down_weight.shape[::-1], out_weight.shape, (8, 128))],
            us=0.3, name="feed_last",
        )
        down_grad = down_back.T
        mix_parts = [m_plane[0]] + [xor_with(m_plane[m], 8 * m, count) for m in range(1, nz)]
        m_keep, m_send = call(
            mix_last_kernel, 0, [("m", pos)] + [("w", a) for a in mix_parts] + [("d", feed_done), ("d", input_done)],
            [("w", (mix_weight.shape[0], 896), F32)] * 2, name="mix_last",
        )
        m_recv = swap_core(m_send)
    else:
        input_grad, input_done = finish_input([])
        m_all = jnp.stack(m_pieces).astype(F32).reshape(2, 2, nz, 32, 896)
        mine_rows = m_all.transpose(2, 1, 0, 3, 4).reshape(count, -1, 896)
        keep_part = lax.psum_scatter(mine_rows * jnp.where(first, 1.0, 0.0), BOTH, scatter_dimension=0)
        far_part = lax.psum_scatter(mine_rows * jnp.where(first, 0.0, 1.0), BOTH, scatter_dimension=0)
        m_keep = jnp.where(first, keep_part, far_part)
        m_recv = jnp.where(first, far_part, keep_part)
    if direct:
        mix_grad, gate_back, bias_grad, *per_row = call(
            final_kernel, 0, [("m", pos), ("w", m_keep), ("w", m_recv)],
            [("w", mix_weight.shape, F32), ("w", gate_weight.shape[::-1], F32), ("w", (heads,), F32)]
            + [("w", gain_first.shape, F32)] * 4,
            us=1.2, name="final",
        )
        gate_grad = gate_back.T
    else:
        m_low = jnp.where(first, m_keep, m_recv)
        m_high = jnp.where(first, m_recv, m_keep)
        mix_grad = jnp.concatenate(
            [part[:, 256 * i : 256 * i + 256] for i in range(3) for part in (m_low, m_high)], axis=1
        )
        gate_grad = jnp.concatenate([m_low[:, 768:772], m_high[:, 768:772]], axis=1)
        bias_grad = jnp.concatenate([m[0, 776:780] + m[0, 780:784] for m in (m_low, m_high)])
        per_row = [m_keep[:, 772 + i] + m_recv[:, 772 + i] for i in range(4)]
    return (
        output, input_grad, mix_grad, gate_grad, bias_grad, out_grad,
        *per_row, up_grad, down_grad,
    )


def solution(mesh):
    rows, spread = P(("dp", "tensor"), None), P(("dp", "tensor"))
    tokens = P("dp", "tensor", None)
    in_specs = (
        tokens, tokens, rows, rows, P(), rows, spread, spread, spread, spread, P("dp", "tensor"), P("tensor", "dp"), P(),
    )
    out_specs = (
        tokens, tokens, rows, rows, P(), rows, spread, spread, spread, spread, P("dp", "tensor"), P("tensor", "dp"),
    )
    return jax.shard_map(body, mesh=mesh, in_specs=in_specs, out_specs=out_specs, check_vma=False)
```
